32 devices in a mesh: groups: 2 (over x), shard: 16 (over z, y, core).
Axes of the slice: x: 2, y: 2, z: 4, core: 2. Of those that a mesh axis runs over, the one named last changes fastest.
Arguments:
- queries: bfloat16 [64, 8192], P(('groups', 'shard')), parts along dimension 0, may hold values from -2.5 to 2.5
- new_kv: bfloat16 [64, 2, 512], P(('groups', 'shard')), parts along dimension 0, may hold values from -2.5 to 2.5
- kv_pages: bfloat16 [512, 2, 32, 512], P(('groups', 'shard')), parts along dimension 0, may hold values from -2.5 to 2.5
- page_table: int32 [64, 8], P('groups'), parts along dimension 0, may hold values from 0 to 255, as said below
- lengths: int32 [64], P('groups'), parts along dimension 0, may hold values from 1 to 256, as said below
- residual: bfloat16 [64, 8192], P('groups', 'shard'), parts along dimension 0, may hold values from -2 to 2
- out_weight: bfloat16 [8192, 8192], P(None, 'shard'), may hold values from -0.1875 to 0.1875
- norm_gain: float32 [8192], P('shard'), may hold values from 0.25 to 1.75
- gate_weight: bfloat16 [8192, 26624], P(None, 'shard'), may hold values from -0.0625 to 0.0625
- up_weight: bfloat16 [8192, 26624], P(None, 'shard'), may hold values from -0.0625 to 0.0625
- down_weight: bfloat16 [26624, 8192], P('shard'), may hold values from -0.0546875 to 0.0546875
Outputs:
- mixed: bfloat16 [64, 8192], P('groups', 'shard'), parts along dimension 0
The draws below stay inside these ranges and needn't reach their ends.
There are 2 independent parts, one for each index of `groups`. The reference program is written for one: setup_inputs(seed, part) draws one part's arguments, and reference() takes and returns one part's arrays. A program takes and returns all parts, laid end to end along the dimension named above; an argument that names none is the same for every part. Nothing has to cross between parts.
Inputs may be any that keep to these rules, and one draw needn't show every extreme that they name: `page_table`: entry (b, k) is the global index of page k of sequence b; every page appears exactly once; pages i * 16 to (i + 1) * 16 - 1 are stored on device i of shard; the 16 pages of the sequences of device i of shard lie one on each device of the aligned block of 16 consecutive devices of shard that contains i. `lengths`: some sequence has exactly 256 cached tokens.
All inputs are finite; a program needn't handle non-finite values.
Results may differ from the reference program's by a relative error of at most 0.015.
Values may be sent and summed in bfloat16 or wider, within the bound.
No kernel may reach another device: no remote copies, remote signals or barrier semaphores. Data moves between devices by JAX's collectives and lax.ppermute only.
A program may use at most 192 MiB of HBM per device.

```python
import math
import jax
import jax.numpy as jnp
from jax import lax

D = 8192
HEADS = 64
KV_HEADS = 4
HEAD_DIM = 128
FF = 26624
PAGE = 32
MAXPG = 8
SEQ_DEV = 2
SEQS = 32
PAGES_DEV = 16
NPAGES = 256


def draw_page_table(key, part):
    key = jax.random.fold_in(key, 11)
    devices_all = NPAGES // PAGES_DEV
    first_key, second_key = jax.random.split(key)
    owner_keys = jax.random.split(first_key, devices_all)
    holder_perm = jax.vmap(lambda sub_key: jax.random.permutation(sub_key, PAGES_DEV))(owner_keys).astype(jnp.int32)
    slot_keys = jax.random.split(second_key, devices_all)
    slot_perm = jax.vmap(lambda sub_key: jax.random.permutation(sub_key, PAGES_DEV))(slot_keys).astype(jnp.int32)
    owner = jnp.arange(SEQS, dtype=jnp.int32) // SEQ_DEV
    within = jnp.arange(SEQS, dtype=jnp.int32) % SEQ_DEV
    order = within[:, None] * MAXPG + jnp.arange(MAXPG, dtype=jnp.int32)[None, :]
    owners = jnp.broadcast_to(owner[:, None], order.shape)
    holder = owners // PAGES_DEV * PAGES_DEV + holder_perm[owners, order]
    slot = slot_perm[holder, owners % PAGES_DEV]
    return (holder * PAGES_DEV + slot).astype(jnp.int32)


def draw_lengths(key, part):
    key = jax.random.fold_in(key, 23)
    first_key, second_key = jax.random.split(key)
    longest = MAXPG * PAGE
    base = jax.random.randint(first_key, (SEQS,), 1, longest + 1)
    chosen = jax.random.randint(second_key, (), 0, SEQS)
    return jnp.where(jnp.arange(SEQS) == chosen, longest, base).astype(jnp.int32)


def strengthened(result, key, source, target, parts, factor):
    def block_of(dim):
        return (jnp.arange(result.shape[dim]) // (result.shape[dim] // parts)).reshape((-1,) + (1,) * (result.ndim - 1 - dim))

    first = jax.random.permutation(key, parts)[block_of(target)]
    other_side = (block_of(target) + parts // 2) % parts
    return jnp.where((block_of(source) == first) | (block_of(source) == other_side), factor * result, result)


def steps_of(own_key, extent, pieces, low, top_value):
    gain, own = 1.0, jax.random.fold_in(own_key, 6)
    for dim, shards_of in pieces:
        heights = jnp.exp(jax.random.uniform(jax.random.fold_in(own, dim), (shards_of,), jnp.float32, low / len(pieces), top_value / len(pieces)))
        gain = gain * jnp.repeat(heights, extent[dim] // shards_of).reshape([-1 if axis == dim else 1 for axis in range(len(extent))])
    return gain


def centred(rng, dims, spread, limit, cuts=(), kind=jnp.bfloat16):
    loudness = steps_of(rng, dims, cuts, -0.22, 0.18) if cuts else 1.0
    array = jax.random.normal(rng, dims, jnp.float32) * spread * loudness
    return jnp.minimum(jnp.maximum(array, -limit), limit).astype(kind)


def heavy_noise(stream_key, shape, deviation, reach, cuts, heavy, held_as=jnp.bfloat16):
    entries = deviation * jax.random.normal(stream_key, shape, jnp.float32)
    if cuts:
        entries = entries * steps_of(stream_key, shape, cuts, -0.22, 0.18)
    return jnp.clip(strengthened(entries, jax.random.fold_in(stream_key, 3), *heavy), -reach, reach).astype(held_as)


def setup_inputs(seed: int = 0, part: int = 0) -> dict:
    streams_of = jax.random.split(jax.random.key(seed), 12)
    part_splits = jax.random.split(jax.random.fold_in(streams_of[11], part), 12)
    return {
        "queries": centred(part_splits[0], (SEQS, D), 1.0, 2.5, ((0, 16),)),
        "new_kv": centred(part_splits[1], (SEQS, 2, KV_HEADS * HEAD_DIM), 1.0, 2.5, ((0, 16),)),
        "kv_pages": centred(part_splits[2], (NPAGES, 2, PAGE, KV_HEADS * HEAD_DIM), 1.0, 2.5, ((0, 16),)),
        "page_table": draw_page_table(jax.random.fold_in(jax.random.fold_in(streams_of[11], part), 71), part),
        "lengths": draw_lengths(jax.random.fold_in(jax.random.fold_in(streams_of[11], part), 71), part),
        "residual": centred(part_splits[5], (SEQS, D), 0.25, 2.0, ((1, 16),)),
        "out_weight": centred(streams_of[6], (D, D), (D // 8) ** -0.5, 0.1875, ((1, 16),)),
        "norm_gain": jnp.clip(1.0 + 0.15 * jax.random.normal(streams_of[7], (D,), jnp.float32), 0.25, 1.75),
        "gate_weight": centred(streams_of[8], (D, FF), D ** -0.5, 0.0625, ((1, 16),)),
        "up_weight": centred(streams_of[9], (D, FF), D ** -0.5, 0.0625, ((1, 16),)),
        "down_weight": heavy_noise(streams_of[10], (FF, D), FF ** -0.5, 0.0546875, ((0, 16),), (0, 1, 16, 2.0)),
    }


norm_eps = 1e-05

def attend_row(query_row, new_row, table_row, length_row, kv_pages):
    group_size = HEADS // KV_HEADS
    context = MAXPG * PAGE
    fetched = kv_pages[table_row]
    key_rows = fetched[:, 0].reshape(context, KV_HEADS, HEAD_DIM)
    value_rows = fetched[:, 1].reshape(context, KV_HEADS, HEAD_DIM)
    key_rows = jnp.concatenate([key_rows, new_row[0].reshape(1, KV_HEADS, HEAD_DIM)], axis=0)
    value_rows = jnp.concatenate([value_rows, new_row[1].reshape(1, KV_HEADS, HEAD_DIM)], axis=0)
    query_heads = query_row.reshape(KV_HEADS, group_size, HEAD_DIM).astype(jnp.float32)
    scores = jnp.einsum('gqd,tgd->gqt', query_heads, key_rows.astype(jnp.float32)) * (1.0 / math.sqrt(HEAD_DIM))
    position = jnp.arange(context + 1, dtype=jnp.int32)
    alive = (position < length_row) | (position == context)
    weights = jnp.where(alive[None, None, :], jnp.exp(scores), jnp.zeros_like(scores))
    denominator = lax.optimization_barrier(jnp.sum(weights, axis=-1))
    rounded = lax.optimization_barrier(weights.astype(jnp.bfloat16)).astype(jnp.float32)
    numerator = jnp.einsum('gqt,tgd->gqd', rounded, value_rows.astype(jnp.float32))
    return (numerator / denominator[..., None]).reshape(D).astype(jnp.bfloat16)

def reference(queries, new_kv, kv_pages, page_table, lengths, residual, out_weight, norm_gain, gate_weight, up_weight, down_weight):
    attended = lax.map(lambda items: attend_row(items[0], items[1], items[2], items[3], kv_pages), (queries, new_kv, page_table, lengths))
    stream = (residual.astype(jnp.float32) + jnp.dot(attended, out_weight, preferred_element_type=jnp.float32)).astype(jnp.bfloat16)
    wide = stream.astype(jnp.float32)
    square_mean = lax.optimization_barrier(jnp.mean(wide * wide, axis=1, keepdims=True))
    normed = (wide * lax.rsqrt(square_mean + norm_eps) * norm_gain[None, :]).astype(jnp.bfloat16)
    gate_acts = jnp.dot(normed, gate_weight, preferred_element_type=jnp.float32)
    up_acts = jnp.dot(normed, up_weight, preferred_element_type=jnp.float32)
    hidden = (jax.nn.silu(gate_acts) * up_acts).astype(jnp.bfloat16)
    down_terms = jnp.dot(hidden, down_weight, preferred_element_type=jnp.float32)
    return (wide + down_terms).astype(jnp.bfloat16)
```

```python
import math

import jax
import jax.numpy as jnp
from jax import lax
from jax.experimental import pallas as pl
from jax.experimental.pallas import tpu as pltpu
from jax.sharding import PartitionSpec as P

D = 8192
HEADS = 64
KV_HEADS = 4
HEAD_DIM = 128


norm_eps = 1e-05


def swapped(array, axis, distance):
    return lax.ppermute(array, axis, [(i, i ^ 1 << distance) for i in range(lax.axis_size(axis))])


def new_token_terms(queries, new_kv, score_scale):
    seq_dev = queries.shape[0]
    group_size = HEADS // KV_HEADS
    query_heads = queries.reshape(seq_dev, KV_HEADS, group_size, HEAD_DIM)
    new_keys = new_kv[:, 0].reshape(seq_dev, KV_HEADS, HEAD_DIM)
    new_values = new_kv[:, 1].reshape(seq_dev, KV_HEADS, HEAD_DIM)
    scores = (
        jnp.einsum("bgqd,bgd->bgq", query_heads, new_keys, preferred_element_type=jnp.float32)
        * score_scale
    )
    weights = jnp.exp(scores)
    numerator = jnp.einsum(
        "bgq,bgd->bgqd",
        weights.astype(jnp.bfloat16),
        new_values,
        preferred_element_type=jnp.float32,
    )
    return (numerator.reshape(seq_dev, D), weights.reshape(seq_dev, HEADS))


def butterfly(items, position, mover):
    count = items[0].shape[0]
    for level in range(count.bit_length() - 1):
        upper_half = position // (1 << level) % 2 == 1
        halves = [
            entry.reshape((count >> level + 1, 2, 1 << level) + entry.shape[1:]) for entry in items
        ]
        outgoing = tuple(
            (jnp.where(upper_half, halves_one[:, 0], halves_one[:, 1]) for halves_one in halves)
        )
        incoming = mover(outgoing, level)
        rebuilt = []
        for entry, halves_one, arrived_one in zip(items, halves, incoming):
            lower_part = jnp.where(upper_half, arrived_one, halves_one[:, 0])
            upper_part = jnp.where(upper_half, halves_one[:, 1], arrived_one)
            rebuilt.append(jnp.stack([lower_part, upper_part], axis=1).reshape(entry.shape))
        items = tuple(rebuilt)
    return items


def body(
    queries,
    new_kv,
    kv_pages,
    page_table,
    lengths,
    residual,
    out_weight,
    norm_gain,
    gate_weight,
    up_weight,
    down_weight,
):
    seq_dev = queries.shape[0]
    page_count = kv_pages.shape[0]
    page_len = kv_pages.shape[2]
    all_seqs = page_table.shape[0]
    max_pages = page_table.shape[1]
    group_size = HEADS // KV_HEADS
    score_scale = 1.0 / math.sqrt(HEAD_DIM)
    device_pos = lax.axis_index("shard")
    own_first = device_pos * seq_dev
    own_lengths = lax.dynamic_slice_in_dim(lengths, own_first, seq_dev, 0)
    own_table = lax.dynamic_slice_in_dim(page_table, own_first, seq_dev, 0)
    holder_local = own_table // page_count % page_count
    page_ids = device_pos * page_count + jnp.arange(page_count, dtype=jnp.int32)
    matches = page_table[None, :, :] == page_ids[:, None, None]
    seq_of = jnp.sum(
        jnp.where(matches, jnp.arange(all_seqs, dtype=jnp.int32)[None, :, None], 0), axis=(1, 2)
    )
    owner_local = seq_of // seq_dev % page_count
    own_numerator, own_denominator = new_token_terms(queries, new_kv, score_scale)
    outgoing = jnp.zeros_like(kv_pages).at[owner_local].set(kv_pages)
    arrived = butterfly(
        (outgoing,), device_pos, lambda sending, level: (swapped(sending[0], "shard", level),)
    )[0]
    fetched = arrived[holder_local]
    context = max_pages * page_len
    key_rows = fetched[:, :, 0].reshape(seq_dev, context, KV_HEADS, HEAD_DIM)
    value_rows = fetched[:, :, 1].reshape(seq_dev, context, KV_HEADS, HEAD_DIM)
    query_heads = queries.reshape(seq_dev, KV_HEADS, group_size, HEAD_DIM)
    scores = (
        jnp.einsum("bgqd,btgd->bgqt", query_heads, key_rows, preferred_element_type=jnp.float32)
        * score_scale
    )
    position = jnp.arange(context, dtype=jnp.int32)
    alive = position[None, :] < own_lengths[:, None]
    weights = jnp.where(alive[:, None, None, :], jnp.exp(scores), 0.0)
    denominator = jnp.sum(weights, axis=-1).reshape(seq_dev, HEADS)
    numerator = jnp.einsum(
        "bgqt,btgd->bgqd",
        weights.astype(jnp.bfloat16),
        value_rows,
        preferred_element_type=jnp.float32,
    )
    numer_rows = numerator.reshape(seq_dev, D) + own_numerator
    denom_rows = denominator + own_denominator
    attended = (
        (numer_rows.reshape(seq_dev, HEADS, HEAD_DIM) / denom_rows[:, :, None])
        .reshape(seq_dev, D)
        .astype(jnp.bfloat16)
    )
    projected = jnp.dot(
        lax.all_gather(attended, "shard", axis=0, tiled=True),
        out_weight,
        preferred_element_type=jnp.float32,
    )
    stream = (residual.astype(jnp.float32) + projected).astype(jnp.bfloat16)
    wide = stream.astype(jnp.float32)
    square_sums = lax.psum(jnp.sum(wide * wide, axis=1), "shard")
    normed = (wide * lax.rsqrt(square_sums / D + norm_eps)[:, None] * norm_gain[None, :]).astype(
        jnp.bfloat16
    )
    block_cols = lax.all_gather(normed, "shard", axis=1, tiled=True)
    gate_acts = jnp.dot(block_cols, gate_weight, preferred_element_type=jnp.float32)
    up_acts = jnp.dot(block_cols, up_weight, preferred_element_type=jnp.float32)
    hidden = (jax.nn.silu(gate_acts) * up_acts).astype(jnp.bfloat16)
    partial_terms = jnp.dot(hidden, down_weight, preferred_element_type=jnp.float32)
    down_terms = lax.psum_scatter(partial_terms, "shard", scatter_dimension=1, tiled=True)
    return (wide + down_terms).astype(jnp.bfloat16)


GROUP = HEADS // KV_HEADS
HEAD_ROWS = 80
MIB = 2**20
VMEM_SPEC = pl.BlockSpec(memory_space=pltpu.VMEM)
SMEM_SPEC = pl.BlockSpec(memory_space=pltpu.SMEM)


def sent(array, distance):
    size = lax.axis_size("shard")
    return lax.ppermute(array, "shard", [(i, i ^ distance) for i in range(size)])


def gathered(piece):
    first = jnp.stack([piece] + [sent(piece, distance) for distance in (4, 8, 12)])
    even = jnp.concatenate([first, sent(first, 2)])
    return even, sent(even, 1)


PEER = (0, 4, 8, 12, 2, 6, 10, 14)


def two_terms(wide):
    high = wide.astype(jnp.bfloat16).astype(jnp.float32)
    return high, wide - high


def pack_kernel(query_ref, gain_ref, out_ref):
    rows = query_ref.shape[0]
    out_ref[:rows, :] = query_ref[...]
    high, rest = two_terms(gain_ref[...])
    middle, low = two_terms(rest)
    filler = jnp.zeros((16 - 3 * high.shape[0], HEAD_DIM), jnp.float32)
    out_ref[rows:, :] = jnp.concatenate([high, middle, low, filler]).astype(jnp.bfloat16)


def packed(queries, norm_gain):
    query_rows = queries.reshape(-1, HEAD_DIM)
    gain_rows = norm_gain.reshape(-1, HEAD_DIM)
    return pl.pallas_call(
        pack_kernel,
        in_specs=[VMEM_SPEC] * 2,
        out_specs=VMEM_SPEC,
        out_shape=jax.ShapeDtypeStruct((query_rows.shape[0] + 16, HEAD_DIM), jnp.bfloat16),
    )(query_rows, gain_rows)


def row_of(column):
    return jnp.swapaxes(jnp.broadcast_to(column, (column.shape[0], HEAD_DIM)), 0, 1)[:1]


def context_terms(query, keys, values, alive):
    numerators, denominators = [], []
    for head in range(KV_HEADS):
        cols = slice(head * HEAD_DIM, (head + 1) * HEAD_DIM)
        scores = lax.dot_general(
            query[head * GROUP : (head + 1) * GROUP],
            keys[:, cols],
            (((1,), (1,)), ((), ())),
            preferred_element_type=jnp.float32,
        ) * (1.0 / math.sqrt(HEAD_DIM))
        weights = jnp.where(alive, jnp.exp(scores), 0.0)
        denominators.append(jnp.sum(weights, axis=1, keepdims=True))
        numerators.append(
            jnp.dot(
                weights.astype(jnp.bfloat16), values[:, cols], preferred_element_type=jnp.float32
            )
        )
    return jnp.concatenate(numerators), jnp.concatenate(denominators)


def pages_kernel(table_ref, even_ref, odd_ref, pages_ref, out_ref):
    me = table_ref[0]
    page_len = pages_ref.shape[2]
    position = lax.broadcasted_iota(jnp.int32, (GROUP, page_len), 1)
    for entry in range(16):
        source = even_ref if entry < 8 else odd_ref
        owner = me ^ (PEER[entry % 8] + entry // 8)
        slot, row, left = (table_ref[1 + 16 * part + owner] for part in range(3))
        query = source[entry % 8, pl.ds(pl.multiple_of(row * HEADS, HEADS), HEADS), :]
        numerator, denominator = context_terms(
            query, pages_ref[slot, 0], pages_ref[slot, 1], position < left
        )
        out_ref[owner, :HEADS, :] = numerator.astype(jnp.bfloat16)
        high, low = two_terms(row_of(denominator))
        last = jnp.concatenate([high[:, :HEADS], low[:, :HEADS]], axis=1)
        out_ref[owner, HEADS:, :] = jnp.concatenate(
            [last, jnp.zeros((HEAD_ROWS - HEADS - 1, HEAD_DIM), jnp.float32)]
        ).astype(jnp.bfloat16)


def page_terms(table, even, odd, kv_pages):
    return pl.pallas_call(
        pages_kernel,
        in_specs=[SMEM_SPEC] + [VMEM_SPEC] * 3,
        out_specs=VMEM_SPEC,
        out_shape=jax.ShapeDtypeStruct((16, HEAD_ROWS, HEAD_DIM), jnp.bfloat16),
        compiler_params=pltpu.CompilerParams(vmem_limit_bytes=16 * MIB),
        cost_estimate=pl.CostEstimate(flops=2**27, bytes_accessed=2**21, transcendentals=2**15),
    )(table, even, odd, kv_pages)


def combine_kernel(table_ref, arrived_ref, query_ref, new_ref, out_ref, wide):
    first_token = lax.broadcasted_iota(jnp.int32, (GROUP, 8), 1) < 1
    totals = []
    for row in range(2):
        keys = jnp.broadcast_to(new_ref[row, 0:1, :], (8, new_ref.shape[2]))
        values = jnp.broadcast_to(new_ref[row, 1:2, :], (8, new_ref.shape[2]))
        totals.append(
            context_terms(
                query_ref[row * HEADS : (row + 1) * HEADS, :], keys, values, first_token
            )
        )
    sums = [numerator for numerator, _ in totals]
    lower = [jnp.zeros((1, HEADS), jnp.float32)] * 2
    for sender in range(16):
        second = table_ref[49 + sender] == 1
        numerator = arrived_ref[sender, :HEADS, :].astype(jnp.float32)
        last = arrived_ref[sender, HEADS:, :].astype(jnp.float32)[:1]
        denominator = last[:, :HEADS] + last[:, HEADS:]
        sums = [
            sums[0] + jnp.where(second, 0.0, numerator),
            sums[1] + jnp.where(second, numerator, 0.0),
        ]
        lower = [
            lower[0] + jnp.where(second, 0.0, denominator),
            lower[1] + jnp.where(second, denominator, 0.0),
        ]
    for row in range(2):
        padded = jnp.concatenate([lower[row], jnp.zeros((1, HEADS), jnp.float32)], axis=1)
        column = jnp.swapaxes(jnp.broadcast_to(padded, (8, HEAD_DIM)), 0, 1)[:HEADS, :1]
        wide[row * HEADS : (row + 1) * HEADS, :] = sums[row] / (column + totals[row][1])
    out_ref[...] = wide[...].astype(jnp.bfloat16)


def combined(table, arrived, query_rows, new_kv):
    return pl.pallas_call(
        combine_kernel,
        in_specs=[SMEM_SPEC] + [VMEM_SPEC] * 3,
        out_specs=VMEM_SPEC,
        out_shape=jax.ShapeDtypeStruct((2 * HEADS, HEAD_DIM), jnp.bfloat16),
        scratch_shapes=[pltpu.VMEM((2 * HEADS, HEAD_DIM), jnp.float32)],
        compiler_params=pltpu.CompilerParams(vmem_limit_bytes=16 * MIB),
        cost_estimate=pl.CostEstimate(flops=2**22, bytes_accessed=2**20, transcendentals=2**11),
    )(table, arrived, query_rows, new_kv)


def out_kernel(table_ref, even_ref, odd_ref, residual_ref, weight_ref, out_ref, wide, left, total):
    step = pl.program_id(0)
    depth = weight_ref.shape[0]

    @pl.when(step == 0)
    def _():
        me = table_ref[0]
        for entry in range(16):
            source = even_ref if entry < 8 else odd_ref
            device = me ^ (PEER[entry % 8] + entry // 8)
            start = pl.multiple_of(device * 2 * HEADS, 2 * HEADS)
            wide[pl.ds(start, 2 * HEADS), :] = source[entry % 8].astype(jnp.float32)
        for head in range(HEADS):
            rows = [wide[pl.ds(row * HEADS + head, 16, 2 * HEADS), :] for row in range(2)]
            left[:, head * HEAD_DIM : (head + 1) * HEAD_DIM] = jnp.concatenate(rows).astype(
                jnp.bfloat16
            )
        total[...] = jnp.zeros_like(total)

    here = pl.ds(pl.multiple_of(step * depth, depth), depth)
    total[...] += jnp.dot(left[:, here], weight_ref[...], preferred_element_type=jnp.float32)

    @pl.when(step == pl.num_programs(0) - 1)
    def _():
        line = lax.broadcasted_iota(jnp.int32, (32, 32), 0)
        entry = lax.broadcasted_iota(jnp.int32, (32, 32), 1)
        turn = ((line % 2) * 16 + line // 2 == entry).astype(jnp.float32)
        turned = lax.dot_general(
            turn,
            total[...],
            (((1,), (0,)), ((), ())),
            precision=lax.Precision.HIGHEST,
            preferred_element_type=jnp.float32,
        )
        out_ref[...] = (residual_ref[...].astype(jnp.float32) + turned).astype(jnp.bfloat16)


def projected(table, even, odd, residual, out_weight):
    depth, (rows, width) = 1024, residual.shape
    return pl.pallas_call(
        out_kernel,
        grid=(D // depth,),
        in_specs=[SMEM_SPEC]
        + [VMEM_SPEC] * 3
        + [pl.BlockSpec((depth, width), lambda step: (step, 0))],
        out_specs=VMEM_SPEC,
        out_shape=jax.ShapeDtypeStruct((rows, width), jnp.bfloat16),
        scratch_shapes=[
            pltpu.VMEM((32 * HEADS, HEAD_DIM), jnp.float32),
            pltpu.VMEM((rows, D), jnp.bfloat16),
            pltpu.VMEM((rows, width), jnp.float32),
        ],
        compiler_params=pltpu.CompilerParams(vmem_limit_bytes=16 * MIB),
        cost_estimate=pl.CostEstimate(
            flops=2 * rows * D * width, bytes_accessed=2 * D * width, transcendentals=0
        ),
    )(table, even, odd, residual, out_weight)


def hidden_kernel(
    table_ref, even_ref, odd_ref, even_gain, odd_gain, gate_ref, up_ref, out_ref, scale, gates, ups
):
    step = pl.program_id(0)
    swap = table_ref[0] % 2 == 1

    @pl.when(step == 0)
    def _():
        squares = jnp.zeros(even_ref.shape[1:], jnp.float32)
        for entry in range(8):
            for source in (even_ref, odd_ref):
                wide = source[entry].astype(jnp.float32)
                squares = squares + wide * wide
        scale[...] = lax.rsqrt(jnp.sum(squares, axis=1, keepdims=True) / D + norm_eps)
        gates[...] = jnp.zeros_like(gates)
        ups[...] = jnp.zeros_like(ups)

    pieces = []
    for stream_ref, gain_ref in ((even_ref, even_gain), (odd_ref, odd_gain)):
        terms = gain_ref[step, 2 * HEADS :, :].astype(jnp.float32)
        gain = terms[0:4] + terms[4:8] + terms[8:12]
        gain = jnp.concatenate([gain[part : part + 1] for part in range(4)], axis=1)
        wide = stream_ref[step].astype(jnp.float32)
        pieces.append((wide * scale[...] * gain).astype(jnp.bfloat16))
    left = jnp.concatenate(
        [jnp.where(swap, pieces[1], pieces[0]), jnp.where(swap, pieces[0], pieces[1])], axis=1
    )
    gates[...] += jnp.dot(left, gate_ref[...], preferred_element_type=jnp.float32)
    ups[...] += jnp.dot(left, up_ref[...], preferred_element_type=jnp.float32)

    @pl.when(step == pl.num_programs(0) - 1)
    def _():
        out_ref[...] = (jax.nn.silu(gates[...]) * ups[...]).astype(jnp.bfloat16)


def pair_of(step, table_ref):
    distance = (step % 4) * 2 + step // 4
    return (table_ref[0] // 2) ^ distance


def hidden_units(table, stream, gain, gate_weight, up_weight):
    rows = stream[0].shape[1]
    width = gate_weight.shape[1]
    depth = 2 * stream[0].shape[2]
    whole = lambda array: pl.BlockSpec(array.shape, lambda step, table: (0,) * array.ndim)
    weights = pl.BlockSpec((depth, width), lambda step, table: (pair_of(step, table), 0))
    return pl.pallas_call(
        hidden_kernel,
        grid_spec=pltpu.PrefetchScalarGridSpec(
            num_scalar_prefetch=1,
            grid=(D // depth,),
            in_specs=[whole(array) for array in (*stream, *gain)] + [weights] * 2,
            out_specs=pl.BlockSpec((rows, width), lambda step, table: (0, 0)),
            scratch_shapes=[
                pltpu.VMEM((rows, 1), jnp.float32),
                pltpu.VMEM((rows, width), jnp.float32),
                pltpu.VMEM((rows, width), jnp.float32),
            ],
        ),
        out_shape=jax.ShapeDtypeStruct((rows, width), jnp.bfloat16),
        compiler_params=pltpu.CompilerParams(vmem_limit_bytes=32 * MIB),
        cost_estimate=pl.CostEstimate(
            flops=4 * rows * D * width, bytes_accessed=4 * D * width, transcendentals=rows * width
        ),
    )(table, *stream, *gain, gate_weight, up_weight)


def down_kernel(table_ref, hidden_ref, weight_ref, out_ref):
    out_ref[0] = jnp.dot(
        hidden_ref[...], weight_ref[...], preferred_element_type=jnp.float32
    ).astype(out_ref.dtype)


def down_terms(table, hidden, down_weight, other, held_as):
    rows, depth = hidden.shape
    width = D // 16

    def block(step, table_ref):
        return (0, 2 * step + (table_ref[0] % 2 ^ other))

    return pl.pallas_call(
        down_kernel,
        grid_spec=pltpu.PrefetchScalarGridSpec(
            num_scalar_prefetch=1,
            grid=(8,),
            in_specs=[
                pl.BlockSpec((rows, depth), lambda step, table: (0, 0)),
                pl.BlockSpec((depth, width), block),
            ],
            out_specs=pl.BlockSpec((1, rows, width), lambda step, table: (step, 0, 0)),
        ),
        out_shape=jax.ShapeDtypeStruct((8, rows, width), held_as),
        compiler_params=pltpu.CompilerParams(vmem_limit_bytes=32 * MIB),
        cost_estimate=pl.CostEstimate(
            flops=16 * rows * depth * width, bytes_accessed=16 * depth * width, transcendentals=0
        ),
    )(table, hidden, down_weight)


def tables(page_table, lengths, page_count, page_len):
    me = lax.axis_index("shard").astype(jnp.int32)
    seqs, pages = page_table.shape
    holder = page_table // page_count
    row = (jnp.arange(seqs, dtype=jnp.int32) % 2)[:, None] + jnp.zeros_like(page_table)
    left = lengths[:, None] - page_len * jnp.arange(pages, dtype=jnp.int32)[None, :]
    found = (holder == me).reshape(-1, 2 * pages)
    parts = [
        jnp.sum(jnp.where(found, part.reshape(-1, 2 * pages), 0), axis=1)
        for part in (page_table % page_count, row, left)
    ]
    own = lax.dynamic_slice_in_dim(holder, 2 * me, 2, 0)
    sender = jnp.arange(16, dtype=jnp.int32)
    parts.append(jnp.sum((own[1][None, :] == sender[:, None]).astype(jnp.int32), axis=1))
    return jnp.concatenate([me[None]] + parts)


def block_body(
    queries,
    new_kv,
    kv_pages,
    page_table,
    lengths,
    residual,
    out_weight,
    norm_gain,
    gate_weight,
    up_weight,
    down_weight,
):
    table = tables(page_table, lengths, kv_pages.shape[0], kv_pages.shape[2])
    own = packed(queries, norm_gain)
    even, odd = gathered(own)
    terms = page_terms(table, even, odd, kv_pages)
    arrived = lax.all_to_all(terms, "shard", 0, 0)
    attended = combined(table, arrived, own[: 2 * HEADS], new_kv)
    stream = projected(table, *gathered(attended), residual, out_weight)
    hidden = hidden_units(table, gathered(stream), (even, odd), gate_weight, up_weight)
    theirs = sent(down_terms(table, hidden, down_weight, 1, jnp.bfloat16), 1)
    mine = down_terms(table, hidden, down_weight, 0, jnp.float32)
    pairs = (mine + theirs.astype(jnp.float32)).astype(jnp.bfloat16)
    same_core = [[core + 2 * step for step in range(8)] for core in range(2)]
    shares = lax.all_to_all(pairs, "shard", 0, 0, axis_index_groups=same_core)
    return (stream.astype(jnp.float32) + jnp.sum(shares.astype(jnp.float32), axis=0)).astype(
        jnp.bfloat16
    )


def solution(mesh):
    placed = (
        P(("groups", "shard"), None),
        P(("groups", "shard"), None, None),
        P(("groups", "shard"), None, None, None),
        P("groups", None),
        P("groups"),
        P("groups", "shard"),
        P(None, "shard"),
        P("shard"),
        P(None, "shard"),
        P(None, "shard"),
        P("shard", None),
    )
    chosen = block_body if mesh.shape["shard"] == 16 else body
    return jax.shard_map(
        chosen, mesh=mesh, in_specs=placed, out_specs=P("groups", "shard"), check_vma=False
    )
```

```python
import functools
import math

import jax
import jax.numpy as jnp
from jax import lax
from jax.experimental import pallas as pl
from jax.experimental.pallas import tpu as pltpu
from jax.sharding import PartitionSpec as P

D = 8192
HEADS = 64
KV_HEADS = 4
HEAD_DIM = 128


norm_eps = 1e-05


def swapped(array, axis, distance):
    return lax.ppermute(array, axis, [(i, i ^ 1 << distance) for i in range(lax.axis_size(axis))])


def new_token_terms(queries, new_kv, score_scale):
    seq_dev = queries.shape[0]
    group_size = HEADS // KV_HEADS
    query_heads = queries.reshape(seq_dev, KV_HEADS, group_size, HEAD_DIM)
    new_keys = new_kv[:, 0].reshape(seq_dev, KV_HEADS, HEAD_DIM)
    new_values = new_kv[:, 1].reshape(seq_dev, KV_HEADS, HEAD_DIM)
    scores = (
        jnp.einsum("bgqd,bgd->bgq", query_heads, new_keys, preferred_element_type=jnp.float32)
        * score_scale
    )
    weights = jnp.exp(scores)
    numerator = jnp.einsum(
        "bgq,bgd->bgqd",
        weights.astype(jnp.bfloat16),
        new_values,
        preferred_element_type=jnp.float32,
    )
    return (numerator.reshape(seq_dev, D), weights.reshape(seq_dev, HEADS))


def butterfly(items, position, mover):
    count = items[0].shape[0]
    for level in range(count.bit_length() - 1):
        upper_half = position // (1 << level) % 2 == 1
        halves = [
            entry.reshape((count >> level + 1, 2, 1 << level) + entry.shape[1:]) for entry in items
        ]
        outgoing = tuple(
            (jnp.where(upper_half, halves_one[:, 0], halves_one[:, 1]) for halves_one in halves)
        )
        incoming = mover(outgoing, level)
        rebuilt = []
        for entry, halves_one, arrived_one in zip(items, halves, incoming):
            lower_part = jnp.where(upper_half, arrived_one, halves_one[:, 0])
            upper_part = jnp.where(upper_half, halves_one[:, 1], arrived_one)
            rebuilt.append(jnp.stack([lower_part, upper_part], axis=1).reshape(entry.shape))
        items = tuple(rebuilt)
    return items


def body(
    queries,
    new_kv,
    kv_pages,
    page_table,
    lengths,
    residual,
    out_weight,
    norm_gain,
    gate_weight,
    up_weight,
    down_weight,
):
    seq_dev = queries.shape[0]
    page_count = kv_pages.shape[0]
    page_len = kv_pages.shape[2]
    all_seqs = page_table.shape[0]
    max_pages = page_table.shape[1]
    group_size = HEADS // KV_HEADS
    score_scale = 1.0 / math.sqrt(HEAD_DIM)
    device_pos = lax.axis_index("shard")
    own_first = device_pos * seq_dev
    own_lengths = lax.dynamic_slice_in_dim(lengths, own_first, seq_dev, 0)
    own_table = lax.dynamic_slice_in_dim(page_table, own_first, seq_dev, 0)
    holder_local = own_table // page_count % page_count
    page_ids = device_pos * page_count + jnp.arange(page_count, dtype=jnp.int32)
    matches = page_table[None, :, :] == page_ids[:, None, None]
    seq_of = jnp.sum(
        jnp.where(matches, jnp.arange(all_seqs, dtype=jnp.int32)[None, :, None], 0), axis=(1, 2)
    )
    owner_local = seq_of // seq_dev % page_count
    own_numerator, own_denominator = new_token_terms(queries, new_kv, score_scale)
    outgoing = jnp.zeros_like(kv_pages).at[owner_local].set(kv_pages)
    arrived = butterfly(
        (outgoing,), device_pos, lambda sending, level: (swapped(sending[0], "shard", level),)
    )[0]
    fetched = arrived[holder_local]
    context = max_pages * page_len
    key_rows = fetched[:, :, 0].reshape(seq_dev, context, KV_HEADS, HEAD_DIM)
    value_rows = fetched[:, :, 1].reshape(seq_dev, context, KV_HEADS, HEAD_DIM)
    query_heads = queries.reshape(seq_dev, KV_HEADS, group_size, HEAD_DIM)
    scores = (
        jnp.einsum("bgqd,btgd->bgqt", query_heads, key_rows, preferred_element_type=jnp.float32)
        * score_scale
    )
    position = jnp.arange(context, dtype=jnp.int32)
    alive = position[None, :] < own_lengths[:, None]
    weights = jnp.where(alive[:, None, None, :], jnp.exp(scores), 0.0)
    denominator = jnp.sum(weights, axis=-1).reshape(seq_dev, HEADS)
    numerator = jnp.einsum(
        "bgqt,btgd->bgqd",
        weights.astype(jnp.bfloat16),
        value_rows,
        preferred_element_type=jnp.float32,
    )
    numer_rows = numerator.reshape(seq_dev, D) + own_numerator
    denom_rows = denominator + own_denominator
    attended = (
        (numer_rows.reshape(seq_dev, HEADS, HEAD_DIM) / denom_rows[:, :, None])
        .reshape(seq_dev, D)
        .astype(jnp.bfloat16)
    )
    projected = jnp.dot(
        lax.all_gather(attended, "shard", axis=0, tiled=True),
        out_weight,
        preferred_element_type=jnp.float32,
    )
    stream = (residual.astype(jnp.float32) + projected).astype(jnp.bfloat16)
    wide = stream.astype(jnp.float32)
    square_sums = lax.psum(jnp.sum(wide * wide, axis=1), "shard")
    normed = (wide * lax.rsqrt(square_sums / D + norm_eps)[:, None] * norm_gain[None, :]).astype(
        jnp.bfloat16
    )
    block_cols = lax.all_gather(normed, "shard", axis=1, tiled=True)
    gate_acts = jnp.dot(block_cols, gate_weight, preferred_element_type=jnp.float32)
    up_acts = jnp.dot(block_cols, up_weight, preferred_element_type=jnp.float32)
    hidden = (jax.nn.silu(gate_acts) * up_acts).astype(jnp.bfloat16)
    partial_terms = jnp.dot(hidden, down_weight, preferred_element_type=jnp.float32)
    down_terms = lax.psum_scatter(partial_terms, "shard", scatter_dimension=1, tiled=True)
    return (wide + down_terms).astype(jnp.bfloat16)


GROUP = HEADS // KV_HEADS
HEAD_ROWS = 72
MIB = 2**20
VMEM_SPEC = pl.BlockSpec(memory_space=pltpu.VMEM)
SMEM_SPEC = pl.BlockSpec(memory_space=pltpu.SMEM)
HBM_SPEC = pl.BlockSpec(memory_space=pltpu.HBM)
CHUNK = 512


def sent(array, distance):
    size = lax.axis_size("shard")
    return lax.ppermute(array, "shard", [(i, i ^ distance) for i in range(size)])


def stack_kernel(count, *refs):
    out_ref, place = refs[-1], 0
    for part in refs[:count]:
        size = part.shape[0] if len(part.shape) == 3 else 1
        out_ref[place : place + size] = part[...].reshape((size,) + part.shape[-2:])
        place += size


def stacked(parts, after):
    size = sum(part.shape[0] if part.ndim == 3 else 1 for part in parts)
    return pl.pallas_call(
        functools.partial(stack_kernel, len(parts)),
        in_specs=[VMEM_SPEC] * len(parts) + [pl.BlockSpec(memory_space=pl.ANY)] * len(after),
        out_specs=VMEM_SPEC,
        out_shape=jax.ShapeDtypeStruct((size,) + parts[0].shape[-2:], parts[0].dtype),
        compiler_params=pltpu.CompilerParams(vmem_limit_bytes=4 * MIB),
        cost_estimate=pl.CostEstimate(flops=0, bytes_accessed=16 * MIB, transcendentals=0),
    )(*parts, *after)


def near_pieces(piece):
    return [piece] + [sent(piece, distance) for distance in (4, 8, 12)]


PEER = (0, 4, 8, 12, 2, 6, 10, 14)


def device_at(me, entry):
    return me ^ (PEER[entry % 8] + entry // 8)


def in_vmem(array):
    return pltpu.with_memory_space_constraint(array, pltpu.VMEM)


def in_hbm(array):
    return pltpu.with_memory_space_constraint(array, pltpu.HBM)


def two_terms(wide):
    high = wide.astype(jnp.bfloat16).astype(jnp.float32)
    return high, wide - high


def pack_kernel(query_hbm, gain_hbm, out_ref, rows_ref, query, gain, wide, sems):
    copies = [
        pltpu.make_async_copy(query_hbm, query, sems.at[0]),
        pltpu.make_async_copy(gain_hbm, gain, sems.at[1]),
    ]
    for copy in copies:
        copy.start()
    for copy in copies:
        copy.wait()
    rows = 2 * HEADS
    for head in range(HEADS):
        cols = slice(head * HEAD_DIM, (head + 1) * HEAD_DIM)
        wide[pl.ds(head, 2, HEADS), :] = query[:, cols].astype(jnp.float32)
    out_ref[:rows, :] = wide[...].astype(jnp.bfloat16)
    rows_ref[...] = wide[...].astype(jnp.bfloat16)
    high, rest = two_terms(gain[...])
    middle, low = two_terms(rest)
    filler = jnp.zeros((16 - 3 * high.shape[0], HEAD_DIM), jnp.float32)
    out_ref[rows:, :] = jnp.concatenate([high, middle, low, filler]).astype(jnp.bfloat16)


def packed(queries, norm_gain):
    rows = 2 * HEADS
    gain = norm_gain.reshape(-1, HEAD_DIM)
    return pl.pallas_call(
        pack_kernel,
        in_specs=[HBM_SPEC] * 2,
        out_specs=[VMEM_SPEC] * 2,
        out_shape=[
            jax.ShapeDtypeStruct((rows + 16, HEAD_DIM), jnp.bfloat16),
            jax.ShapeDtypeStruct((rows, HEAD_DIM), jnp.bfloat16),
        ],
        scratch_shapes=[
            pltpu.VMEM(queries.shape, jnp.bfloat16),
            pltpu.VMEM(gain.shape, jnp.float32),
            pltpu.VMEM((rows, HEAD_DIM), jnp.float32),
            pltpu.SemaphoreType.DMA((2,)),
        ],
        compiler_params=pltpu.CompilerParams(vmem_limit_bytes=4 * MIB),
    )(in_hbm(queries), in_hbm(gain))


def context_terms(query, keys, values, alive):
    numerators, denominators = [], []
    for head in range(KV_HEADS):
        cols = slice(head * HEAD_DIM, (head + 1) * HEAD_DIM)
        scores = lax.dot_general(
            query[head * GROUP : (head + 1) * GROUP],
            keys[:, cols],
            (((1,), (1,)), ((), ())),
            preferred_element_type=jnp.float32,
        ) * (1.0 / math.sqrt(HEAD_DIM))
        weights = jnp.where(alive, jnp.exp(scores), 0.0)
        denominators.append(jnp.sum(weights, axis=1, keepdims=True))
        numerators.append(
            jnp.dot(
                weights.astype(jnp.bfloat16), values[:, cols], preferred_element_type=jnp.float32
            )
        )
    return jnp.concatenate(numerators), jnp.concatenate(denominators)


def ready_kernel(table_ref, query_ref, pages_hbm, new_hbm, pages, found_ref, new_ref, of_second, new, sems):
    count, _, page_len, features = pages.shape
    sequences = 2 * 16
    per_row = (table_ref.shape[0] - 1) // sequences - 1
    me = table_ref[(per_row + 1) * sequences]
    copies = [pltpu.make_async_copy(new_hbm, new, sems.at[4])]
    for part in range(4):
        here = pl.ds(part * count // 4, count // 4)
        copies.append(
            pltpu.make_async_copy(pages_hbm.at[here], pages.at[here], sems.at[part])
        )
    for copy in copies:
        copy.start()
    found_ref[0] = me
    for entry in range(16):
        owner = device_at(me, entry)
        place = 0
        for index in range(2 * per_row):
            hit = table_ref[2 * owner * per_row + index] // count == me
            place = jnp.where(hit, index, place)
        slot = table_ref[2 * owner * per_row + place] % count
        row = place // per_row
        left = table_ref[sequences * per_row + 2 * owner + row] - page_len * (place % per_row)
        for place, value in enumerate((slot, row, left)):
            found_ref[1 + 3 * entry + place] = value
    for index in range(2 * per_row):
        holder = table_ref[2 * me * per_row + index] // count
        of_second[pl.ds(holder, 1), :] = jnp.full(
            (1, HEAD_DIM), index // per_row, dtype=jnp.float32
        )
    first_token = lax.broadcasted_iota(jnp.int32, (GROUP, 8), 1) < 1
    copies[0].wait()
    for row in range(2):
        lines = slice(row * HEADS, (row + 1) * HEADS)
        numerator, total = context_terms(
            query_ref[lines, :],
            jnp.broadcast_to(new[row, 0:1, :], (8, features)),
            jnp.broadcast_to(new[row, 1:2, :], (8, features)),
            first_token,
        )
        new_ref[0, lines, :] = numerator
        new_ref[1, lines, :] = jnp.broadcast_to(total, (HEADS, HEAD_DIM))
    for copy in copies[1:]:
        copy.wait()


def readied(table, query_rows, kv_pages, new_kv):
    return pl.pallas_call(
        ready_kernel,
        in_specs=[SMEM_SPEC, VMEM_SPEC] + [HBM_SPEC] * 2,
        out_specs=[VMEM_SPEC, SMEM_SPEC, VMEM_SPEC, VMEM_SPEC],
        out_shape=[
            pltpu.VMEM(kv_pages.shape, kv_pages.dtype),
            jax.ShapeDtypeStruct((49,), jnp.int32),
            jax.ShapeDtypeStruct((2, 2 * HEADS, HEAD_DIM), jnp.float32),
            jax.ShapeDtypeStruct((16, HEAD_DIM), jnp.float32),
        ],
        scratch_shapes=[pltpu.VMEM(new_kv.shape, jnp.bfloat16), pltpu.SemaphoreType.DMA((5,))],
        compiler_params=pltpu.CompilerParams(vmem_limit_bytes=4 * MIB),
        cost_estimate=pl.CostEstimate(flops=2**22, bytes_accessed=2**21, transcendentals=2**11),
    )(table, query_rows, in_hbm(kv_pages), in_hbm(new_kv))


def pages_kernel(entries, found_ref, *refs):
    refs = list(refs)
    near_ref, second_ref = (refs.pop(0), refs.pop(0)) if entries[0] == 0 else (None, None)
    odd_ref = None if entries[0] == 0 else refs.pop(0)
    pages = refs.pop(0)
    if entries[0] > 0:
        refs.pop(0)
    out_ref, scores, weights = refs
    page_len, features = pages.shape[2:]
    me = found_ref[0]
    line = lax.broadcasted_iota(jnp.int32, (HEADS, features), 0) // GROUP
    block = lax.broadcasted_iota(jnp.int32, (HEADS, features), 1) // HEAD_DIM
    own_block = (line == block).astype(jnp.float32).astype(jnp.bfloat16)
    slots = [found_ref[1 + 3 * entry] for entry in entries]
    for here, entry in enumerate(entries):
        source, place = piece_at(near_ref, second_ref, odd_ref, entry)
        row = found_ref[2 + 3 * entry]
        query = source[place, pl.ds(pl.multiple_of(row * HEADS, HEADS), HEADS), :]
        spread = jnp.concatenate([query] * KV_HEADS, axis=1) * own_block
        scores[here] = lax.dot_general(
            spread,
            pages[slots[here], 0],
            (((1,), (1,)), ((), ())),
            preferred_element_type=jnp.float32,
        )
    position = lax.broadcasted_iota(jnp.int32, (HEADS, page_len), 1)
    lane = lax.broadcasted_iota(jnp.int32, (HEADS, HEAD_DIM), 1)
    denominators = jnp.zeros((HEADS, HEAD_DIM), jnp.float32)
    for here, entry in enumerate(entries):
        raised = jnp.exp(scores[here] * (1.0 / math.sqrt(HEAD_DIM)))
        weight = jnp.where(position < found_ref[3 + 3 * entry], raised, 0.0)
        weights[here] = weight.astype(jnp.bfloat16)
        total = jnp.sum(weight, axis=1, keepdims=True)
        denominators = jnp.where(lane == here, total, denominators)
    for here, entry in enumerate(entries):
        numerator = jnp.dot(
            weights[here], pages[slots[here], 1], preferred_element_type=jnp.float32
        )
        for head in range(KV_HEADS):
            lines = slice(head * GROUP, (head + 1) * GROUP)
            out_ref[device_at(me, entry), lines, :] = numerator[
                lines, head * HEAD_DIM : (head + 1) * HEAD_DIM
            ].astype(jnp.bfloat16)
    high, low = two_terms(jnp.swapaxes(denominators, 0, 1)[: len(entries)])
    lasts = jnp.concatenate([high, low], axis=1)
    first_line = lax.broadcasted_iota(jnp.int32, (HEAD_ROWS - HEADS, HEAD_DIM), 0) == 0
    for here, entry in enumerate(entries):
        out_ref[device_at(me, entry), HEADS:, :] = jnp.where(
            first_line, lasts[here : here + 1], 0.0
        ).astype(jnp.bfloat16)


def piece_at(near, second, odd, entry):
    if entry < 4:
        return near, entry
    return (second, entry - 4) if entry < 8 else (odd, entry - 8)


def page_terms(found, entries, pieces, pages, before=()):
    return pl.pallas_call(
        functools.partial(pages_kernel, entries),
        in_specs=[SMEM_SPEC] + [VMEM_SPEC] * (len(pieces) + 1 + len(before)),
        out_specs=VMEM_SPEC,
        out_shape=jax.ShapeDtypeStruct((16, HEAD_ROWS, HEAD_DIM), jnp.bfloat16),
        scratch_shapes=[
            pltpu.VMEM((len(entries), HEADS, pages.shape[2]), jnp.float32),
            pltpu.VMEM((len(entries), HEADS, pages.shape[2]), jnp.bfloat16),
        ],
        input_output_aliases={len(pieces) + 2: 0} if before else {},
        compiler_params=pltpu.CompilerParams(vmem_limit_bytes=6 * MIB),
        cost_estimate=pl.CostEstimate(flops=2**26, bytes_accessed=2**20, transcendentals=2**14),
    )(found, *pieces, in_vmem(pages), *before)


def combine_kernel(arrived_ref, new_ref, of_second, out_ref):
    sums = [new_ref[0, row * HEADS : (row + 1) * HEADS, :] for row in range(2)]
    lower = [jnp.zeros((1, HEADS), jnp.float32)] * 2
    for sender in range(16):
        shares = of_second[sender : sender + 1, :]
        numerator = arrived_ref[sender, :HEADS, :].astype(jnp.float32)
        last = arrived_ref[sender, HEADS:, :].astype(jnp.float32)[:1]
        denominator = last[:, :HEADS] + last[:, HEADS:]
        for row, share in enumerate((1.0 - shares, shares)):
            sums[row] = sums[row] + numerator * share
            lower[row] = lower[row] + denominator * share[:, :HEADS]
    for row in range(2):
        lines = slice(row * HEADS, (row + 1) * HEADS)
        padded = jnp.concatenate([lower[row], jnp.zeros((1, HEADS), jnp.float32)], axis=1)
        column = jnp.swapaxes(jnp.broadcast_to(padded, (8, HEAD_DIM)), 0, 1)[:HEADS, :1]
        out_ref[lines, :] = (sums[row] / (column + new_ref[1, lines, :])).astype(jnp.bfloat16)


def combined(arrived, new_terms, of_second):
    return pl.pallas_call(
        combine_kernel,
        in_specs=[VMEM_SPEC] * 3,
        out_specs=VMEM_SPEC,
        out_shape=jax.ShapeDtypeStruct((2 * HEADS, HEAD_DIM), jnp.bfloat16),
        compiler_params=pltpu.CompilerParams(vmem_limit_bytes=10 * MIB),
        cost_estimate=pl.CostEstimate(flops=2**22, bytes_accessed=48*2**20, transcendentals=2**11),
    )(arrived, new_terms, of_second)


FETCHES = 8


def fetch_kernel(copies_of, me_ref, after_ref, weight_hbm, out_ref, sems):
    copies = [
        pltpu.make_async_copy(source, target, sems.at[place])
        for place, (source, target) in enumerate(copies_of(me_ref[0], weight_hbm, out_ref))
    ]
    for copy in copies:
        copy.start()
    for copy in copies:
        copy.wait()


def fetched(me, weight, shape, copies_of, after):
    size = math.prod(shape)
    return pl.pallas_call(
        functools.partial(fetch_kernel, copies_of),
        in_specs=[SMEM_SPEC, pl.BlockSpec(memory_space=pl.ANY), HBM_SPEC],
        out_specs=VMEM_SPEC,
        out_shape=pltpu.VMEM(shape, weight.dtype),
        scratch_shapes=[pltpu.SemaphoreType.DMA((FETCHES,))],
        compiler_params=pltpu.CompilerParams(vmem_limit_bytes=MIB),
        cost_estimate=pl.CostEstimate(flops=0, bytes_accessed=2 * size, transcendentals=0),
    )(me, after, in_hbm(weight))


def all_rows(me, weight_hbm, out_ref):
    rows = out_ref.shape[0] // FETCHES
    for part in range(FETCHES):
        here = pl.ds(part * rows, rows)
        yield weight_hbm.at[here], out_ref.at[here]


def device_rows(entries, me, weight_hbm, out_ref):
    for place, entry in enumerate(entries):
        here = pl.ds(pl.multiple_of(device_at(me, entry) * CHUNK, CHUNK), CHUNK)
        yield weight_hbm.at[here], out_ref.at[place]


def own_core_columns(me, weight_hbm, out_ref):
    for index in range(8):
        here = pl.ds(block_columns(me, index, 0), CHUNK)
        yield weight_hbm.at[:, here], out_ref.at[index]


def out_kernel(
    me_ref,
    near_ref,
    second_ref,
    odd_ref,
    weight_ref,
    residual_hbm,
    out_ref,
    wide,
    left,
    residual,
    sem,
):
    copy = pltpu.make_async_copy(residual_hbm, residual, sem)
    copy.start()
    me = me_ref[0]
    for entry in range(16):
        source, place = piece_at(near_ref, second_ref, odd_ref, entry)
        start = pl.multiple_of(device_at(me, entry) * 2 * HEADS, 2 * HEADS)
        wide[pl.ds(start, 2 * HEADS), :] = source[place].astype(jnp.float32)
    for head in range(HEADS):
        rows = [wide[pl.ds(row * HEADS + head, 16, 2 * HEADS), :] for row in range(2)]
        left[:, head * HEAD_DIM : (head + 1) * HEAD_DIM] = jnp.concatenate(rows).astype(
            jnp.bfloat16
        )
    depth = 1024
    total = jnp.zeros(out_ref.shape, jnp.float32)
    for start in range(0, D, depth):
        here = slice(start, start + depth)
        total += jnp.dot(left[:, here], weight_ref[here, :], preferred_element_type=jnp.float32)
    line = lax.broadcasted_iota(jnp.int32, (32, 32), 0)
    entry = lax.broadcasted_iota(jnp.int32, (32, 32), 1)
    turn = ((line % 2) * 16 + line // 2 == entry).astype(jnp.float32)
    turned = lax.dot_general(
        turn,
        total,
        (((1,), (0,)), ((), ())),
        precision=lax.Precision.HIGHEST,
        preferred_element_type=jnp.float32,
    )
    copy.wait()
    out_ref[...] = (residual[...].astype(jnp.float32) + turned).astype(jnp.bfloat16)


def projected(me, near, second, odd, residual, held_weight):
    rows, width = residual.shape
    return pl.pallas_call(
        out_kernel,
        in_specs=[SMEM_SPEC] + [VMEM_SPEC] * 4 + [HBM_SPEC],
        out_specs=VMEM_SPEC,
        out_shape=jax.ShapeDtypeStruct((rows, width), jnp.bfloat16),
        scratch_shapes=[
            pltpu.VMEM((32 * HEADS, HEAD_DIM), jnp.float32),
            pltpu.VMEM((rows, D), jnp.bfloat16),
            pltpu.VMEM((rows, width), jnp.bfloat16),
            pltpu.SemaphoreType.DMA,
        ],
        compiler_params=pltpu.CompilerParams(vmem_limit_bytes=4 * MIB),
        cost_estimate=pl.CostEstimate(
            flops=2 * rows * D * width, bytes_accessed=2 * D * width, transcendentals=0
        ),
    )(me, near, second, odd, held_weight, in_hbm(residual))


def block_columns(me, index, other):
    return pl.multiple_of((2 * index + (me % 2 ^ other)) * CHUNK, CHUNK)


def normed_pieces(entries, pieces, gain_ref, squares):
    lefts = []
    for place, entry in enumerate(entries):
        stream = pieces[place][...] if len(pieces) == len(entries) else pieces[0][place]
        wide = stream.astype(jnp.float32)
        squares = squares + wide * wide
        terms = gain_ref[entry % 4 if entry < 8 else entry - 8, 2 * HEADS :, :]
        terms = terms.astype(jnp.float32)
        gain = terms[0:4] + terms[4:8] + terms[8:12]
        gain = jnp.concatenate([gain[part : part + 1] for part in range(4)], axis=1)
        lefts.append((wide * gain).astype(jnp.bfloat16))
    return lefts, squares


def rows_of(me, entries):
    return [
        pl.ds(pl.multiple_of(device_at(me, entry) * CHUNK, CHUNK), CHUNK) for entry in entries
    ]


def add_terms(total, start, left, weight, place):
    terms = jnp.dot(left, weight, preferred_element_type=jnp.float32)
    if place > 0:
        total[...] += terms
    else:
        total[...] = terms if start is None else start[...] + terms


def feed_kernel(entries, piece_count, *refs):
    refs = list(refs)
    take = lambda number: [refs.pop(0) for _ in range(number)]
    (me_ref,) = take(1)
    pieces = take(piece_count)
    gain_ref, gate_hbm, up_hbm = take(3)
    gates_in, ups_in, squares_in = [None] * 3 if entries[0] == 0 else take(3)
    gates, ups, squares_out, gate_held, up_held, gate_sems, up_sems = refs
    gate_copies, up_copies = [], []
    for place, here in enumerate(rows_of(me_ref[0], entries)):
        gate_copies.append(
            pltpu.make_async_copy(gate_hbm.at[here], gate_held.at[place], gate_sems.at[place])
        )
        up_copies.append(
            pltpu.make_async_copy(up_hbm.at[here], up_held.at[place], up_sems.at[place])
        )
        gate_copies[place].start()
        up_copies[place].start()
    squares = 0.0 if squares_in is None else squares_in[...]
    lefts, squares_out[...] = normed_pieces(entries, pieces, gain_ref, squares)
    for place in range(len(entries)):
        gate_copies[place].wait()
        add_terms(gates, gates_in, lefts[place], gate_held[place], place)
        up_copies[place].wait()
        add_terms(ups, ups_in, lefts[place], up_held[place], place)


def feed(me, entries, pieces, gain, sums, gate_weight, up_weight):
    rows = pieces[0].shape[-2]
    width = gate_weight.shape[1]
    count = len(entries)
    total = jax.ShapeDtypeStruct((rows, width), jnp.float32)
    held = pltpu.VMEM((count, CHUNK, width), jnp.bfloat16)
    return pl.pallas_call(
        functools.partial(feed_kernel, entries, len(pieces)),
        in_specs=[SMEM_SPEC]
        + [VMEM_SPEC] * (len(pieces) + 1)
        + [HBM_SPEC] * 2
        + [VMEM_SPEC] * len(sums),
        out_specs=[VMEM_SPEC] * 3,
        out_shape=[total, total, jax.ShapeDtypeStruct((rows, CHUNK), jnp.float32)],
        scratch_shapes=[held, held] + [pltpu.SemaphoreType.DMA((count,))] * 2,
        compiler_params=pltpu.CompilerParams(
            vmem_limit_bytes=4 * count * CHUNK * width + 2 * MIB
        ),
        cost_estimate=pl.CostEstimate(
            flops=4 * rows * count * CHUNK * width,
            bytes_accessed=4 * count * CHUNK * width,
            transcendentals=0,
        ),
    )(me, *pieces, gain, in_hbm(gate_weight), in_hbm(up_weight), *sums)


def hidden_kernel(
    entries,
    me_ref,
    odd_ref,
    gain_ref,
    early,
    gate_hbm,
    up_hbm,
    down_hbm,
    gates_in,
    ups_in,
    squares_in,
    hidden_ref,
    out_ref,
    gates,
    ups,
    gate_held,
    up_held,
    down_held,
    gate_sems,
    up_sems,
    down_sems,
):
    me = me_ref[0]
    count, first = len(entries), early.shape[0]
    rows = rows_of(me, entries)
    gate_copies = [
        pltpu.make_async_copy(gate_hbm.at[here], gate_held.at[place], gate_sems.at[place])
        for place, here in enumerate(rows[first:])
    ]
    up_copies = [
        pltpu.make_async_copy(up_hbm.at[here], up_held.at[place], up_sems.at[place])
        for place, here in enumerate(rows)
    ]
    down_copies = [
        pltpu.make_async_copy(
            down_hbm.at[:, pl.ds(block_columns(me, index, 1), CHUNK)],
            down_held.at[index],
            down_sems.at[index],
        )
        for index in range(8)
    ]
    for place in range(count):
        up_copies[place].start()
        if place >= first:
            gate_copies[place - first].start()
    lefts, squares = normed_pieces(entries, [odd_ref], gain_ref, squares_in[...])
    for place in range(count):
        if place < first:
            weight = early[place]
        else:
            gate_copies[place - first].wait()
            weight = gate_held[place - first]
        add_terms(gates, gates_in, lefts[place], weight, place)
        up_copies[place].wait()
        add_terms(ups, ups_in, lefts[place], up_held[place], place)
        down_copies[place].start()
    scale = lax.rsqrt(jnp.sum(squares, axis=1, keepdims=True) / D + norm_eps)
    hidden_ref[...] = (jax.nn.silu(gates[...] * scale) * (ups[...] * scale)).astype(jnp.bfloat16)
    for index in range(8):
        down_copies[index].wait()
        out_ref[index] = jnp.dot(
            hidden_ref[...], down_held[index], preferred_element_type=jnp.float32
        ).astype(jnp.bfloat16)


def hidden_units(me, entries, odd, gain, early, gate_weight, up_weight, down_weight, sums):
    rows = odd.shape[1]
    width = gate_weight.shape[1]
    count = len(entries)
    later = count - early.shape[0]
    total = pltpu.VMEM((rows, width), jnp.float32)
    return pl.pallas_call(
        functools.partial(hidden_kernel, entries),
        in_specs=[SMEM_SPEC] + [VMEM_SPEC] * 3 + [HBM_SPEC] * 3 + [VMEM_SPEC] * 3,
        out_specs=[VMEM_SPEC] * 2,
        out_shape=[
            jax.ShapeDtypeStruct((rows, width), jnp.bfloat16),
            jax.ShapeDtypeStruct((8, rows, CHUNK), jnp.bfloat16),
        ],
        scratch_shapes=[
            total,
            total,
            pltpu.VMEM((later, CHUNK, width), jnp.bfloat16),
            pltpu.VMEM((count, CHUNK, width), jnp.bfloat16),
            pltpu.VMEM((8, width, CHUNK), jnp.bfloat16),
            pltpu.SemaphoreType.DMA((later,)),
            pltpu.SemaphoreType.DMA((count,)),
            pltpu.SemaphoreType.DMA((8,)),
        ],
        compiler_params=pltpu.CompilerParams(
            vmem_limit_bytes=2 * (later + count + 8) * CHUNK * width + 2 * MIB
        ),
        cost_estimate=pl.CostEstimate(
            flops=2 * rows * 3 * count * CHUNK * width,
            bytes_accessed=2 * 3 * count * CHUNK * width,
            transcendentals=rows * width,
        ),
    )(
        me,
        odd,
        gain,
        in_vmem(early),
        in_hbm(gate_weight),
        in_hbm(up_weight),
        in_hbm(down_weight),
        *sums,
    )


def down_kernel(hidden_ref, held_ref, out_ref):
    for index in range(8):
        out_ref[index] = jnp.dot(
            hidden_ref[...], held_ref[index], preferred_element_type=jnp.float32
        )


def own_core_terms(hidden, held):
    rows, depth = hidden.shape
    return pl.pallas_call(
        down_kernel,
        in_specs=[VMEM_SPEC] * 2,
        out_specs=VMEM_SPEC,
        out_shape=jax.ShapeDtypeStruct((8, rows, CHUNK), jnp.float32),
        compiler_params=pltpu.CompilerParams(vmem_limit_bytes=4 * MIB),
        cost_estimate=pl.CostEstimate(
            flops=rows * depth * D, bytes_accessed=depth * D, transcendentals=0
        ),
    )(hidden, in_vmem(held))


def pair_kernel(mine_ref, theirs_ref, out_ref):
    for index in range(8):
        out_ref[index] = (mine_ref[index] + theirs_ref[index].astype(jnp.float32)).astype(
            jnp.bfloat16
        )


def paired(mine, theirs):
    return pl.pallas_call(
        pair_kernel,
        in_specs=[VMEM_SPEC] * 2,
        out_specs=VMEM_SPEC,
        out_shape=jax.ShapeDtypeStruct(theirs.shape, jnp.bfloat16),
        compiler_params=pltpu.CompilerParams(vmem_limit_bytes=4 * MIB),
    )(mine, theirs)


def finish_kernel(stream_ref, shares_ref, out_ref):
    total = stream_ref[...].astype(jnp.float32)
    for index in range(8):
        total = total + shares_ref[index].astype(jnp.float32)
    out_ref[...] = total.astype(jnp.bfloat16)


def finished(stream, shares):
    return pl.pallas_call(
        finish_kernel,
        in_specs=[VMEM_SPEC] * 2,
        out_specs=VMEM_SPEC,
        out_shape=jax.ShapeDtypeStruct(stream.shape, jnp.bfloat16),
        compiler_params=pltpu.CompilerParams(vmem_limit_bytes=4 * MIB),
    )(stream, shares)


def block_body(
    queries,
    new_kv,
    kv_pages,
    page_table,
    lengths,
    residual,
    out_weight,
    norm_gain,
    gate_weight,
    up_weight,
    down_weight,
):
    me = lax.axis_index("shard").astype(jnp.int32)[None]
    table = jnp.concatenate([page_table.reshape(-1), lengths, me])
    own, query_rows = packed(queries, norm_gain)
    late = tuple(range(8, 16))
    early_shape = (5, CHUNK, gate_weight.shape[1])
    early = fetched(
        me, gate_weight, early_shape, functools.partial(device_rows, late[:5]), table
    )
    near = stacked(near_pieces(own), (early,))
    second = sent(near, 2)
    pages, found, new_terms, of_second = readied(table, query_rows, kv_pages, new_kv)
    odd = sent(stacked([near, second], (new_terms,)), 1)
    gains = near, second, odd
    terms = page_terms(found, tuple(range(8)), (near, second), pages)
    terms = page_terms(found, late, (odd,), pages, (terms,))
    arrived = lax.all_to_all(terms, "shard", 0, 0)
    attended = combined(arrived, new_terms, of_second)
    near = stacked(near_pieces(attended), ())
    second = sent(near, 2)
    down_shape = (8, down_weight.shape[0], CHUNK)
    down_held = fetched(me, down_weight, down_shape, own_core_columns, near)
    odd = sent(stacked([near, second], (down_held,)), 1)
    stream = projected(me, near, second, odd, residual, out_weight)
    weights = gate_weight, up_weight
    near = near_pieces(stream)
    sums = feed(me, (0,), near[:1], gains[0], (), *weights)
    first = stacked(near, sums[:1])
    second = sent(first, 2)
    sums = feed(me, (1, 2, 3), near[1:], gains[0], sums, *weights)
    odd = sent(stacked([first, second], sums[:1]), 1)
    sums = feed(me, (4, 5, 6, 7), [second], gains[1], sums, *weights)
    hidden, theirs = hidden_units(me, late, odd, gains[2], early, *weights, down_weight, sums)
    theirs = sent(theirs, 1)
    pairs = paired(own_core_terms(hidden, down_held), theirs)
    same_core = [[core + 2 * step for step in range(8)] for core in range(2)]
    shares = lax.all_to_all(pairs, "shard", 0, 0, axis_index_groups=same_core)
    return finished(stream, shares)


def solution(mesh):
    placed = (
        P(("groups", "shard"), None),
        P(("groups", "shard"), None, None),
        P(("groups", "shard"), None, None, None),
        P("groups", None),
        P("groups"),
        P("groups", "shard"),
        P(None, "shard"),
        P("shard"),
        P(None, "shard"),
        P(None, "shard"),
        P("shard", None),
    )
    chosen = block_body if mesh.shape["shard"] == 16 else body
    return jax.shard_map(
        chosen, mesh=mesh, in_specs=placed, out_specs=P("groups", "shard"), check_vma=False
    )
```

```python
import functools
import math

import jax
import jax.numpy as jnp
from jax import lax
from jax.experimental import pallas as pl
from jax.experimental.pallas import tpu as pltpu
from jax.sharding import PartitionSpec as P

D = 8192
HEADS = 64
KV_HEADS = 4
HEAD_DIM = 128


norm_eps = 1e-05


def swapped(array, axis, distance):
    return lax.ppermute(array, axis, [(i, i ^ 1 << distance) for i in range(lax.axis_size(axis))])


def new_token_terms(queries, new_kv, score_scale):
    seq_dev = queries.shape[0]
    group_size = HEADS // KV_HEADS
    query_heads = queries.reshape(seq_dev, KV_HEADS, group_size, HEAD_DIM)
    new_keys = new_kv[:, 0].reshape(seq_dev, KV_HEADS, HEAD_DIM)
    new_values = new_kv[:, 1].reshape(seq_dev, KV_HEADS, HEAD_DIM)
    scores = (
        jnp.einsum("bgqd,bgd->bgq", query_heads, new_keys, preferred_element_type=jnp.float32)
        * score_scale
    )
    weights = jnp.exp(scores)
    numerator = jnp.einsum(
        "bgq,bgd->bgqd",
        weights.astype(jnp.bfloat16),
        new_values,
        preferred_element_type=jnp.float32,
    )
    return (numerator.reshape(seq_dev, D), weights.reshape(seq_dev, HEADS))


def butterfly(items, position, mover):
    count = items[0].shape[0]
    for level in range(count.bit_length() - 1):
        upper_half = position // (1 << level) % 2 == 1
        halves = [
            entry.reshape((count >> level + 1, 2, 1 << level) + entry.shape[1:]) for entry in items
        ]
        outgoing = tuple(
            (jnp.where(upper_half, halves_one[:, 0], halves_one[:, 1]) for halves_one in halves)
        )
        incoming = mover(outgoing, level)
        rebuilt = []
        for entry, halves_one, arrived_one in zip(items, halves, incoming):
            lower_part = jnp.where(upper_half, arrived_one, halves_one[:, 0])
            upper_part = jnp.where(upper_half, halves_one[:, 1], arrived_one)
            rebuilt.append(jnp.stack([lower_part, upper_part], axis=1).reshape(entry.shape))
        items = tuple(rebuilt)
    return items


def body(
    queries,
    new_kv,
    kv_pages,
    page_table,
    lengths,
    residual,
    out_weight,
    norm_gain,
    gate_weight,
    up_weight,
    down_weight,
):
    seq_dev = queries.shape[0]
    page_count = kv_pages.shape[0]
    page_len = kv_pages.shape[2]
    all_seqs = page_table.shape[0]
    max_pages = page_table.shape[1]
    group_size = HEADS // KV_HEADS
    score_scale = 1.0 / math.sqrt(HEAD_DIM)
    device_pos = lax.axis_index("shard")
    own_first = device_pos * seq_dev
    own_lengths = lax.dynamic_slice_in_dim(lengths, own_first, seq_dev, 0)
    own_table = lax.dynamic_slice_in_dim(page_table, own_first, seq_dev, 0)
    holder_local = own_table // page_count % page_count
    page_ids = device_pos * page_count + jnp.arange(page_count, dtype=jnp.int32)
    matches = page_table[None, :, :] == page_ids[:, None, None]
    seq_of = jnp.sum(
        jnp.where(matches, jnp.arange(all_seqs, dtype=jnp.int32)[None, :, None], 0), axis=(1, 2)
    )
    owner_local = seq_of // seq_dev % page_count
    own_numerator, own_denominator = new_token_terms(queries, new_kv, score_scale)
    outgoing = jnp.zeros_like(kv_pages).at[owner_local].set(kv_pages)
    arrived = butterfly(
        (outgoing,), device_pos, lambda sending, level: (swapped(sending[0], "shard", level),)
    )[0]
    fetched = arrived[holder_local]
    context = max_pages * page_len
    key_rows = fetched[:, :, 0].reshape(seq_dev, context, KV_HEADS, HEAD_DIM)
    value_rows = fetched[:, :, 1].reshape(seq_dev, context, KV_HEADS, HEAD_DIM)
    query_heads = queries.reshape(seq_dev, KV_HEADS, group_size, HEAD_DIM)
    scores = (
        jnp.einsum("bgqd,btgd->bgqt", query_heads, key_rows, preferred_element_type=jnp.float32)
        * score_scale
    )
    position = jnp.arange(context, dtype=jnp.int32)
    alive = position[None, :] < own_lengths[:, None]
    weights = jnp.where(alive[:, None, None, :], jnp.exp(scores), 0.0)
    denominator = jnp.sum(weights, axis=-1).reshape(seq_dev, HEADS)
    numerator = jnp.einsum(
        "bgqt,btgd->bgqd",
        weights.astype(jnp.bfloat16),
        value_rows,
        preferred_element_type=jnp.float32,
    )
    numer_rows = numerator.reshape(seq_dev, D) + own_numerator
    denom_rows = denominator + own_denominator
    attended = (
        (numer_rows.reshape(seq_dev, HEADS, HEAD_DIM) / denom_rows[:, :, None])
        .reshape(seq_dev, D)
        .astype(jnp.bfloat16)
    )
    projected = jnp.dot(
        lax.all_gather(attended, "shard", axis=0, tiled=True),
        out_weight,
        preferred_element_type=jnp.float32,
    )
    stream = (residual.astype(jnp.float32) + projected).astype(jnp.bfloat16)
    wide = stream.astype(jnp.float32)
    square_sums = lax.psum(jnp.sum(wide * wide, axis=1), "shard")
    normed = (wide * lax.rsqrt(square_sums / D + norm_eps)[:, None] * norm_gain[None, :]).astype(
        jnp.bfloat16
    )
    block_cols = lax.all_gather(normed, "shard", axis=1, tiled=True)
    gate_acts = jnp.dot(block_cols, gate_weight, preferred_element_type=jnp.float32)
    up_acts = jnp.dot(block_cols, up_weight, preferred_element_type=jnp.float32)
    hidden = (jax.nn.silu(gate_acts) * up_acts).astype(jnp.bfloat16)
    partial_terms = jnp.dot(hidden, down_weight, preferred_element_type=jnp.float32)
    down_terms = lax.psum_scatter(partial_terms, "shard", scatter_dimension=1, tiled=True)
    return (wide + down_terms).astype(jnp.bfloat16)


GROUP = HEADS // KV_HEADS
HEAD_ROWS = 72
MIB = 2**20
VMEM_SPEC = pl.BlockSpec(memory_space=pltpu.VMEM)
SMEM_SPEC = pl.BlockSpec(memory_space=pltpu.SMEM)
HBM_SPEC = pl.BlockSpec(memory_space=pltpu.HBM)
CHUNK = 512


def sent(array, distance):
    size = lax.axis_size("shard")
    return lax.ppermute(array, "shard", [(i, i ^ distance) for i in range(size)])


def stack_kernel(count, *refs):
    out_ref, place = refs[-1], 0
    for part in refs[:count]:
        size = part.shape[0] if len(part.shape) == 3 else 1
        out_ref[place : place + size] = part[...].reshape((size,) + part.shape[-2:])
        place += size


def stacked(parts, after):
    size = sum(part.shape[0] if part.ndim == 3 else 1 for part in parts)
    return pl.pallas_call(
        functools.partial(stack_kernel, len(parts)),
        in_specs=[VMEM_SPEC] * len(parts) + [pl.BlockSpec(memory_space=pl.ANY)] * len(after),
        out_specs=VMEM_SPEC,
        out_shape=jax.ShapeDtypeStruct((size,) + parts[0].shape[-2:], parts[0].dtype),
        compiler_params=pltpu.CompilerParams(vmem_limit_bytes=4 * MIB),
        cost_estimate=pl.CostEstimate(flops=0, bytes_accessed=16 * MIB, transcendentals=0),
    )(*parts, *after)


def near_pieces(piece):
    return [piece] + [sent(piece, distance) for distance in (4, 8, 12)]


def device_at(me, entry):
    return me ^ (entry % 4 * 4 + entry // 4 % 2 * 2 + entry // 8)


def started(count, copy_at):
    def start(place, carry):
        copy_at(place).start()
        return carry

    lax.fori_loop(0, count, start, 0)


def in_vmem(array):
    return pltpu.with_memory_space_constraint(array, pltpu.VMEM)


def in_hbm(array):
    return pltpu.with_memory_space_constraint(array, pltpu.HBM)


def two_terms(wide):
    high = wide.astype(jnp.bfloat16).astype(jnp.float32)
    return high, wide - high


def pack_kernel(query_hbm, gain_hbm, out_ref, rows_ref, query, gain, wide, sems):
    copies = [
        pltpu.make_async_copy(query_hbm, query, sems.at[0]),
        pltpu.make_async_copy(gain_hbm, gain, sems.at[1]),
    ]
    for copy in copies:
        copy.start()
    for copy in copies:
        copy.wait()
    rows = 2 * HEADS
    for head in range(HEADS):
        cols = slice(head * HEAD_DIM, (head + 1) * HEAD_DIM)
        wide[pl.ds(head, 2, HEADS), :] = query[:, cols].astype(jnp.float32)
    out_ref[:rows, :] = wide[...].astype(jnp.bfloat16)
    rows_ref[...] = wide[...].astype(jnp.bfloat16)
    high, rest = two_terms(gain[...])
    middle, low = two_terms(rest)
    filler = jnp.zeros((16 - 3 * high.shape[0], HEAD_DIM), jnp.float32)
    out_ref[rows:, :] = jnp.concatenate([high, middle, low, filler]).astype(jnp.bfloat16)


def packed(queries, norm_gain):
    rows = 2 * HEADS
    gain = norm_gain.reshape(-1, HEAD_DIM)
    return pl.pallas_call(
        pack_kernel,
        in_specs=[HBM_SPEC] * 2,
        out_specs=[VMEM_SPEC] * 2,
        out_shape=[
            jax.ShapeDtypeStruct((rows + 16, HEAD_DIM), jnp.bfloat16),
            jax.ShapeDtypeStruct((rows, HEAD_DIM), jnp.bfloat16),
        ],
        scratch_shapes=[
            pltpu.VMEM(queries.shape, jnp.bfloat16),
            pltpu.VMEM(gain.shape, jnp.float32),
            pltpu.VMEM((rows, HEAD_DIM), jnp.float32),
            pltpu.SemaphoreType.DMA((2,)),
        ],
        compiler_params=pltpu.CompilerParams(vmem_limit_bytes=4 * MIB),
    )(in_hbm(queries), in_hbm(gain))


def context_terms(query, keys, values, alive):
    numerators, denominators = [], []
    for head in range(KV_HEADS):
        cols = slice(head * HEAD_DIM, (head + 1) * HEAD_DIM)
        scores = lax.dot_general(
            query[head * GROUP : (head + 1) * GROUP],
            keys[:, cols],
            (((1,), (1,)), ((), ())),
            preferred_element_type=jnp.float32,
        ) * (1.0 / math.sqrt(HEAD_DIM))
        weights = jnp.where(alive, jnp.exp(scores), 0.0)
        denominators.append(jnp.sum(weights, axis=1, keepdims=True))
        numerators.append(
            jnp.dot(
                weights.astype(jnp.bfloat16), values[:, cols], preferred_element_type=jnp.float32
            )
        )
    return jnp.concatenate(numerators), jnp.concatenate(denominators)


def ready_kernel(table_ref, query_ref, pages_hbm, new_hbm, pages, left_ref, second_ref, new_ref, new, sems):
    _, _, page_len, features = pages.shape
    count = pages_hbm.shape[0]
    sequences = 2 * 16
    per_row = (table_ref.shape[0] - 1) // sequences - 1
    me = table_ref[(per_row + 1) * sequences]
    new_copy = pltpu.make_async_copy(new_hbm, new, sems.at[16])
    new_copy.start()
    page_copy = lambda slot, entry: pltpu.make_async_copy(
        pages_hbm.at[slot], pages.at[entry], sems.at[entry]
    )
    line = lambda value: jnp.full((1, HEAD_DIM), value, dtype=jnp.int32)

    def ready(entry, carry):
        owner = device_at(me, entry)
        place, other = 0, 0
        for index in range(2 * per_row):
            holder = table_ref[2 * owner * per_row + index] // count
            place = jnp.where(holder == me, index, place)
            other = jnp.where(holder == me ^ 1, index, other)
        row = place // per_row
        slot = table_ref[2 * owner * per_row + place] % count
        page_copy(slot, entry).start()
        left = table_ref[sequences * per_row + 2 * owner + row] - page_len * (place % per_row)
        here = pl.ds(entry, 1)
        left_ref[here, :] = line(left)
        second_ref[here, :] = line(row)
        second_ref[pl.ds(16 + entry, 1), :] = line(other // per_row)
        return carry

    lax.fori_loop(0, 16, ready, 0)
    first_token = lax.broadcasted_iota(jnp.int32, (GROUP, 8), 1) < 1
    new_copy.wait()
    for row in range(2):
        lines = slice(row * HEADS, (row + 1) * HEADS)
        numerator, total = context_terms(
            query_ref[lines, :],
            jnp.broadcast_to(new[row, 0:1, :], (8, features)),
            jnp.broadcast_to(new[row, 1:2, :], (8, features)),
            first_token,
        )
        new_ref[0, lines, :] = numerator
        new_ref[1, lines, :] = jnp.broadcast_to(total, (HEADS, HEAD_DIM))
    for entry in range(16):
        page_copy(0, entry).wait()


def readied(table, query_rows, kv_pages, new_kv):
    return pl.pallas_call(
        ready_kernel,
        in_specs=[SMEM_SPEC, VMEM_SPEC] + [HBM_SPEC] * 2,
        out_specs=[VMEM_SPEC] * 4,
        out_shape=[
            pltpu.VMEM(kv_pages.shape, kv_pages.dtype),
            jax.ShapeDtypeStruct((16, HEAD_DIM), jnp.int32),
            jax.ShapeDtypeStruct((32, HEAD_DIM), jnp.int32),
            jax.ShapeDtypeStruct((2, 2 * HEADS, HEAD_DIM), jnp.float32),
        ],
        scratch_shapes=[pltpu.VMEM(new_kv.shape, jnp.bfloat16), pltpu.SemaphoreType.DMA((17,))],
        compiler_params=pltpu.CompilerParams(vmem_limit_bytes=4 * MIB),
        cost_estimate=pl.CostEstimate(flops=2**22, bytes_accessed=2**21, transcendentals=2**11),
    )(table, query_rows, in_hbm(kv_pages), in_hbm(new_kv))


def pages_kernel(entries, left_ref, second_ref, *refs):
    refs = list(refs)
    near, across = (refs.pop(0), refs.pop(0)) if entries[0] < 8 else (None, None)
    odd = None if entries[0] < 8 else refs.pop(0)
    pages, out_ref, scores, weights = refs[0], *refs[-3:]
    page_len, features = pages.shape[2:]
    line = lax.broadcasted_iota(jnp.int32, (HEADS, features), 0) // GROUP
    block = lax.broadcasted_iota(jnp.int32, (HEADS, features), 1) // HEAD_DIM
    own_block = (line == block).astype(jnp.float32).astype(jnp.bfloat16)
    for here, entry in enumerate(entries):
        source, place = piece_at(near, across, odd, entry)
        second = second_ref[entry : entry + 1, :].astype(jnp.float32)
        query = source[place, :HEADS, :].astype(jnp.float32) * (1.0 - second)
        query += source[place, HEADS : 2 * HEADS, :].astype(jnp.float32) * second
        query = query.astype(jnp.bfloat16)
        spread = jnp.concatenate([query] * KV_HEADS, axis=1) * own_block
        scores[here] = lax.dot_general(
            spread,
            pages[entry, 0],
            (((1,), (1,)), ((), ())),
            preferred_element_type=jnp.float32,
        )
    position = lax.broadcasted_iota(jnp.int32, (HEADS, page_len), 1)
    lane = lax.broadcasted_iota(jnp.int32, (HEADS, HEAD_DIM), 1)
    denominators = jnp.zeros((HEADS, HEAD_DIM), jnp.float32)
    for here, entry in enumerate(entries):
        raised = jnp.exp(scores[here] * (1.0 / math.sqrt(HEAD_DIM)))
        weight = jnp.where(position < left_ref[entry : entry + 1, :page_len], raised, 0.0)
        weights[here] = weight.astype(jnp.bfloat16)
        total = jnp.sum(weight, axis=1, keepdims=True)
        denominators = jnp.where(lane == here, total, denominators)
    for here, entry in enumerate(entries):
        numerator = jnp.dot(
            weights[here], pages[entry, 1], preferred_element_type=jnp.float32
        )
        for head in range(KV_HEADS):
            lines = slice(head * GROUP, (head + 1) * GROUP)
            out_ref[here, lines, :] = numerator[
                lines, head * HEAD_DIM : (head + 1) * HEAD_DIM
            ].astype(jnp.bfloat16)
    high, low = two_terms(jnp.swapaxes(denominators, 0, 1)[: len(entries)])
    lasts = jnp.concatenate([high, low], axis=1)
    first_line = lax.broadcasted_iota(jnp.int32, (HEAD_ROWS - HEADS, HEAD_DIM), 0) == 0
    for here, entry in enumerate(entries):
        out_ref[here, HEADS:, :] = jnp.where(
            first_line, lasts[here : here + 1], 0.0
        ).astype(jnp.bfloat16)


def piece_at(near, second, odd, entry):
    if entry < 4:
        return near, entry
    return (second, entry - 4) if entry < 8 else (odd, entry - 8)


def page_terms(left, second, entries, pieces, pages, beside=()):
    return pl.pallas_call(
        functools.partial(pages_kernel, entries),
        in_specs=[VMEM_SPEC] * (len(pieces) + 3)
        + [pl.BlockSpec(memory_space=pl.ANY)] * len(beside),
        out_specs=VMEM_SPEC,
        out_shape=jax.ShapeDtypeStruct((len(entries), HEAD_ROWS, HEAD_DIM), jnp.bfloat16),
        scratch_shapes=[
            pltpu.VMEM((len(entries), HEADS, pages.shape[2]), jnp.float32),
            pltpu.VMEM((len(entries), HEADS, pages.shape[2]), jnp.bfloat16),
        ],
        compiler_params=pltpu.CompilerParams(vmem_limit_bytes=6 * MIB),
        cost_estimate=pl.CostEstimate(flops=2**26, bytes_accessed=2**20, transcendentals=2**14),
    )(left, second, *pieces, in_vmem(pages), *beside)


def opened(piece):
    last = piece[HEADS:, :].astype(jnp.float32)[:1]
    return piece[:HEADS, :].astype(jnp.float32), last[:, :HEADS] + last[:, HEADS:]


def closed(numerator, denominator):
    last = jnp.concatenate(two_terms(denominator), axis=1)
    first_line = lax.broadcasted_iota(jnp.int32, (HEAD_ROWS - HEADS, HEAD_DIM), 0) == 0
    return numerator.astype(jnp.bfloat16), jnp.where(first_line, last, 0.0).astype(jnp.bfloat16)


def two_rows(second_ref, entry, mine, theirs):
    sums = [[0.0, 0.0], [0.0, 0.0]]
    for line, (numerator, denominator) in zip((entry, 16 + entry), (mine, theirs)):
        second = second_ref[line : line + 1, :].astype(jnp.float32)
        for row, share in enumerate((1.0 - second, second)):
            sums[row][0] = sums[row][0] + numerator * share
            sums[row][1] = sums[row][1] + denominator * share[:, :HEADS]
    return sums


def core_kernel(second_ref, mine_ref, theirs_ref, out_ref):
    for place in range(4):
        mine, theirs = opened(mine_ref[place]), opened(theirs_ref[4 + place])
        for row, terms in enumerate(two_rows(second_ref, 4 + place, mine, theirs)):
            out_ref[place, row, :HEADS, :], out_ref[place, row, HEADS:, :] = closed(*terms)


def across_core(second, mine, theirs):
    return pl.pallas_call(
        core_kernel,
        in_specs=[VMEM_SPEC] * 3,
        out_specs=VMEM_SPEC,
        out_shape=jax.ShapeDtypeStruct((4, 2, HEAD_ROWS, HEAD_DIM), jnp.bfloat16),
        compiler_params=pltpu.CompilerParams(vmem_limit_bytes=4 * MIB),
    )(second, mine, theirs)


def chip_kernel(second_ref, mine_ref, theirs_ref, arrived_ref, unused_ref, *out_refs):
    for place in range(4):
        mine, theirs = opened(mine_ref[place]), opened(theirs_ref[place])
        for row, terms in enumerate(two_rows(second_ref, place, mine, theirs)):
            numerator, denominator = opened(arrived_ref[place, row])
            sums = closed(terms[0] + numerator, terms[1] + denominator)
            out_refs[place][row, :HEADS, :], out_refs[place][row, HEADS:, :] = sums


def across_y(second, mine, theirs, arrived, beside):
    return pl.pallas_call(
        chip_kernel,
        in_specs=[VMEM_SPEC] * 4 + [pl.BlockSpec(memory_space=pl.ANY)],
        out_specs=[VMEM_SPEC] * 4,
        out_shape=[jax.ShapeDtypeStruct((2, HEAD_ROWS, HEAD_DIM), jnp.bfloat16)] * 4,
        compiler_params=pltpu.CompilerParams(vmem_limit_bytes=4 * MIB),
    )(second, mine, theirs, arrived, beside)


def combine_kernel(*refs):
    shares, new_ref, out_ref = refs[:4], refs[4], refs[-1]
    for row in range(2):
        lines = slice(row * HEADS, (row + 1) * HEADS)
        total, lower = new_ref[0, lines, :], jnp.zeros((1, HEADS), jnp.float32)
        for share in shares:
            numerator, denominator = opened(share[row])
            total = total + numerator
            lower = lower + denominator
        padded = jnp.concatenate([lower, jnp.zeros((1, HEADS), jnp.float32)], axis=1)
        column = jnp.swapaxes(jnp.broadcast_to(padded, (8, HEAD_DIM)), 0, 1)[:HEADS, :1]
        out_ref[lines, :] = (total / (column + new_ref[1, lines, :])).astype(jnp.bfloat16)


def combined(shares, new_terms, beside):
    return pl.pallas_call(
        combine_kernel,
        in_specs=[VMEM_SPEC] * 5 + [pl.BlockSpec(memory_space=pl.ANY)],
        out_specs=VMEM_SPEC,
        out_shape=jax.ShapeDtypeStruct((2 * HEADS, HEAD_DIM), jnp.bfloat16),
        compiler_params=pltpu.CompilerParams(vmem_limit_bytes=4 * MIB),
        cost_estimate=pl.CostEstimate(
            flops=2**22, bytes_accessed=48 * MIB, transcendentals=2**11
        ),
    )(*shares, new_terms, beside)


def fetch_kernel(parts, after_ref, *refs):
    weights, outs, sems = refs[: len(parts)], refs[len(parts) : -1], refs[-1]
    me = lax.axis_index("shard")
    copies = []
    for (place_of, entries), weight_hbm, out_ref in zip(parts, weights, outs):
        for place, entry in enumerate(entries):
            copies.append(
                pltpu.make_async_copy(
                    place_of(weight_hbm, device_at(me, entry)),
                    out_ref.at[place],
                    sems.at[len(copies)],
                )
            )
    for copy in copies:
        copy.start()
    for copy in copies:
        copy.wait()


def fetched(after, *parts):
    count = sum(len(entries) for _, _, entries in parts)
    weights = [weight for weight, _, _ in parts]
    shapes = [
        pltpu.VMEM((len(entries),) + place_of(weight, None), weight.dtype)
        for weight, place_of, entries in parts
    ]
    size = sum(math.prod(shape.shape) for shape in shapes)
    return pl.pallas_call(
        functools.partial(fetch_kernel, [part[1:] for part in parts]),
        in_specs=[pl.BlockSpec(memory_space=pl.ANY)] + [HBM_SPEC] * len(parts),
        out_specs=[VMEM_SPEC] * len(parts),
        out_shape=shapes,
        scratch_shapes=[pltpu.SemaphoreType.DMA((count,))],
        compiler_params=pltpu.CompilerParams(vmem_limit_bytes=MIB),
        cost_estimate=pl.CostEstimate(flops=0, bytes_accessed=2 * size, transcendentals=0),
    )(after, *[in_hbm(weight) for weight in weights])


def rows_at(weight, device):
    if device is None:
        return (CHUNK, weight.shape[1])
    return weight.at[pl.ds(pl.multiple_of(device * CHUNK, CHUNK), CHUNK)]


def columns_at(weight, device):
    if device is None:
        return (weight.shape[0], CHUNK)
    return weight.at[:, pl.ds(pl.multiple_of(device * CHUNK, CHUNK), CHUNK)]


def out_kernel(
    near_ref,
    second_ref,
    odd_ref,
    weight_ref,
    residual,
    out_ref,
    wide,
    left,
):
    me = lax.axis_index("shard")
    for entry in range(16):
        source, place = piece_at(near_ref, second_ref, odd_ref, entry)
        start = pl.multiple_of(device_at(me, entry) * 2 * HEADS, 2 * HEADS)
        wide[pl.ds(start, 2 * HEADS), :] = source[place].astype(jnp.float32)
    for head in range(HEADS):
        rows = [wide[pl.ds(row * HEADS + head, 16, 2 * HEADS), :] for row in range(2)]
        left[:, head * HEAD_DIM : (head + 1) * HEAD_DIM] = jnp.concatenate(rows).astype(
            jnp.bfloat16
        )
    total = jnp.dot(left[...], weight_ref[...], preferred_element_type=jnp.float32)
    line = lax.broadcasted_iota(jnp.int32, (32, 32), 0)
    entry = lax.broadcasted_iota(jnp.int32, (32, 32), 1)
    turn = ((line % 2) * 16 + line // 2 == entry).astype(jnp.float32)
    turned = lax.dot_general(
        turn,
        total,
        (((1,), (0,)), ((), ())),
        precision=lax.Precision.HIGHEST,
        preferred_element_type=jnp.float32,
    )
    out_ref[...] = (residual[...].astype(jnp.float32) + turned).astype(jnp.bfloat16)


def projected(near, second, odd, residual, held_weight):
    rows, width = residual.shape
    return pl.pallas_call(
        out_kernel,
        in_specs=[VMEM_SPEC] * 5,
        out_specs=VMEM_SPEC,
        out_shape=jax.ShapeDtypeStruct((rows, width), jnp.bfloat16),
        scratch_shapes=[
            pltpu.VMEM((32 * HEADS, HEAD_DIM), jnp.float32),
            pltpu.VMEM((rows, D), jnp.bfloat16),
        ],
        compiler_params=pltpu.CompilerParams(vmem_limit_bytes=4 * MIB),
        cost_estimate=pl.CostEstimate(
            flops=2 * rows * D * width, bytes_accessed=2 * D * width, transcendentals=0
        ),
    )(near, second, odd, held_weight, residual)


def normed_pieces(entries, pieces, gain_ref, squares):
    lefts = []
    for place, entry in enumerate(entries):
        stream = pieces[place][...] if len(pieces) == len(entries) else pieces[0][place]
        wide = stream.astype(jnp.float32)
        squares = squares + wide * wide
        terms = gain_ref[entry % 4 if entry < 8 else entry - 8, 2 * HEADS :, :]
        terms = terms.astype(jnp.float32)
        gain = terms[0:4] + terms[4:8] + terms[8:12]
        gain = jnp.concatenate([gain[part : part + 1] for part in range(4)], axis=1)
        lefts.append((wide * gain).astype(jnp.bfloat16))
    return lefts, squares


def terms_of(lefts, blocks):
    left = jnp.concatenate(lefts, axis=1)
    weight = blocks[...].reshape(left.shape[1], blocks.shape[-1])
    return jnp.dot(left, weight, preferred_element_type=jnp.float32)


def feed_kernel(entries, piece_count, held, *refs):
    refs = list(refs)
    take = lambda number: [refs.pop(0) for _ in range(number)]
    pieces = take(piece_count)
    gain_ref, gate_ref, up_ref = take(3)
    gates_in, ups_in, squares_in = [None] * 3 if entries[0] == 0 else take(3)
    gates, ups, squares_out = take(3)
    copies = []
    if not held:
        sources = gate_ref, up_ref
        *targets, sems = refs
        gate_ref, up_ref = targets
        me = lax.axis_index("shard")
        count = len(entries)
        copies = [
            lambda place, number=number: pltpu.make_async_copy(
                rows_at(sources[number], device_at(me, entries[0] + place)),
                targets[number].at[place],
                sems.at[number * count + place],
            )
            for number in range(2)
        ]
        for copy_at in copies:
            started(count, copy_at)
    squares = 0.0 if squares_in is None else squares_in[...]
    lefts, squares_out[...] = normed_pieces(entries, pieces, gain_ref, squares)
    for number, (total, start, blocks) in enumerate(
        ((gates, gates_in, gate_ref), (ups, ups_in, up_ref))
    ):
        for place in range(len(entries) if copies else 0):
            copies[number](place).wait()
        terms = terms_of(lefts, blocks)
        total[...] = terms if start is None else start[...] + terms


def feed(entries, pieces, gain, sums, gate_weight, up_weight, held=False):
    rows = pieces[0].shape[-2]
    width = gate_weight.shape[-1]
    count = len(entries)
    total = jax.ShapeDtypeStruct((rows, width), jnp.float32)
    here = in_vmem if held else in_hbm
    slots = pltpu.VMEM((count, CHUNK, width), jnp.bfloat16)
    return pl.pallas_call(
        functools.partial(feed_kernel, entries, len(pieces), held),
        in_specs=[VMEM_SPEC] * (len(pieces) + 1)
        + [VMEM_SPEC if held else HBM_SPEC] * 2
        + [VMEM_SPEC] * len(sums),
        out_specs=[VMEM_SPEC] * 3,
        out_shape=[total, total, jax.ShapeDtypeStruct((rows, CHUNK), jnp.float32)],
        scratch_shapes=[] if held else [slots, slots, pltpu.SemaphoreType.DMA((2 * count,))],
        compiler_params=pltpu.CompilerParams(
            vmem_limit_bytes=2 * MIB + (0 if held else 4 * count * CHUNK * width)
        ),
        cost_estimate=pl.CostEstimate(
            flops=4 * rows * count * CHUNK * width,
            bytes_accessed=4 * count * CHUNK * width,
            transcendentals=0,
        ),
    )(*pieces, gain, here(gate_weight), here(up_weight), *sums)


def hidden_kernel(entries, early_counts, *refs):
    refs = list(refs)
    take = lambda number: [refs.pop(0) for _ in range(number)]
    odd_ref, gain_ref = take(2)
    early = [take(number) for number in early_counts]
    sources = take(2)
    (down_hbm,) = take(1)
    starts = take(2)
    squares_in, hidden_ref, out_ref = take(3)
    totals = take(2)
    held, sems = take(2), take(2)
    down_held, down_sems = refs
    me = lax.axis_index("shard")
    count = len(entries)
    counts = [buffer.shape[0] for buffer in held]
    copies = [
        lambda place, number=number: pltpu.make_async_copy(
            rows_at(sources[number], device_at(me, entries[-1] + 1 - counts[number] + place)),
            held[number].at[place],
            sems[number].at[place],
        )
        for number in range(2)
    ]
    down_copy = lambda place: pltpu.make_async_copy(
        columns_at(down_hbm, device_at(me, entries[0] + place)),
        down_held.at[place],
        down_sems.at[place],
    )
    for number in range(2):
        started(counts[number], copies[number])
    started(count, down_copy)
    lefts, squares = normed_pieces(entries, [odd_ref], gain_ref, squares_in[...])
    places = [0, 0]
    for number in range(2):
        total = starts[number][...]
        for part in early[number]:
            place = places[number]
            places[number] += part.shape[0]
            total += terms_of(lefts[place : places[number]], part)
        totals[number][...] = total
    for number in range(2):
        for place in range(counts[number]):
            copies[number](place).wait()
        totals[number][...] += terms_of(lefts[places[number] :], held[number])
    scale = lax.rsqrt(jnp.sum(squares, axis=1, keepdims=True) / D + norm_eps)
    gates, ups = totals[0][...] * scale, totals[1][...] * scale
    hidden_ref[...] = (jax.nn.silu(gates) * ups).astype(jnp.bfloat16)
    for place in range(count):
        down_copy(place).wait()
        out_ref[place] = jnp.dot(
            hidden_ref[...], down_held[place], preferred_element_type=jnp.float32
        ).astype(jnp.bfloat16)


def hidden_units(entries, odd, gain, early, weights, down_weight, sums):
    rows = odd.shape[1]
    width = weights[0].shape[1]
    count = len(entries)
    later = [count - sum(part.shape[0] for part in parts) for parts in early]
    total = pltpu.VMEM((rows, width), jnp.float32)
    held = [pltpu.VMEM((number, CHUNK, width), jnp.bfloat16) for number in later]
    early_parts = [part for parts in early for part in parts]
    return pl.pallas_call(
        functools.partial(hidden_kernel, entries, [len(parts) for parts in early]),
        in_specs=[VMEM_SPEC] * (2 + len(early_parts)) + [HBM_SPEC] * 3 + [VMEM_SPEC] * 3,
        out_specs=[VMEM_SPEC] * 2,
        out_shape=[
            jax.ShapeDtypeStruct((rows, width), jnp.bfloat16),
            jax.ShapeDtypeStruct((count, rows, CHUNK), jnp.bfloat16),
        ],
        scratch_shapes=[total, total]
        + held
        + [pltpu.SemaphoreType.DMA((number,)) for number in later]
        + [pltpu.VMEM((count, width, CHUNK), jnp.bfloat16), pltpu.SemaphoreType.DMA((count,))],
        compiler_params=pltpu.CompilerParams(
            vmem_limit_bytes=2 * (sum(later) + count) * CHUNK * width + 2 * MIB
        ),
        cost_estimate=pl.CostEstimate(
            flops=2 * rows * 3 * count * CHUNK * width,
            bytes_accessed=2 * 3 * count * CHUNK * width,
            transcendentals=rows * width,
        ),
    )(
        odd,
        gain,
        *[in_vmem(part) for part in early_parts],
        *[in_hbm(weight) for weight in weights],
        in_hbm(down_weight),
        *sums,
    )


def down_kernel(choice, hidden_ref, *refs):
    out_ref = refs[-1]
    for place, (number, index) in enumerate(choice):
        out_ref[place] = jnp.dot(
            hidden_ref[...], refs[number][index], preferred_element_type=jnp.float32
        )


def down_terms(hidden, parts, choice):
    rows, depth = hidden.shape
    return pl.pallas_call(
        functools.partial(down_kernel, choice),
        in_specs=[VMEM_SPEC] * (1 + len(parts)),
        out_specs=VMEM_SPEC,
        out_shape=jax.ShapeDtypeStruct((len(choice), rows, CHUNK), jnp.float32),
        compiler_params=pltpu.CompilerParams(vmem_limit_bytes=4 * MIB),
        cost_estimate=pl.CostEstimate(
            flops=2 * rows * depth * CHUNK * len(choice),
            bytes_accessed=2 * depth * CHUNK * len(choice),
            transcendentals=0,
        ),
    )(hidden, *[in_vmem(part) for part in parts])


def far_kernel(mine_ref, theirs_ref, out_ref):
    for place in range(4):
        out_ref[place] = (mine_ref[place] + theirs_ref[4 + place].astype(jnp.float32)).astype(
            jnp.bfloat16
        )


def far_pairs(mine, theirs):
    return pl.pallas_call(
        far_kernel,
        in_specs=[VMEM_SPEC] * 2,
        out_specs=VMEM_SPEC,
        out_shape=jax.ShapeDtypeStruct((4,) + theirs.shape[1:], jnp.bfloat16),
        compiler_params=pltpu.CompilerParams(vmem_limit_bytes=4 * MIB),
    )(mine, theirs)


def near_kernel(mine_ref, theirs_ref, arrived_ref, own_ref, *out_refs):
    for place, out_ref in enumerate((own_ref,) + out_refs):
        total = mine_ref[place] + theirs_ref[place].astype(jnp.float32)
        total = total + arrived_ref[place].astype(jnp.float32)
        out_ref[...] = total.astype(out_ref.dtype)


def near_sums(mine, theirs, arrived):
    block = theirs.shape[1:]
    return pl.pallas_call(
        near_kernel,
        in_specs=[VMEM_SPEC] * 3,
        out_specs=[VMEM_SPEC] * 4,
        out_shape=[jax.ShapeDtypeStruct(block, jnp.float32)]
        + [jax.ShapeDtypeStruct(block, jnp.bfloat16)] * 3,
        compiler_params=pltpu.CompilerParams(vmem_limit_bytes=4 * MIB),
    )(mine, theirs, arrived)


def finish_kernel(stream_ref, *refs):
    total = stream_ref[...].astype(jnp.float32)
    for share in refs[:-1]:
        total = total + share[...].astype(jnp.float32)
    refs[-1][...] = total.astype(jnp.bfloat16)


def finished(stream, shares):
    return pl.pallas_call(
        finish_kernel,
        in_specs=[VMEM_SPEC] * (1 + len(shares)),
        out_specs=VMEM_SPEC,
        out_shape=jax.ShapeDtypeStruct(stream.shape, jnp.bfloat16),
        compiler_params=pltpu.CompilerParams(vmem_limit_bytes=4 * MIB),
    )(stream, *shares)


def block_body(
    queries,
    new_kv,
    kv_pages,
    page_table,
    lengths,
    residual,
    out_weight,
    norm_gain,
    gate_weight,
    up_weight,
    down_weight,
):
    me = lax.axis_index("shard").astype(jnp.int32)[None]
    table = jnp.concatenate([page_table.reshape(-1), lengths, me])
    own, query_rows = packed(queries, norm_gain)
    middle, late = (4, 5, 6, 7), tuple(range(8, 16))

    pages, left, of_second, new_terms = readied(table, query_rows, kv_pages, new_kv)
    near = stacked(near_pieces(own), (new_terms,))
    second = sent(near, 2)
    (early_gate,) = fetched(near, (gate_weight, rows_at, late[:5]))
    odd = sent(stacked([near, second], (early_gate,)), 1)
    gains = near, second, odd
    along = page_terms(left, of_second, (0, 1, 2, 3), (near, second), pages)
    theirs = page_terms(left, of_second, late, (odd,), pages, (along,))
    across = page_terms(left, of_second, middle, (near, second), pages)

    theirs = sent(theirs, 1)
    across = across_core(of_second, across, theirs)
    arrived = sent(across, 2)
    gate_held, early_first = fetched(
        across, (gate_weight, rows_at, middle), (up_weight, rows_at, late[:2])
    )
    own, *others = across_y(of_second, along, theirs, arrived, gate_held)
    up_held, early_second = fetched(
        own, (up_weight, rows_at, middle), (up_weight, rows_at, late[2:4])
    )
    shares = [sent(other, distance) for other, distance in zip(others[::-1], (12, 8, 4))]
    attended = combined(shares + [own], new_terms, up_held)

    down_first, early_third = fetched(
        attended, (down_weight, columns_at, middle[:2]), (up_weight, rows_at, late[4:6])
    )
    near = stacked(near_pieces(attended), (down_first,))
    second = sent(near, 2)
    (down_rest,) = fetched(near, (down_weight, columns_at, middle[2:] + (0, 1, 2, 3)))
    odd = sent(stacked([near, second], (down_rest,)), 1)
    stream = projected(near, second, odd, residual, out_weight)

    weights = gate_weight, up_weight
    near = near_pieces(stream)
    sums = feed((0,), near[:1], gains[0], (), *weights)
    first = stacked(near, sums[:1])
    second = sent(first, 2)
    sums = feed((1, 2, 3), near[1:], gains[0], sums, *weights)
    odd = sent(stacked([first, second], sums[:1]), 1)
    sums = feed(middle, [second], gains[1], sums, gate_held, up_held, held=True)
    early = (early_gate,), (early_first, early_second, early_third)
    hidden, theirs = hidden_units(late, odd, gains[2], early, weights, down_weight, sums)

    theirs = sent(theirs, 1)
    far = down_terms(hidden, (down_first, down_rest), ((0, 0), (0, 1), (1, 0), (1, 1)))
    arrived = sent(far_pairs(far, theirs), 2)
    mine = down_terms(hidden, (down_rest,), ((0, 2), (0, 3), (0, 4), (0, 5)))
    own, *others = near_sums(mine, theirs, arrived)
    shares = [sent(other, distance) for other, distance in zip(others[::-1], (12, 8, 4))]
    return finished(stream, shares + [own])


def solution(mesh):
    placed = (
        P(("groups", "shard"), None),
        P(("groups", "shard"), None, None),
        P(("groups", "shard"), None, None, None),
        P("groups", None),
        P("groups"),
        P("groups", "shard"),
        P(None, "shard"),
        P("shard"),
        P(None, "shard"),
        P(None, "shard"),
        P("shard", None),
    )
    chosen = block_body if mesh.shape["shard"] == 16 else body
    return jax.shard_map(
        chosen, mesh=mesh, in_specs=placed, out_specs=P("groups", "shard"), check_vma=False
    )
```

```python
import functools
import math

import jax
import jax.numpy as jnp
from jax import lax
from jax.experimental import pallas as pl
from jax.experimental.pallas import tpu as pltpu
from jax.sharding import PartitionSpec as P

D = 8192
HEADS = 64
KV_HEADS = 4
HEAD_DIM = 128


norm_eps = 1e-05


def swapped(array, axis, distance):
    return lax.ppermute(array, axis, [(i, i ^ 1 << distance) for i in range(lax.axis_size(axis))])


def new_token_terms(queries, new_kv, score_scale):
    seq_dev = queries.shape[0]
    group_size = HEADS // KV_HEADS
    query_heads = queries.reshape(seq_dev, KV_HEADS, group_size, HEAD_DIM)
    new_keys = new_kv[:, 0].reshape(seq_dev, KV_HEADS, HEAD_DIM)
    new_values = new_kv[:, 1].reshape(seq_dev, KV_HEADS, HEAD_DIM)
    scores = (
        jnp.einsum("bgqd,bgd->bgq", query_heads, new_keys, preferred_element_type=jnp.float32)
        * score_scale
    )
    weights = jnp.exp(scores)
    numerator = jnp.einsum(
        "bgq,bgd->bgqd",
        weights.astype(jnp.bfloat16),
        new_values,
        preferred_element_type=jnp.float32,
    )
    return (numerator.reshape(seq_dev, D), weights.reshape(seq_dev, HEADS))


def butterfly(items, position, mover):
    count = items[0].shape[0]
    for level in range(count.bit_length() - 1):
        upper_half = position // (1 << level) % 2 == 1
        halves = [
            entry.reshape((count >> level + 1, 2, 1 << level) + entry.shape[1:]) for entry in items
        ]
        outgoing = tuple(
            (jnp.where(upper_half, halves_one[:, 0], halves_one[:, 1]) for halves_one in halves)
        )
        incoming = mover(outgoing, level)
        rebuilt = []
        for entry, halves_one, arrived_one in zip(items, halves, incoming):
            lower_part = jnp.where(upper_half, arrived_one, halves_one[:, 0])
            upper_part = jnp.where(upper_half, halves_one[:, 1], arrived_one)
            rebuilt.append(jnp.stack([lower_part, upper_part], axis=1).reshape(entry.shape))
        items = tuple(rebuilt)
    return items


def body(
    queries,
    new_kv,
    kv_pages,
    page_table,
    lengths,
    residual,
    out_weight,
    norm_gain,
    gate_weight,
    up_weight,
    down_weight,
):
    seq_dev = queries.shape[0]
    page_count = kv_pages.shape[0]
    page_len = kv_pages.shape[2]
    all_seqs = page_table.shape[0]
    max_pages = page_table.shape[1]
    group_size = HEADS // KV_HEADS
    score_scale = 1.0 / math.sqrt(HEAD_DIM)
    device_pos = lax.axis_index("shard")
    own_first = device_pos * seq_dev
    own_lengths = lax.dynamic_slice_in_dim(lengths, own_first, seq_dev, 0)
    own_table = lax.dynamic_slice_in_dim(page_table, own_first, seq_dev, 0)
    holder_local = own_table // page_count % page_count
    page_ids = device_pos * page_count + jnp.arange(page_count, dtype=jnp.int32)
    matches = page_table[None, :, :] == page_ids[:, None, None]
    seq_of = jnp.sum(
        jnp.where(matches, jnp.arange(all_seqs, dtype=jnp.int32)[None, :, None], 0), axis=(1, 2)
    )
    owner_local = seq_of // seq_dev % page_count
    own_numerator, own_denominator = new_token_terms(queries, new_kv, score_scale)
    outgoing = jnp.zeros_like(kv_pages).at[owner_local].set(kv_pages)
    arrived = butterfly(
        (outgoing,), device_pos, lambda sending, level: (swapped(sending[0], "shard", level),)
    )[0]
    fetched = arrived[holder_local]
    context = max_pages * page_len
    key_rows = fetched[:, :, 0].reshape(seq_dev, context, KV_HEADS, HEAD_DIM)
    value_rows = fetched[:, :, 1].reshape(seq_dev, context, KV_HEADS, HEAD_DIM)
    query_heads = queries.reshape(seq_dev, KV_HEADS, group_size, HEAD_DIM)
    scores = (
        jnp.einsum("bgqd,btgd->bgqt", query_heads, key_rows, preferred_element_type=jnp.float32)
        * score_scale
    )
    position = jnp.arange(context, dtype=jnp.int32)
    alive = position[None, :] < own_lengths[:, None]
    weights = jnp.where(alive[:, None, None, :], jnp.exp(scores), 0.0)
    denominator = jnp.sum(weights, axis=-1).reshape(seq_dev, HEADS)
    numerator = jnp.einsum(
        "bgqt,btgd->bgqd",
        weights.astype(jnp.bfloat16),
        value_rows,
        preferred_element_type=jnp.float32,
    )
    numer_rows = numerator.reshape(seq_dev, D) + own_numerator
    denom_rows = denominator + own_denominator
    attended = (
        (numer_rows.reshape(seq_dev, HEADS, HEAD_DIM) / denom_rows[:, :, None])
        .reshape(seq_dev, D)
        .astype(jnp.bfloat16)
    )
    projected = jnp.dot(
        lax.all_gather(attended, "shard", axis=0, tiled=True),
        out_weight,
        preferred_element_type=jnp.float32,
    )
    stream = (residual.astype(jnp.float32) + projected).astype(jnp.bfloat16)
    wide = stream.astype(jnp.float32)
    square_sums = lax.psum(jnp.sum(wide * wide, axis=1), "shard")
    normed = (wide * lax.rsqrt(square_sums / D + norm_eps)[:, None] * norm_gain[None, :]).astype(
        jnp.bfloat16
    )
    block_cols = lax.all_gather(normed, "shard", axis=1, tiled=True)
    gate_acts = jnp.dot(block_cols, gate_weight, preferred_element_type=jnp.float32)
    up_acts = jnp.dot(block_cols, up_weight, preferred_element_type=jnp.float32)
    hidden = (jax.nn.silu(gate_acts) * up_acts).astype(jnp.bfloat16)
    partial_terms = jnp.dot(hidden, down_weight, preferred_element_type=jnp.float32)
    down_terms = lax.psum_scatter(partial_terms, "shard", scatter_dimension=1, tiled=True)
    return (wide + down_terms).astype(jnp.bfloat16)


GROUP = HEADS // KV_HEADS
TAIL = 16
MIB = 2**20
VMEM_SPEC = pl.BlockSpec(memory_space=pltpu.VMEM)
SMEM_SPEC = pl.BlockSpec(memory_space=pltpu.SMEM)
HBM_SPEC = pl.BlockSpec(memory_space=pltpu.HBM)
CHUNK = 512


def sent(array, distance):
    size = lax.axis_size("shard")
    return lax.ppermute(array, "shard", [(i, i ^ distance) for i in range(size)])


def stack_kernel(count, *refs):
    out_ref, place = refs[-1], 0
    for part in refs[:count]:
        size = part.shape[0] if len(part.shape) == 3 else 1
        out_ref[place : place + size] = part[...].reshape((size,) + part.shape[-2:])
        place += size


def stacked(parts, after):
    size = sum(part.shape[0] if part.ndim == 3 else 1 for part in parts)
    return pl.pallas_call(
        functools.partial(stack_kernel, len(parts)),
        in_specs=[VMEM_SPEC] * len(parts) + [pl.BlockSpec(memory_space=pl.ANY)] * len(after),
        out_specs=VMEM_SPEC,
        out_shape=jax.ShapeDtypeStruct((size,) + parts[0].shape[-2:], parts[0].dtype),
        compiler_params=pltpu.CompilerParams(vmem_limit_bytes=4 * MIB),
        cost_estimate=pl.CostEstimate(flops=0, bytes_accessed=16 * MIB, transcendentals=0),
    )(*parts, *after)


def near_pieces(piece):
    return [piece] + [sent(piece, distance) for distance in (4, 8, 12)]


def device_at(me, entry):
    return me ^ (entry % 4 * 4 + entry // 4 % 2 * 2 + entry // 8)


def started(count, *copies):
    def start(place, carry):
        for copy_at in copies:
            copy_at(place).start()
        return carry

    lax.fori_loop(0, count, start, 0)


def in_vmem(array):
    return pltpu.with_memory_space_constraint(array, pltpu.VMEM)


def in_hbm(array):
    return pltpu.with_memory_space_constraint(array, pltpu.HBM)


def two_terms(wide):
    high = wide.astype(jnp.bfloat16).astype(jnp.float32)
    return high, wide - high


def pack_kernel(query_hbm, gain_hbm, out_ref, rows_ref, query, gain, wide, sems):
    copies = [
        pltpu.make_async_copy(query_hbm, query, sems.at[0]),
        pltpu.make_async_copy(gain_hbm, gain, sems.at[1]),
    ]
    for copy in copies:
        copy.start()
    for copy in copies:
        copy.wait()
    rows = 2 * HEADS
    for head in range(HEADS):
        cols = slice(head * HEAD_DIM, (head + 1) * HEAD_DIM)
        wide[pl.ds(head, 2, HEADS), :] = query[:, cols].astype(jnp.float32)
    out_ref[:rows, :] = wide[...].astype(jnp.bfloat16)
    rows_ref[...] = wide[...].astype(jnp.bfloat16)
    high, rest = two_terms(gain[...])
    middle, low = two_terms(rest)
    filler = jnp.zeros((16 - 3 * high.shape[0], HEAD_DIM), jnp.float32)
    out_ref[rows:, :] = jnp.concatenate([high, middle, low, filler]).astype(jnp.bfloat16)


def packed(queries, norm_gain):
    rows = 2 * HEADS
    gain = norm_gain.reshape(-1, HEAD_DIM)
    return pl.pallas_call(
        pack_kernel,
        in_specs=[HBM_SPEC] * 2,
        out_specs=[VMEM_SPEC] * 2,
        out_shape=[
            jax.ShapeDtypeStruct((rows + 16, HEAD_DIM), jnp.bfloat16),
            jax.ShapeDtypeStruct((rows, HEAD_DIM), jnp.bfloat16),
        ],
        scratch_shapes=[
            pltpu.VMEM(queries.shape, jnp.bfloat16),
            pltpu.VMEM(gain.shape, jnp.float32),
            pltpu.VMEM((rows, HEAD_DIM), jnp.float32),
            pltpu.SemaphoreType.DMA((2,)),
        ],
        compiler_params=pltpu.CompilerParams(vmem_limit_bytes=4 * MIB),
    )(in_hbm(queries), in_hbm(gain))


def context_terms(query, keys, values, alive):
    numerators, denominators = [], []
    for head in range(KV_HEADS):
        cols = slice(head * HEAD_DIM, (head + 1) * HEAD_DIM)
        scores = lax.dot_general(
            query[head * GROUP : (head + 1) * GROUP],
            keys[:, cols],
            (((1,), (1,)), ((), ())),
            preferred_element_type=jnp.float32,
        ) * (1.0 / math.sqrt(HEAD_DIM))
        weights = jnp.where(alive, jnp.exp(scores), 0.0)
        denominators.append(jnp.sum(weights, axis=1, keepdims=True))
        numerators.append(
            jnp.dot(
                weights.astype(jnp.bfloat16), values[:, cols], preferred_element_type=jnp.float32
            )
        )
    return jnp.concatenate(numerators), jnp.concatenate(denominators)


def ready_kernel(table_ref, query_ref, pages_hbm, new_hbm, after_ref, pages, left_ref, second_ref, new_ref, lower_ref, new, sems):
    _, _, page_len, features = pages.shape
    count = pages_hbm.shape[0]
    sequences = 2 * 16
    per_row = (table_ref.shape[0] - 1) // sequences - 1
    me = table_ref[(per_row + 1) * sequences]
    new_copy = pltpu.make_async_copy(new_hbm, new, sems.at[16])
    new_copy.start()
    page_copy = lambda slot, entry: pltpu.make_async_copy(
        pages_hbm.at[slot], pages.at[entry], sems.at[entry]
    )
    line = lambda value: jnp.full((1, HEAD_DIM), value, dtype=jnp.int32)

    def ready(entry, carry):
        owner = device_at(me, entry)
        place, other = 0, 0
        for index in range(2 * per_row):
            holder = table_ref[2 * owner * per_row + index] // count
            place = jnp.where(holder == me, index, place)
            other = jnp.where(holder == me ^ 1, index, other)
        row = place // per_row
        slot = table_ref[2 * owner * per_row + place] % count
        page_copy(slot, entry).start()
        left = table_ref[sequences * per_row + 2 * owner + row] - page_len * (place % per_row)
        here = pl.ds(entry, 1)
        left_ref[here, :] = line(left)
        second_ref[here, :] = line(row)
        second_ref[pl.ds(16 + entry, 1), :] = line(other // per_row)
        return carry

    lax.fori_loop(0, 16, ready, 0)
    first_token = lax.broadcasted_iota(jnp.int32, (GROUP, 8), 1) < 1
    new_copy.wait()
    for row in range(2):
        lines = slice(row * HEADS, (row + 1) * HEADS)
        numerator, total = context_terms(
            query_ref[lines, :],
            jnp.broadcast_to(new[row, 0:1, :], (8, features)),
            jnp.broadcast_to(new[row, 1:2, :], (8, features)),
            first_token,
        )
        new_ref[lines, :] = numerator
        lower = jnp.swapaxes(jnp.broadcast_to(total, (HEADS, HEAD_DIM)), 0, 1)
        lower_ref[8 * row : 8 * (row + 1), :] = lower[:8]
    for entry in range(16):
        page_copy(0, entry).wait()


def readied(table, query_rows, kv_pages, new_kv, after):
    return pl.pallas_call(
        ready_kernel,
        in_specs=[SMEM_SPEC, VMEM_SPEC] + [HBM_SPEC] * 2 + [pl.BlockSpec(memory_space=pl.ANY)],
        out_specs=[VMEM_SPEC] * 5,
        out_shape=[
            pltpu.VMEM(kv_pages.shape, kv_pages.dtype),
            jax.ShapeDtypeStruct((16, HEAD_DIM), jnp.int32),
            jax.ShapeDtypeStruct((32, HEAD_DIM), jnp.int32),
            jax.ShapeDtypeStruct((2 * HEADS, HEAD_DIM), jnp.float32),
            jax.ShapeDtypeStruct((16, HEADS), jnp.float32),
        ],
        scratch_shapes=[pltpu.VMEM(new_kv.shape, jnp.bfloat16), pltpu.SemaphoreType.DMA((17,))],
        compiler_params=pltpu.CompilerParams(vmem_limit_bytes=4 * MIB),
        cost_estimate=pl.CostEstimate(flops=2**22, bytes_accessed=2**21, transcendentals=2**11),
    )(table, query_rows, in_hbm(kv_pages), in_hbm(new_kv), after)


def pages_kernel(entries, left_ref, second_ref, *refs):
    refs = list(refs)
    near, across = (refs.pop(0), refs.pop(0)) if entries[0] < 8 else (None, None)
    odd = None if entries[0] < 8 else refs.pop(0)
    pages, out_ref, scores, weights = refs[0], *refs[-3:]
    page_len, features = pages.shape[2:]
    line = lax.broadcasted_iota(jnp.int32, (HEADS, features), 0) // GROUP
    block = lax.broadcasted_iota(jnp.int32, (HEADS, features), 1) // HEAD_DIM
    own_block = (line == block).astype(jnp.float32).astype(jnp.bfloat16)
    for here, entry in enumerate(entries):
        source, place = piece_at(near, across, odd, entry)
        second = second_ref[entry : entry + 1, :].astype(jnp.float32)
        query = source[place, :HEADS, :].astype(jnp.float32) * (1.0 - second)
        query += source[place, HEADS : 2 * HEADS, :].astype(jnp.float32) * second
        query = query.astype(jnp.bfloat16)
        spread = jnp.concatenate([query] * KV_HEADS, axis=1) * own_block
        scores[here] = lax.dot_general(
            spread,
            pages[entry, 0],
            (((1,), (1,)), ((), ())),
            preferred_element_type=jnp.float32,
        )
    position = lax.broadcasted_iota(jnp.int32, (HEADS, page_len), 1)
    lane = lax.broadcasted_iota(jnp.int32, (HEADS, HEAD_DIM), 1)
    denominators = jnp.zeros((HEADS, HEAD_DIM), jnp.float32)
    for here, entry in enumerate(entries):
        raised = jnp.exp(scores[here] * (1.0 / math.sqrt(HEAD_DIM)))
        weight = jnp.where(position < left_ref[entry : entry + 1, :page_len], raised, 0.0)
        weights[here] = weight.astype(jnp.bfloat16)
        total = jnp.sum(weight, axis=1, keepdims=True)
        denominators = jnp.where(lane == here, total, denominators)
    for here, entry in enumerate(entries):
        numerator = jnp.dot(
            weights[here], pages[entry, 1], preferred_element_type=jnp.float32
        )
        for head in range(KV_HEADS):
            lines = slice(head * GROUP, (head + 1) * GROUP)
            out_ref[here * HEADS + head * GROUP : here * HEADS + (head + 1) * GROUP, :] = numerator[
                lines, head * HEAD_DIM : (head + 1) * HEAD_DIM
            ].astype(jnp.bfloat16)
    sealed(out_ref, jnp.swapaxes(denominators, 0, 1)[: len(entries)])


def sealed(out_ref, denominators):
    count = denominators.shape[0]
    filler = jnp.zeros((TAIL - count, HEAD_DIM), jnp.float32)
    lasts = jnp.concatenate(two_terms(denominators), axis=1)
    out_ref[count * HEADS :, :] = jnp.concatenate([lasts, filler]).astype(jnp.bfloat16)


def opened(message, place):
    start = message.shape[0] - TAIL
    last = message[start:, :].astype(jnp.float32)[place : place + 1]
    numerator = message[place * HEADS : (place + 1) * HEADS, :].astype(jnp.float32)
    return numerator, last[:, :HEADS] + last[:, HEADS:]


def piece_at(near, second, odd, entry):
    if entry < 4:
        return near, entry
    return (second, entry - 4) if entry < 8 else (odd, entry - 8)


def page_terms(left, second, entries, pieces, pages, beside=()):
    return pl.pallas_call(
        functools.partial(pages_kernel, entries),
        in_specs=[VMEM_SPEC] * (len(pieces) + 3)
        + [pl.BlockSpec(memory_space=pl.ANY)] * len(beside),
        out_specs=VMEM_SPEC,
        out_shape=jax.ShapeDtypeStruct((len(entries) * HEADS + TAIL, HEAD_DIM), jnp.bfloat16),
        scratch_shapes=[
            pltpu.VMEM((len(entries), HEADS, pages.shape[2]), jnp.float32),
            pltpu.VMEM((len(entries), HEADS, pages.shape[2]), jnp.bfloat16),
        ],
        compiler_params=pltpu.CompilerParams(vmem_limit_bytes=6 * MIB),
        cost_estimate=pl.CostEstimate(flops=2**26, bytes_accessed=2**20, transcendentals=2**14),
    )(left, second, *pieces, in_vmem(pages), *beside)


def two_rows(second_ref, entry, mine, theirs):
    sums = [[0.0, 0.0], [0.0, 0.0]]
    for line, (numerator, denominator) in zip((entry, 16 + entry), (mine, theirs)):
        second = second_ref[line : line + 1, :].astype(jnp.float32)
        for row, share in enumerate((1.0 - second, second)):
            sums[row][0] = sums[row][0] + numerator * share
            sums[row][1] = sums[row][1] + denominator * share[:, :HEADS]
    return sums


def core_kernel(second_ref, mine_ref, theirs_ref, out_ref):
    lowers = []
    for place in range(4):
        mine, theirs = opened(mine_ref, place), opened(theirs_ref, 4 + place)
        for row, (part, lower) in enumerate(two_rows(second_ref, 4 + place, mine, theirs)):
            start = (2 * place + row) * HEADS
            out_ref[start : start + HEADS, :] = part.astype(jnp.bfloat16)
            lowers.append(lower)
    sealed(out_ref, jnp.concatenate(lowers))


def across_core(second, mine, theirs):
    return pl.pallas_call(
        core_kernel,
        in_specs=[VMEM_SPEC] * 3,
        out_specs=VMEM_SPEC,
        out_shape=jax.ShapeDtypeStruct((8 * HEADS + TAIL, HEAD_DIM), jnp.bfloat16),
        compiler_params=pltpu.CompilerParams(vmem_limit_bytes=4 * MIB),
    )(second, mine, theirs)


def chip_kernel(second_ref, mine_ref, theirs_ref, arrived_ref, new_ref, lower_ref, *refs):
    out_ref = refs[-1]
    lowers = []
    for place in range(4):
        mine, theirs = opened(mine_ref, place), opened(theirs_ref, place)
        for row, (part, lower) in enumerate(two_rows(second_ref, place, mine, theirs)):
            arrived, arrived_lower = opened(arrived_ref, 2 * place + row)
            part, lower = part + arrived, lower + arrived_lower
            if place == 0:
                part = part + new_ref[row * HEADS : (row + 1) * HEADS, :]
                lower = lower + lower_ref[8 * row : 8 * row + 1, :]
            start = (2 * place + row) * HEADS
            out_ref[start : start + HEADS, :] = part.astype(jnp.bfloat16)
            lowers.append(lower)
    sealed(out_ref, jnp.concatenate(lowers))


def across_y(second, mine, theirs, arrived, new_terms, beside):
    return pl.pallas_call(
        chip_kernel,
        in_specs=[VMEM_SPEC] * 6 + [pl.BlockSpec(memory_space=pl.ANY)] * len(beside),
        out_specs=VMEM_SPEC,
        out_shape=jax.ShapeDtypeStruct((8 * HEADS + TAIL, HEAD_DIM), jnp.bfloat16),
        compiler_params=pltpu.CompilerParams(vmem_limit_bytes=4 * MIB),
    )(second, mine, theirs, arrived, *new_terms, *beside)


def combine_kernel(*refs):
    shares, out_ref = refs[:4], refs[-1]
    parts, lowers = [], []
    for place in range(4):
        for row in range(2):
            terms = [opened(share, 2 * (place ^ j) + row) for j, share in enumerate(shares)]
            parts.append(sum(part for part, _ in terms))
            lowers.append(sum(lower for _, lower in terms))
    lower = jnp.concatenate([jnp.concatenate(lowers), jnp.zeros((8, HEADS), jnp.float32)], axis=1)
    columns = jnp.swapaxes(lower, 0, 1)
    for index, part in enumerate(parts):
        lines = slice(index % 2 * HEADS, (index % 2 + 1) * HEADS)
        column = columns[:HEADS, index : index + 1]
        out_ref[index // 2, lines, :] = (part / column).astype(jnp.bfloat16)


def combined(shares, beside):
    return pl.pallas_call(
        combine_kernel,
        in_specs=[VMEM_SPEC] * 4 + [pl.BlockSpec(memory_space=pl.ANY)] * len(beside),
        out_specs=VMEM_SPEC,
        out_shape=jax.ShapeDtypeStruct((4, 2 * HEADS, HEAD_DIM), jnp.bfloat16),
        compiler_params=pltpu.CompilerParams(vmem_limit_bytes=4 * MIB),
        cost_estimate=pl.CostEstimate(
            flops=2**22, bytes_accessed=48 * MIB, transcendentals=2**11
        ),
    )(*shares, *beside)


def fetch_kernel(parts, after_ref, *refs):
    weights, outs, sems = refs[: len(parts)], refs[len(parts) : -1], refs[-1]
    me = lax.axis_index("shard")
    copies = []
    for (place_of, entries), weight_hbm, out_ref in zip(parts, weights, outs):
        for place, entry in enumerate(entries):
            copies.append(
                pltpu.make_async_copy(
                    place_of(weight_hbm, device_at(me, entry)),
                    out_ref.at[place],
                    sems.at[len(copies)],
                )
            )
    for copy in copies:
        copy.start()
    for copy in copies:
        copy.wait()


def fetched(after, *parts):
    count = sum(len(entries) for _, _, entries in parts)
    weights = [weight for weight, _, _ in parts]
    shapes = [
        pltpu.VMEM((len(entries),) + place_of(weight, None), weight.dtype)
        for weight, place_of, entries in parts
    ]
    size = sum(math.prod(shape.shape) for shape in shapes)
    return pl.pallas_call(
        functools.partial(fetch_kernel, [part[1:] for part in parts]),
        in_specs=[pl.BlockSpec(memory_space=pl.ANY)] + [HBM_SPEC] * len(parts),
        out_specs=[VMEM_SPEC] * len(parts),
        out_shape=shapes,
        scratch_shapes=[pltpu.SemaphoreType.DMA((count,))],
        compiler_params=pltpu.CompilerParams(vmem_limit_bytes=MIB),
        cost_estimate=pl.CostEstimate(flops=0, bytes_accessed=2 * size, transcendentals=0),
    )(after, *[in_hbm(weight) for weight in weights])


def rows_at(weight, device):
    if device is None:
        return (CHUNK, weight.shape[1])
    return weight.at[pl.ds(pl.multiple_of(device * CHUNK, CHUNK), CHUNK)]


def columns_at(weight, device):
    if device is None:
        return (weight.shape[0], CHUNK)
    return weight.at[:, pl.ds(pl.multiple_of(device * CHUNK, CHUNK), CHUNK)]


def out_kernel(
    near_ref,
    second_ref,
    odd_ref,
    weight_ref,
    residual,
    out_ref,
    wide,
    left,
):
    me = lax.axis_index("shard")
    for entry in range(16):
        source, place = piece_at(near_ref, second_ref, odd_ref, entry)
        start = pl.multiple_of(device_at(me, entry) * 2 * HEADS, 2 * HEADS)
        wide[pl.ds(start, 2 * HEADS), :] = source[place].astype(jnp.float32)
    for head in range(HEADS):
        rows = [wide[pl.ds(row * HEADS + head, 16, 2 * HEADS), :] for row in range(2)]
        left[:, head * HEAD_DIM : (head + 1) * HEAD_DIM] = jnp.concatenate(rows).astype(
            jnp.bfloat16
        )
    total = jnp.dot(left[...], weight_ref[...], preferred_element_type=jnp.float32)
    line = lax.broadcasted_iota(jnp.int32, (32, 32), 0)
    entry = lax.broadcasted_iota(jnp.int32, (32, 32), 1)
    turn = ((line % 2) * 16 + line // 2 == entry).astype(jnp.float32)
    turned = lax.dot_general(
        turn,
        total,
        (((1,), (0,)), ((), ())),
        precision=lax.Precision.HIGHEST,
        preferred_element_type=jnp.float32,
    )
    out_ref[...] = (residual[...].astype(jnp.float32) + turned).astype(jnp.bfloat16)


def projected(near, second, odd, residual, held_weight):
    rows, width = residual.shape
    return pl.pallas_call(
        out_kernel,
        in_specs=[VMEM_SPEC] * 5,
        out_specs=VMEM_SPEC,
        out_shape=jax.ShapeDtypeStruct((rows, width), jnp.bfloat16),
        scratch_shapes=[
            pltpu.VMEM((32 * HEADS, HEAD_DIM), jnp.float32),
            pltpu.VMEM((rows, D), jnp.bfloat16),
        ],
        compiler_params=pltpu.CompilerParams(vmem_limit_bytes=4 * MIB),
        cost_estimate=pl.CostEstimate(
            flops=2 * rows * D * width, bytes_accessed=2 * D * width, transcendentals=0
        ),
    )(near, second, odd, held_weight, residual)


def normed_pieces(entries, pieces, gain_ref, squares):
    lefts = []
    for place, entry in enumerate(entries):
        stream = pieces[place][...] if len(pieces) == len(entries) else pieces[0][place]
        wide = stream.astype(jnp.float32)
        squares = squares + wide * wide
        terms = gain_ref[entry % 4 if entry < 8 else entry - 8, 2 * HEADS :, :]
        terms = terms.astype(jnp.float32)
        gain = terms[0:4] + terms[4:8] + terms[8:12]
        gain = jnp.concatenate([gain[part : part + 1] for part in range(4)], axis=1)
        lefts.append((wide * gain).astype(jnp.bfloat16))
    return lefts, squares


def terms_of(lefts, blocks):
    left = jnp.concatenate(lefts, axis=1)
    weight = blocks[...].reshape(left.shape[1], blocks.shape[-1])
    return jnp.dot(left, weight, preferred_element_type=jnp.float32)


def feed_kernel(entries, piece_count, held, *refs):
    refs = list(refs)
    take = lambda number: [refs.pop(0) for _ in range(number)]
    pieces = take(piece_count)
    gain_ref, gate_ref, up_ref = take(3)
    gates_in, ups_in, squares_in = [None] * 3 if entries[0] == 0 else take(3)
    gates, ups, squares_out = take(3)
    copies = []
    if not held:
        sources = gate_ref, up_ref
        *targets, sems = refs
        gate_ref, up_ref = targets
        me = lax.axis_index("shard")
        count = len(entries)
        copies = [
            lambda place, number=number: pltpu.make_async_copy(
                rows_at(sources[number], device_at(me, entries[0] + place)),
                targets[number].at[place],
                sems.at[number * count + place],
            )
            for number in range(2)
        ]
        started(count, *copies)
    squares = 0.0 if squares_in is None else squares_in[...]
    lefts, squares_out[...] = normed_pieces(entries, pieces, gain_ref, squares)
    both = ((gates, gates_in, gate_ref), (ups, ups_in, up_ref))
    if held:
        for total, start, blocks in both:
            total[...] = start[...] + terms_of(lefts, blocks)
        return
    for place in range(len(entries)):
        for number, (total, start, blocks) in enumerate(both):
            copies[number](place).wait()
            terms = jnp.dot(lefts[place], blocks[place], preferred_element_type=jnp.float32)
            if place > 0:
                total[...] += terms
            else:
                total[...] = terms if start is None else start[...] + terms


def feed(entries, pieces, gain, sums, gate_weight, up_weight, held=False):
    rows = pieces[0].shape[-2]
    width = gate_weight.shape[-1]
    count = len(entries)
    total = jax.ShapeDtypeStruct((rows, width), jnp.float32)
    here = in_vmem if held else in_hbm
    slots = pltpu.VMEM((count, CHUNK, width), jnp.bfloat16)
    return pl.pallas_call(
        functools.partial(feed_kernel, entries, len(pieces), held),
        in_specs=[VMEM_SPEC] * (len(pieces) + 1)
        + [VMEM_SPEC if held else HBM_SPEC] * 2
        + [VMEM_SPEC] * len(sums),
        out_specs=[VMEM_SPEC] * 3,
        out_shape=[total, total, jax.ShapeDtypeStruct((rows, CHUNK), jnp.float32)],
        scratch_shapes=[] if held else [slots, slots, pltpu.SemaphoreType.DMA((2 * count,))],
        compiler_params=pltpu.CompilerParams(
            vmem_limit_bytes=2 * MIB + (0 if held else 4 * count * CHUNK * width)
        ),
        cost_estimate=pl.CostEstimate(
            flops=4 * rows * count * CHUNK * width,
            bytes_accessed=4 * count * CHUNK * width,
            transcendentals=0,
        ),
    )(*pieces, gain, here(gate_weight), here(up_weight), *sums)


def hidden_kernel(entries, early_counts, *refs):
    refs = list(refs)
    take = lambda number: [refs.pop(0) for _ in range(number)]
    odd_ref, gain_ref = take(2)
    early = [take(number) for number in early_counts]
    sources = take(2)
    (down_hbm,) = take(1)
    starts = take(2)
    squares_in, hidden_ref, out_ref = take(3)
    totals = take(2)
    held, sems = take(2), take(2)
    down_held, down_sems = refs
    me = lax.axis_index("shard")
    count = len(entries)
    counts = [buffer.shape[0] for buffer in held]
    copies = [
        lambda place, number=number: pltpu.make_async_copy(
            rows_at(sources[number], device_at(me, entries[-1] + 1 - counts[number] + place)),
            held[number].at[place],
            sems[number].at[place],
        )
        for number in range(2)
    ]
    down_copy = lambda place: pltpu.make_async_copy(
        columns_at(down_hbm, device_at(me, entries[0] + place)),
        down_held.at[place],
        down_sems.at[place],
    )
    for number in range(2):
        started(counts[number], copies[number])
    started(count, down_copy)
    lefts, squares = normed_pieces(entries, [odd_ref], gain_ref, squares_in[...])
    places = [0, 0]
    for number in range(2):
        total = starts[number][...]
        for part in early[number]:
            place = places[number]
            places[number] += part.shape[0]
            total += terms_of(lefts[place : places[number]], part)
        totals[number][...] = total
    for number in range(2):
        for place in range(counts[number]):
            copies[number](place).wait()
        totals[number][...] += terms_of(lefts[places[number] :], held[number])
    scale = lax.rsqrt(jnp.sum(squares, axis=1, keepdims=True) / D + norm_eps)
    gates, ups = totals[0][...] * scale, totals[1][...] * scale
    hidden_ref[...] = (jax.nn.silu(gates) * ups).astype(jnp.bfloat16)
    for place in range(count):
        down_copy(place).wait()
        out_ref[place] = jnp.dot(
            hidden_ref[...], down_held[place], preferred_element_type=jnp.float32
        ).astype(jnp.bfloat16)


def hidden_units(entries, odd, gain, early, weights, down_weight, sums):
    rows = odd.shape[1]
    width = weights[0].shape[1]
    count = len(entries)
    later = [count - sum(part.shape[0] for part in parts) for parts in early]
    total = pltpu.VMEM((rows, width), jnp.float32)
    held = [pltpu.VMEM((number, CHUNK, width), jnp.bfloat16) for number in later]
    early_parts = [part for parts in early for part in parts]
    return pl.pallas_call(
        functools.partial(hidden_kernel, entries, [len(parts) for parts in early]),
        in_specs=[VMEM_SPEC] * (2 + len(early_parts)) + [HBM_SPEC] * 3 + [VMEM_SPEC] * 3,
        out_specs=[VMEM_SPEC] * 2,
        out_shape=[
            jax.ShapeDtypeStruct((rows, width), jnp.bfloat16),
            jax.ShapeDtypeStruct((count, rows, CHUNK), jnp.bfloat16),
        ],
        scratch_shapes=[total, total]
        + held
        + [pltpu.SemaphoreType.DMA((number,)) for number in later]
        + [pltpu.VMEM((count, width, CHUNK), jnp.bfloat16), pltpu.SemaphoreType.DMA((count,))],
        compiler_params=pltpu.CompilerParams(
            vmem_limit_bytes=2 * (sum(later) + count) * CHUNK * width + 2 * MIB
        ),
        cost_estimate=pl.CostEstimate(
            flops=2 * rows * 3 * count * CHUNK * width,
            bytes_accessed=2 * 3 * count * CHUNK * width,
            transcendentals=rows * width,
        ),
    )(
        odd,
        gain,
        *[in_vmem(part) for part in early_parts],
        *[in_hbm(weight) for weight in weights],
        in_hbm(down_weight),
        *sums,
    )


def down_kernel(hidden_ref, held_ref, out_ref):
    for place in range(held_ref.shape[0]):
        out_ref[place] = jnp.dot(
            hidden_ref[...], held_ref[place], preferred_element_type=jnp.float32
        )


def down_terms(hidden, held):
    rows, depth = hidden.shape
    count = held.shape[0]
    return pl.pallas_call(
        down_kernel,
        in_specs=[VMEM_SPEC] * 2,
        out_specs=VMEM_SPEC,
        out_shape=jax.ShapeDtypeStruct((count, rows, CHUNK), jnp.float32),
        compiler_params=pltpu.CompilerParams(vmem_limit_bytes=4 * MIB),
        cost_estimate=pl.CostEstimate(
            flops=2 * rows * depth * CHUNK * count,
            bytes_accessed=2 * depth * CHUNK * count,
            transcendentals=0,
        ),
    )(hidden, in_vmem(held))


def far_kernel(mine_ref, theirs_ref, out_ref):
    for place in range(4):
        out_ref[place] = (mine_ref[place] + theirs_ref[4 + place].astype(jnp.float32)).astype(
            jnp.bfloat16
        )


def far_pairs(mine, theirs):
    return pl.pallas_call(
        far_kernel,
        in_specs=[VMEM_SPEC] * 2,
        out_specs=VMEM_SPEC,
        out_shape=jax.ShapeDtypeStruct((4,) + theirs.shape[1:], jnp.bfloat16),
        compiler_params=pltpu.CompilerParams(vmem_limit_bytes=4 * MIB),
    )(mine, theirs)


def near_kernel(mine_ref, theirs_ref, arrived_ref, own_ref, *out_refs):
    for place, out_ref in enumerate((own_ref,) + out_refs):
        total = mine_ref[place] + theirs_ref[place].astype(jnp.float32)
        total = total + arrived_ref[place].astype(jnp.float32)
        out_ref[...] = total.astype(out_ref.dtype)


def near_sums(mine, theirs, arrived):
    block = theirs.shape[1:]
    return pl.pallas_call(
        near_kernel,
        in_specs=[VMEM_SPEC] * 3,
        out_specs=[VMEM_SPEC] * 4,
        out_shape=[jax.ShapeDtypeStruct(block, jnp.float32)]
        + [jax.ShapeDtypeStruct(block, jnp.bfloat16)] * 3,
        compiler_params=pltpu.CompilerParams(vmem_limit_bytes=4 * MIB),
    )(mine, theirs, arrived)


def finish_kernel(stream_ref, *refs):
    total = stream_ref[...].astype(jnp.float32)
    for share in refs[:-1]:
        total = total + share[...].astype(jnp.float32)
    refs[-1][...] = total.astype(jnp.bfloat16)


def finished(stream, shares):
    return pl.pallas_call(
        finish_kernel,
        in_specs=[VMEM_SPEC] * (1 + len(shares)),
        out_specs=VMEM_SPEC,
        out_shape=jax.ShapeDtypeStruct(stream.shape, jnp.bfloat16),
        compiler_params=pltpu.CompilerParams(vmem_limit_bytes=4 * MIB),
    )(stream, *shares)


def block_body(
    queries,
    new_kv,
    kv_pages,
    page_table,
    lengths,
    residual,
    out_weight,
    norm_gain,
    gate_weight,
    up_weight,
    down_weight,
):
    me = lax.axis_index("shard").astype(jnp.int32)[None]
    table = jnp.concatenate([page_table.reshape(-1), lengths, me])
    own, query_rows = packed(queries, norm_gain)
    middle, late = (4, 5, 6, 7), tuple(range(8, 16))

    (early_gate,) = fetched(table, (gate_weight, rows_at, late[:3]))
    near = stacked(near_pieces(own), (early_gate,))
    second = sent(near, 2)
    pages, left, of_second, *new_terms = readied(table, query_rows, kv_pages, new_kv, near)
    odd = sent(stacked([near, second], new_terms[:1]), 1)
    gains = near, second, odd
    along = page_terms(left, of_second, (0, 1, 2, 3), (near, second), pages)
    theirs = page_terms(left, of_second, late, (odd,), pages, (along,))
    across = page_terms(left, of_second, middle, (near, second), pages)

    theirs = sent(theirs, 1)
    across = across_core(of_second, across, theirs)
    arrived = sent(across, 2)
    gate_held, early_first = fetched(
        across, (gate_weight, rows_at, middle), (up_weight, rows_at, late[:2])
    )
    own = across_y(of_second, along, theirs, arrived, new_terms, (gate_held,))
    up_held, early_second, down_first = fetched(
        own,
        (up_weight, rows_at, middle),
        (up_weight, rows_at, late[2:6]),
        (down_weight, columns_at, middle),
    )
    near = combined(near_pieces(own), (up_held,))

    second = sent(near, 2)
    (down_rest,) = fetched(near, (down_weight, columns_at, (0, 1, 2, 3)))
    odd = sent(stacked([near, second], (down_rest,)), 1)
    stream = projected(near, second, odd, residual, out_weight)

    weights = gate_weight, up_weight
    near = near_pieces(stream)
    sums = feed((0,), near[:1], gains[0], (), *weights)
    first = stacked(near, sums[:1])
    second = sent(first, 2)
    sums = feed((1, 2, 3), near[1:], gains[0], sums, *weights)
    odd = sent(stacked([first, second], sums[:1]), 1)
    sums = feed(middle, [second], gains[1], sums, gate_held, up_held, held=True)
    early = (early_gate,), (early_first, early_second)
    hidden, theirs = hidden_units(late, odd, gains[2], early, weights, down_weight, sums)

    theirs = sent(theirs, 1)
    far = down_terms(hidden, down_first)
    arrived = sent(far_pairs(far, theirs), 2)
    mine = down_terms(hidden, down_rest)
    own, *others = near_sums(mine, theirs, arrived)
    shares = [sent(other, distance) for other, distance in zip(others[::-1], (12, 8, 4))]
    return finished(stream, shares + [own])


def solution(mesh):
    placed = (
        P(("groups", "shard"), None),
        P(("groups", "shard"), None, None),
        P(("groups", "shard"), None, None, None),
        P("groups", None),
        P("groups"),
        P("groups", "shard"),
        P(None, "shard"),
        P("shard"),
        P(None, "shard"),
        P(None, "shard"),
        P("shard", None),
    )
    chosen = block_body if mesh.shape["shard"] == 16 else body
    return jax.shard_map(
        chosen, mesh=mesh, in_specs=placed, out_specs=P("groups", "shard"), check_vma=False
    )
```

```python
import functools
import math

import jax
import jax.numpy as jnp
from jax import lax
from jax.experimental import pallas as pl
from jax.experimental.pallas import tpu as pltpu
from jax.sharding import PartitionSpec as P

D = 8192
HEADS = 64
KV_HEADS = 4
HEAD_DIM = 128


norm_eps = 1e-05


def swapped(array, axis, distance):
    return lax.ppermute(array, axis, [(i, i ^ 1 << distance) for i in range(lax.axis_size(axis))])


def new_token_terms(queries, new_kv, score_scale):
    seq_dev = queries.shape[0]
    group_size = HEADS // KV_HEADS
    query_heads = queries.reshape(seq_dev, KV_HEADS, group_size, HEAD_DIM)
    new_keys = new_kv[:, 0].reshape(seq_dev, KV_HEADS, HEAD_DIM)
    new_values = new_kv[:, 1].reshape(seq_dev, KV_HEADS, HEAD_DIM)
    scores = (
        jnp.einsum("bgqd,bgd->bgq", query_heads, new_keys, preferred_element_type=jnp.float32)
        * score_scale
    )
    weights = jnp.exp(scores)
    numerator = jnp.einsum(
        "bgq,bgd->bgqd",
        weights.astype(jnp.bfloat16),
        new_values,
        preferred_element_type=jnp.float32,
    )
    return (numerator.reshape(seq_dev, D), weights.reshape(seq_dev, HEADS))


def butterfly(items, position, mover):
    count = items[0].shape[0]
    for level in range(count.bit_length() - 1):
        upper_half = position // (1 << level) % 2 == 1
        halves = [
            entry.reshape((count >> level + 1, 2, 1 << level) + entry.shape[1:]) for entry in items
        ]
        outgoing = tuple(
            (jnp.where(upper_half, halves_one[:, 0], halves_one[:, 1]) for halves_one in halves)
        )
        incoming = mover(outgoing, level)
        rebuilt = []
        for entry, halves_one, arrived_one in zip(items, halves, incoming):
            lower_part = jnp.where(upper_half, arrived_one, halves_one[:, 0])
            upper_part = jnp.where(upper_half, halves_one[:, 1], arrived_one)
            rebuilt.append(jnp.stack([lower_part, upper_part], axis=1).reshape(entry.shape))
        items = tuple(rebuilt)
    return items


def body(
    queries,
    new_kv,
    kv_pages,
    page_table,
    lengths,
    residual,
    out_weight,
    norm_gain,
    gate_weight,
    up_weight,
    down_weight,
):
    seq_dev = queries.shape[0]
    page_count = kv_pages.shape[0]
    page_len = kv_pages.shape[2]
    all_seqs = page_table.shape[0]
    max_pages = page_table.shape[1]
    group_size = HEADS // KV_HEADS
    score_scale = 1.0 / math.sqrt(HEAD_DIM)
    device_pos = lax.axis_index("shard")
    own_first = device_pos * seq_dev
    own_lengths = lax.dynamic_slice_in_dim(lengths, own_first, seq_dev, 0)
    own_table = lax.dynamic_slice_in_dim(page_table, own_first, seq_dev, 0)
    holder_local = own_table // page_count % page_count
    page_ids = device_pos * page_count + jnp.arange(page_count, dtype=jnp.int32)
    matches = page_table[None, :, :] == page_ids[:, None, None]
    seq_of = jnp.sum(
        jnp.where(matches, jnp.arange(all_seqs, dtype=jnp.int32)[None, :, None], 0), axis=(1, 2)
    )
    owner_local = seq_of // seq_dev % page_count
    own_numerator, own_denominator = new_token_terms(queries, new_kv, score_scale)
    outgoing = jnp.zeros_like(kv_pages).at[owner_local].set(kv_pages)
    arrived = butterfly(
        (outgoing,), device_pos, lambda sending, level: (swapped(sending[0], "shard", level),)
    )[0]
    fetched = arrived[holder_local]
    context = max_pages * page_len
    key_rows = fetched[:, :, 0].reshape(seq_dev, context, KV_HEADS, HEAD_DIM)
    value_rows = fetched[:, :, 1].reshape(seq_dev, context, KV_HEADS, HEAD_DIM)
    query_heads = queries.reshape(seq_dev, KV_HEADS, group_size, HEAD_DIM)
    scores = (
        jnp.einsum("bgqd,btgd->bgqt", query_heads, key_rows, preferred_element_type=jnp.float32)
        * score_scale
    )
    position = jnp.arange(context, dtype=jnp.int32)
    alive = position[None, :] < own_lengths[:, None]
    weights = jnp.where(alive[:, None, None, :], jnp.exp(scores), 0.0)
    denominator = jnp.sum(weights, axis=-1).reshape(seq_dev, HEADS)
    numerator = jnp.einsum(
        "bgqt,btgd->bgqd",
        weights.astype(jnp.bfloat16),
        value_rows,
        preferred_element_type=jnp.float32,
    )
    numer_rows = numerator.reshape(seq_dev, D) + own_numerator
    denom_rows = denominator + own_denominator
    attended = (
        (numer_rows.reshape(seq_dev, HEADS, HEAD_DIM) / denom_rows[:, :, None])
        .reshape(seq_dev, D)
        .astype(jnp.bfloat16)
    )
    projected = jnp.dot(
        lax.all_gather(attended, "shard", axis=0, tiled=True),
        out_weight,
        preferred_element_type=jnp.float32,
    )
    stream = (residual.astype(jnp.float32) + projected).astype(jnp.bfloat16)
    wide = stream.astype(jnp.float32)
    square_sums = lax.psum(jnp.sum(wide * wide, axis=1), "shard")
    normed = (wide * lax.rsqrt(square_sums / D + norm_eps)[:, None] * norm_gain[None, :]).astype(
        jnp.bfloat16
    )
    block_cols = lax.all_gather(normed, "shard", axis=1, tiled=True)
    gate_acts = jnp.dot(block_cols, gate_weight, preferred_element_type=jnp.float32)
    up_acts = jnp.dot(block_cols, up_weight, preferred_element_type=jnp.float32)
    hidden = (jax.nn.silu(gate_acts) * up_acts).astype(jnp.bfloat16)
    partial_terms = jnp.dot(hidden, down_weight, preferred_element_type=jnp.float32)
    down_terms = lax.psum_scatter(partial_terms, "shard", scatter_dimension=1, tiled=True)
    return (wide + down_terms).astype(jnp.bfloat16)


GROUP = HEADS // KV_HEADS
TAIL = 16
MIB = 2**20
VMEM_SPEC = pl.BlockSpec(memory_space=pltpu.VMEM)
SMEM_SPEC = pl.BlockSpec(memory_space=pltpu.SMEM)
HBM_SPEC = pl.BlockSpec(memory_space=pltpu.HBM)
CHUNK = 512


def sent(array, distance):
    size = lax.axis_size("shard")
    return lax.ppermute(array, "shard", [(i, i ^ distance) for i in range(size)])


def stack_kernel(count, *refs):
    out_ref, place = refs[-1], 0
    for part in refs[:count]:
        size = part.shape[0] if len(part.shape) == 3 else 1
        out_ref[place : place + size] = part[...].reshape((size,) + part.shape[-2:])
        place += size


def stacked(parts, after):
    size = sum(part.shape[0] if part.ndim == 3 else 1 for part in parts)
    return pl.pallas_call(
        functools.partial(stack_kernel, len(parts)),
        in_specs=[VMEM_SPEC] * len(parts) + [pl.BlockSpec(memory_space=pl.ANY)] * len(after),
        out_specs=VMEM_SPEC,
        out_shape=jax.ShapeDtypeStruct((size,) + parts[0].shape[-2:], parts[0].dtype),
        compiler_params=pltpu.CompilerParams(vmem_limit_bytes=4 * MIB),
        cost_estimate=pl.CostEstimate(flops=0, bytes_accessed=16 * MIB, transcendentals=0),
    )(*parts, *after)


def near_pieces(piece):
    return [piece] + [sent(piece, distance) for distance in (4, 8, 12)]


def device_at(me, entry):
    return me ^ (entry % 4 * 4 + entry // 4 % 2 * 2 + entry // 8)


def started(count, *copies):
    def start(place, carry):
        for copy_at in copies:
            copy_at(place).start()
        return carry

    lax.fori_loop(0, count, start, 0)


def in_vmem(array):
    return pltpu.with_memory_space_constraint(array, pltpu.VMEM)


def in_hbm(array):
    return pltpu.with_memory_space_constraint(array, pltpu.HBM)


def two_terms(wide):
    high = wide.astype(jnp.bfloat16).astype(jnp.float32)
    return high, wide - high


def pack_kernel(query_hbm, gain_hbm, out_ref, rows_ref, query, gain, wide, sems):
    copies = [
        pltpu.make_async_copy(query_hbm, query, sems.at[0]),
        pltpu.make_async_copy(gain_hbm, gain, sems.at[1]),
    ]
    for copy in copies:
        copy.start()
    for copy in copies:
        copy.wait()
    rows = 2 * HEADS
    for head in range(HEADS):
        cols = slice(head * HEAD_DIM, (head + 1) * HEAD_DIM)
        wide[pl.ds(head, 2, HEADS), :] = query[:, cols].astype(jnp.float32)
    out_ref[:rows, :] = wide[...].astype(jnp.bfloat16)
    rows_ref[...] = wide[...].astype(jnp.bfloat16)
    high, rest = two_terms(gain[...])
    middle, low = two_terms(rest)
    filler = jnp.zeros((16 - 3 * high.shape[0], HEAD_DIM), jnp.float32)
    out_ref[rows:, :] = jnp.concatenate([high, middle, low, filler]).astype(jnp.bfloat16)


def packed(queries, norm_gain):
    rows = 2 * HEADS
    gain = norm_gain.reshape(-1, HEAD_DIM)
    return pl.pallas_call(
        pack_kernel,
        in_specs=[HBM_SPEC] * 2,
        out_specs=[VMEM_SPEC] * 2,
        out_shape=[
            jax.ShapeDtypeStruct((rows + 16, HEAD_DIM), jnp.bfloat16),
            jax.ShapeDtypeStruct((rows, HEAD_DIM), jnp.bfloat16),
        ],
        scratch_shapes=[
            pltpu.VMEM(queries.shape, jnp.bfloat16),
            pltpu.VMEM(gain.shape, jnp.float32),
            pltpu.VMEM((rows, HEAD_DIM), jnp.float32),
            pltpu.SemaphoreType.DMA((2,)),
        ],
        compiler_params=pltpu.CompilerParams(vmem_limit_bytes=4 * MIB),
    )(in_hbm(queries), in_hbm(gain))


def context_terms(query, keys, values, alive):
    numerators, denominators = [], []
    for head in range(KV_HEADS):
        cols = slice(head * HEAD_DIM, (head + 1) * HEAD_DIM)
        scores = lax.dot_general(
            query[head * GROUP : (head + 1) * GROUP],
            keys[:, cols],
            (((1,), (1,)), ((), ())),
            preferred_element_type=jnp.float32,
        ) * (1.0 / math.sqrt(HEAD_DIM))
        weights = jnp.where(alive, jnp.exp(scores), 0.0)
        denominators.append(jnp.sum(weights, axis=1, keepdims=True))
        numerators.append(
            jnp.dot(
                weights.astype(jnp.bfloat16), values[:, cols], preferred_element_type=jnp.float32
            )
        )
    return jnp.concatenate(numerators), jnp.concatenate(denominators)


def ready_kernel(table_ref, query_ref, pages_hbm, new_hbm, after_ref, pages, left_ref, second_ref, new_ref, lower_ref, new, sems):
    _, _, page_len, features = pages.shape
    count = pages_hbm.shape[0]
    sequences = 2 * 16
    per_row = (table_ref.shape[0] - 1) // sequences - 1
    me = table_ref[(per_row + 1) * sequences]
    new_copy = pltpu.make_async_copy(new_hbm, new, sems.at[16])
    new_copy.start()
    page_copy = lambda slot, entry: pltpu.make_async_copy(
        pages_hbm.at[slot], pages.at[entry], sems.at[entry]
    )
    line = lambda value: jnp.full((1, HEAD_DIM), value, dtype=jnp.int32)

    def ready(entry, carry):
        owner = device_at(me, entry)
        place, other = 0, 0
        for index in range(2 * per_row):
            holder = table_ref[2 * owner * per_row + index] // count
            place = jnp.where(holder == me, index, place)
            other = jnp.where(holder == me ^ 1, index, other)
        row = place // per_row
        slot = table_ref[2 * owner * per_row + place] % count
        page_copy(slot, entry).start()
        left = table_ref[sequences * per_row + 2 * owner + row] - page_len * (place % per_row)
        here = pl.ds(entry, 1)
        left_ref[here, :] = line(left)
        second_ref[here, :] = line(row)
        second_ref[pl.ds(16 + entry, 1), :] = line(other // per_row)
        return carry

    lax.fori_loop(0, 16, ready, 0)
    first_token = lax.broadcasted_iota(jnp.int32, (GROUP, 8), 1) < 1
    new_copy.wait()
    for row in range(2):
        lines = slice(row * HEADS, (row + 1) * HEADS)
        numerator, total = context_terms(
            query_ref[lines, :],
            jnp.broadcast_to(new[row, 0:1, :], (8, features)),
            jnp.broadcast_to(new[row, 1:2, :], (8, features)),
            first_token,
        )
        new_ref[lines, :] = numerator
        lower = jnp.swapaxes(jnp.broadcast_to(total, (HEADS, HEAD_DIM)), 0, 1)
        lower_ref[8 * row : 8 * (row + 1), :] = lower[:8]
    for entry in range(16):
        page_copy(0, entry).wait()


def readied(table, query_rows, kv_pages, new_kv, after):
    return pl.pallas_call(
        ready_kernel,
        in_specs=[SMEM_SPEC, VMEM_SPEC] + [HBM_SPEC] * 2 + [pl.BlockSpec(memory_space=pl.ANY)],
        out_specs=[VMEM_SPEC] * 5,
        out_shape=[
            pltpu.VMEM(kv_pages.shape, kv_pages.dtype),
            jax.ShapeDtypeStruct((16, HEAD_DIM), jnp.int32),
            jax.ShapeDtypeStruct((32, HEAD_DIM), jnp.int32),
            jax.ShapeDtypeStruct((2 * HEADS, HEAD_DIM), jnp.float32),
            jax.ShapeDtypeStruct((16, HEADS), jnp.float32),
        ],
        scratch_shapes=[pltpu.VMEM(new_kv.shape, jnp.bfloat16), pltpu.SemaphoreType.DMA((17,))],
        compiler_params=pltpu.CompilerParams(vmem_limit_bytes=4 * MIB),
        cost_estimate=pl.CostEstimate(flops=2**22, bytes_accessed=2**21, transcendentals=2**11),
    )(table, query_rows, in_hbm(kv_pages), in_hbm(new_kv), after)


def pages_kernel(entries, left_ref, second_ref, *refs):
    refs = list(refs)
    near, across = (refs.pop(0), refs.pop(0)) if entries[0] < 8 else (None, None)
    odd = None if entries[0] < 8 else refs.pop(0)
    pages, out_ref, scores, weights = refs[0], *refs[-3:]
    page_len, features = pages.shape[2:]
    line = lax.broadcasted_iota(jnp.int32, (HEADS, features), 0) // GROUP
    block = lax.broadcasted_iota(jnp.int32, (HEADS, features), 1) // HEAD_DIM
    own_block = (line == block).astype(jnp.float32).astype(jnp.bfloat16)
    for here, entry in enumerate(entries):
        source, place = piece_at(near, across, odd, entry)
        second = second_ref[entry : entry + 1, :].astype(jnp.float32)
        query = source[place, :HEADS, :].astype(jnp.float32) * (1.0 - second)
        query += source[place, HEADS : 2 * HEADS, :].astype(jnp.float32) * second
        query = query.astype(jnp.bfloat16)
        spread = jnp.concatenate([query] * KV_HEADS, axis=1) * own_block
        scores[here] = lax.dot_general(
            spread,
            pages[entry, 0],
            (((1,), (1,)), ((), ())),
            preferred_element_type=jnp.float32,
        )
    position = lax.broadcasted_iota(jnp.int32, (HEADS, page_len), 1)
    lane = lax.broadcasted_iota(jnp.int32, (HEADS, HEAD_DIM), 1)
    denominators = jnp.zeros((HEADS, HEAD_DIM), jnp.float32)
    for here, entry in enumerate(entries):
        raised = jnp.exp(scores[here] * (1.0 / math.sqrt(HEAD_DIM)))
        weight = jnp.where(position < left_ref[entry : entry + 1, :page_len], raised, 0.0)
        weights[here] = weight.astype(jnp.bfloat16)
        total = jnp.sum(weight, axis=1, keepdims=True)
        denominators = jnp.where(lane == here, total, denominators)
    for here, entry in enumerate(entries):
        numerator = jnp.dot(
            weights[here], pages[entry, 1], preferred_element_type=jnp.float32
        )
        for head in range(KV_HEADS):
            lines = slice(head * GROUP, (head + 1) * GROUP)
            out_ref[here * HEADS + head * GROUP : here * HEADS + (head + 1) * GROUP, :] = numerator[
                lines, head * HEAD_DIM : (head + 1) * HEAD_DIM
            ].astype(jnp.bfloat16)
    sealed(out_ref, jnp.swapaxes(denominators, 0, 1)[: len(entries)])


def sealed(out_ref, denominators):
    count = denominators.shape[0]
    filler = jnp.zeros((TAIL - count, HEAD_DIM), jnp.float32)
    lasts = jnp.concatenate(two_terms(denominators), axis=1)
    out_ref[count * HEADS :, :] = jnp.concatenate([lasts, filler]).astype(jnp.bfloat16)


def opened(message, place):
    start = message.shape[0] - TAIL
    last = message[start:, :].astype(jnp.float32)[place : place + 1]
    numerator = message[place * HEADS : (place + 1) * HEADS, :].astype(jnp.float32)
    return numerator, last[:, :HEADS] + last[:, HEADS:]


def piece_at(near, second, odd, entry):
    if entry < 4:
        return near, entry
    return (second, entry - 4) if entry < 8 else (odd, entry - 8)


def page_terms(left, second, entries, pieces, pages, beside=()):
    return pl.pallas_call(
        functools.partial(pages_kernel, entries),
        in_specs=[VMEM_SPEC] * (len(pieces) + 3)
        + [pl.BlockSpec(memory_space=pl.ANY)] * len(beside),
        out_specs=VMEM_SPEC,
        out_shape=jax.ShapeDtypeStruct((len(entries) * HEADS + TAIL, HEAD_DIM), jnp.bfloat16),
        scratch_shapes=[
            pltpu.VMEM((len(entries), HEADS, pages.shape[2]), jnp.float32),
            pltpu.VMEM((len(entries), HEADS, pages.shape[2]), jnp.bfloat16),
        ],
        compiler_params=pltpu.CompilerParams(vmem_limit_bytes=6 * MIB),
        cost_estimate=pl.CostEstimate(flops=2**26, bytes_accessed=2**20, transcendentals=2**14),
    )(left, second, *pieces, in_vmem(pages), *beside)


def two_rows(second_ref, entry, mine, theirs):
    sums = [[0.0, 0.0], [0.0, 0.0]]
    for line, (numerator, denominator) in zip((entry, 16 + entry), (mine, theirs)):
        second = second_ref[line : line + 1, :].astype(jnp.float32)
        for row, share in enumerate((1.0 - second, second)):
            sums[row][0] = sums[row][0] + numerator * share
            sums[row][1] = sums[row][1] + denominator * share[:, :HEADS]
    return sums


def core_kernel(second_ref, mine_ref, theirs_ref, out_ref):
    lowers = []
    for place in range(4):
        mine, theirs = opened(mine_ref, place), opened(theirs_ref, 4 + place)
        for row, (part, lower) in enumerate(two_rows(second_ref, 4 + place, mine, theirs)):
            start = (2 * place + row) * HEADS
            out_ref[start : start + HEADS, :] = part.astype(jnp.bfloat16)
            lowers.append(lower)
    sealed(out_ref, jnp.concatenate(lowers))


def across_core(second, mine, theirs):
    return pl.pallas_call(
        core_kernel,
        in_specs=[VMEM_SPEC] * 3,
        out_specs=VMEM_SPEC,
        out_shape=jax.ShapeDtypeStruct((8 * HEADS + TAIL, HEAD_DIM), jnp.bfloat16),
        compiler_params=pltpu.CompilerParams(vmem_limit_bytes=4 * MIB),
    )(second, mine, theirs)


def chip_kernel(second_ref, mine_ref, theirs_ref, arrived_ref, new_ref, lower_ref, *refs):
    out_ref = refs[-1]
    lowers = []
    for place in range(4):
        mine, theirs = opened(mine_ref, place), opened(theirs_ref, place)
        for row, (part, lower) in enumerate(two_rows(second_ref, place, mine, theirs)):
            arrived, arrived_lower = opened(arrived_ref, 2 * place + row)
            part, lower = part + arrived, lower + arrived_lower
            if place == 0:
                part = part + new_ref[row * HEADS : (row + 1) * HEADS, :]
                lower = lower + lower_ref[8 * row : 8 * row + 1, :]
            start = (2 * place + row) * HEADS
            out_ref[start : start + HEADS, :] = part.astype(jnp.bfloat16)
            lowers.append(lower)
    sealed(out_ref, jnp.concatenate(lowers))


def across_y(second, mine, theirs, arrived, new_terms, beside):
    return pl.pallas_call(
        chip_kernel,
        in_specs=[VMEM_SPEC] * 6 + [pl.BlockSpec(memory_space=pl.ANY)] * len(beside),
        out_specs=VMEM_SPEC,
        out_shape=jax.ShapeDtypeStruct((8 * HEADS + TAIL, HEAD_DIM), jnp.bfloat16),
        compiler_params=pltpu.CompilerParams(vmem_limit_bytes=4 * MIB),
    )(second, mine, theirs, arrived, *new_terms, *beside)


def combine_kernel(*refs):
    shares, out_ref = refs[:4], refs[-1]
    parts, lowers = [], []
    for place in range(4):
        for row in range(2):
            terms = [opened(share, 2 * (place ^ j) + row) for j, share in enumerate(shares)]
            parts.append(sum(part for part, _ in terms))
            lowers.append(sum(lower for _, lower in terms))
    lower = jnp.concatenate([jnp.concatenate(lowers), jnp.zeros((8, HEADS), jnp.float32)], axis=1)
    columns = jnp.swapaxes(lower, 0, 1)
    for index, part in enumerate(parts):
        lines = slice(index % 2 * HEADS, (index % 2 + 1) * HEADS)
        column = columns[:HEADS, index : index + 1]
        out_ref[index // 2, lines, :] = (part / column).astype(jnp.bfloat16)


def combined(shares, beside):
    return pl.pallas_call(
        combine_kernel,
        in_specs=[VMEM_SPEC] * 4 + [pl.BlockSpec(memory_space=pl.ANY)] * len(beside),
        out_specs=VMEM_SPEC,
        out_shape=jax.ShapeDtypeStruct((4, 2 * HEADS, HEAD_DIM), jnp.bfloat16),
        compiler_params=pltpu.CompilerParams(vmem_limit_bytes=4 * MIB),
        cost_estimate=pl.CostEstimate(
            flops=2**22, bytes_accessed=48 * MIB, transcendentals=2**11
        ),
    )(*shares, *beside)


def fetch_kernel(parts, after_ref, *refs):
    weights, outs, sems = refs[: len(parts)], refs[len(parts) : -1], refs[-1]
    me = lax.axis_index("shard")
    copies = []
    for (place_of, entries), weight_hbm, out_ref in zip(parts, weights, outs):
        for place, entry in enumerate(entries):
            copies.append(
                pltpu.make_async_copy(
                    place_of(weight_hbm, device_at(me, entry)),
                    out_ref.at[place],
                    sems.at[len(copies)],
                )
            )
    for copy in copies:
        copy.start()
    for copy in copies:
        copy.wait()


def fetched(after, *parts):
    count = sum(len(entries) for _, _, entries in parts)
    weights = [weight for weight, _, _ in parts]
    shapes = [
        pltpu.VMEM((len(entries),) + place_of(weight, None), weight.dtype)
        for weight, place_of, entries in parts
    ]
    size = sum(math.prod(shape.shape) for shape in shapes)
    return pl.pallas_call(
        functools.partial(fetch_kernel, [part[1:] for part in parts]),
        in_specs=[pl.BlockSpec(memory_space=pl.ANY)] + [HBM_SPEC] * len(parts),
        out_specs=[VMEM_SPEC] * len(parts),
        out_shape=shapes,
        scratch_shapes=[pltpu.SemaphoreType.DMA((count,))],
        compiler_params=pltpu.CompilerParams(vmem_limit_bytes=MIB),
        cost_estimate=pl.CostEstimate(flops=0, bytes_accessed=2 * size, transcendentals=0),
    )(after, *[in_hbm(weight) for weight in weights])


def rows_at(weight, device):
    if device is None:
        return (CHUNK, weight.shape[1])
    return weight.at[pl.ds(pl.multiple_of(device * CHUNK, CHUNK), CHUNK)]


def columns_at(weight, device):
    if device is None:
        return (weight.shape[0], CHUNK)
    return weight.at[:, pl.ds(pl.multiple_of(device * CHUNK, CHUNK), CHUNK)]


def out_kernel(
    near_ref,
    second_ref,
    odd_ref,
    weight_ref,
    residual,
    out_ref,
    wide,
    left,
):
    me = lax.axis_index("shard")
    for entry in range(16):
        source, place = piece_at(near_ref, second_ref, odd_ref, entry)
        start = pl.multiple_of(device_at(me, entry) * 2 * HEADS, 2 * HEADS)
        wide[pl.ds(start, 2 * HEADS), :] = source[place].astype(jnp.float32)
    for head in range(HEADS):
        rows = [wide[pl.ds(row * HEADS + head, 16, 2 * HEADS), :] for row in range(2)]
        left[:, head * HEAD_DIM : (head + 1) * HEAD_DIM] = jnp.concatenate(rows).astype(
            jnp.bfloat16
        )
    total = jnp.dot(left[...], weight_ref[...], preferred_element_type=jnp.float32)
    line = lax.broadcasted_iota(jnp.int32, (32, 32), 0)
    entry = lax.broadcasted_iota(jnp.int32, (32, 32), 1)
    turn = ((line % 2) * 16 + line // 2 == entry).astype(jnp.float32)
    turned = lax.dot_general(
        turn,
        total,
        (((1,), (0,)), ((), ())),
        precision=lax.Precision.HIGHEST,
        preferred_element_type=jnp.float32,
    )
    out_ref[...] = (residual[...].astype(jnp.float32) + turned).astype(jnp.bfloat16)


def projected(near, second, odd, residual, held_weight):
    rows, width = residual.shape
    return pl.pallas_call(
        out_kernel,
        in_specs=[VMEM_SPEC] * 5,
        out_specs=VMEM_SPEC,
        out_shape=jax.ShapeDtypeStruct((rows, width), jnp.bfloat16),
        scratch_shapes=[
            pltpu.VMEM((32 * HEADS, HEAD_DIM), jnp.float32),
            pltpu.VMEM((rows, D), jnp.bfloat16),
        ],
        compiler_params=pltpu.CompilerParams(vmem_limit_bytes=4 * MIB),
        cost_estimate=pl.CostEstimate(
            flops=2 * rows * D * width, bytes_accessed=2 * D * width, transcendentals=0
        ),
    )(near, second, odd, held_weight, residual)


def normed_pieces(entries, pieces, gain_ref, squares):
    lefts = []
    for place, entry in enumerate(entries):
        stream = pieces[place][...] if len(pieces) == len(entries) else pieces[0][place]
        wide = stream.astype(jnp.float32)
        squares = squares + wide * wide
        terms = gain_ref[entry % 4 if entry < 8 else entry - 8, 2 * HEADS :, :]
        terms = terms.astype(jnp.float32)
        gain = terms[0:4] + terms[4:8] + terms[8:12]
        gain = jnp.concatenate([gain[part : part + 1] for part in range(4)], axis=1)
        lefts.append((wide * gain).astype(jnp.bfloat16))
    return lefts, squares


def product(left, weight_at, width):
    step = 128 if width % 128 == 0 else width
    tiles = [
        jnp.dot(left, weight_at(slice(start, start + step)), preferred_element_type=jnp.float32)
        for start in range(0, width, step)
    ]
    return jnp.concatenate(tiles, axis=1)


def terms_of(lefts, blocks):
    left = jnp.concatenate(lefts, axis=1)
    here = lambda cols: blocks[:, :, cols].reshape(left.shape[1], -1)
    return product(left, here, blocks.shape[-1])


def feed_kernel(entries, piece_count, held, ahead, *refs):
    refs = list(refs)
    take = lambda number: [refs.pop(0) for _ in range(number)]
    pieces = take(piece_count)
    gain_ref, gate_ref, up_ref = take(3)
    gates_in, ups_in, squares_in = [None] * 3 if entries[0] == 0 else take(3)
    ahead_hbm = take(1)[0] if ahead else None
    gates, ups, squares_out = take(3)
    copies = []
    if ahead:
        ahead_out, ahead_sems = refs
        me = lax.axis_index("shard")
        ahead_copy = lambda place: pltpu.make_async_copy(
            rows_at(ahead_hbm, device_at(me, ahead[0] + place)),
            ahead_out.at[place],
            ahead_sems.at[place],
        )
        started(len(ahead), ahead_copy)
    if not held:
        sources = gate_ref, up_ref
        *targets, sems = refs
        gate_ref, up_ref = targets
        me = lax.axis_index("shard")
        count = len(entries)
        copies = [
            lambda place, number=number: pltpu.make_async_copy(
                rows_at(sources[number], device_at(me, entries[0] + place)),
                targets[number].at[place],
                sems.at[number * count + place],
            )
            for number in range(2)
        ]
        started(count, *copies)
    squares = 0.0 if squares_in is None else squares_in[...]
    lefts, squares_out[...] = normed_pieces(entries, pieces, gain_ref, squares)
    both = ((gates, gates_in, gate_ref), (ups, ups_in, up_ref))
    if held:
        for total, start, blocks in both:
            total[...] = start[...] + terms_of(lefts, blocks)
        for place in range(len(ahead)):
            ahead_copy(place).wait()
        return
    for place in range(len(entries)):
        for number, (total, start, blocks) in enumerate(both):
            copies[number](place).wait()
            terms = jnp.dot(lefts[place], blocks[place], preferred_element_type=jnp.float32)
            if place > 0:
                total[...] += terms
            else:
                total[...] = terms if start is None else start[...] + terms


def feed(entries, pieces, gain, sums, gate_weight, up_weight, held=False, ahead=(), ahead_weight=None):
    rows = pieces[0].shape[-2]
    width = gate_weight.shape[-1]
    count = len(entries)
    total = jax.ShapeDtypeStruct((rows, width), jnp.float32)
    here = in_vmem if held else in_hbm
    slots = pltpu.VMEM((count, CHUNK, width), jnp.bfloat16)
    return pl.pallas_call(
        functools.partial(feed_kernel, entries, len(pieces), held, ahead),
        in_specs=[VMEM_SPEC] * (len(pieces) + 1)
        + [VMEM_SPEC if held else HBM_SPEC] * 2
        + [VMEM_SPEC] * len(sums)
        + [HBM_SPEC] * bool(ahead),
        out_specs=[VMEM_SPEC] * (3 + bool(ahead)),
        out_shape=[total, total, jax.ShapeDtypeStruct((rows, CHUNK), jnp.float32)]
        + [pltpu.VMEM((len(ahead), CHUNK, width), jnp.bfloat16)] * bool(ahead),
        scratch_shapes=[pltpu.SemaphoreType.DMA((max(len(ahead), 1),))] * bool(ahead)
        if held
        else [slots, slots, pltpu.SemaphoreType.DMA((2 * count,))],
        compiler_params=pltpu.CompilerParams(
            vmem_limit_bytes=2 * MIB + (0 if held else 4 * count * CHUNK * width)
        ),
        cost_estimate=pl.CostEstimate(
            flops=4 * rows * count * CHUNK * width,
            bytes_accessed=4 * count * CHUNK * width,
            transcendentals=0,
        ),
    )(*pieces, gain, here(gate_weight), here(up_weight), *sums, *([in_hbm(ahead_weight)] if ahead else []))


def hidden_kernel(entries, early_counts, *refs):
    refs = list(refs)
    take = lambda number: [refs.pop(0) for _ in range(number)]
    odd_ref, gain_ref = take(2)
    early = [take(number) for number in early_counts]
    sources = take(2)
    (down_hbm,) = take(1)
    starts = take(2)
    squares_in, hidden_ref, out_ref = take(3)
    totals = take(2)
    held, sems = take(2), take(2)
    down_held, down_sems = refs
    me = lax.axis_index("shard")
    count = len(entries)
    counts = [buffer.shape[0] for buffer in held]
    copies = [
        lambda place, number=number: pltpu.make_async_copy(
            rows_at(sources[number], device_at(me, entries[-1] + 1 - counts[number] + place)),
            held[number].at[place],
            sems[number].at[place],
        )
        for number in range(2)
    ]
    down_copy = lambda place: pltpu.make_async_copy(
        columns_at(down_hbm, device_at(me, entries[0] + place)),
        down_held.at[place],
        down_sems.at[place],
    )
    for number in range(2):
        started(counts[number], copies[number])
    started(count, down_copy)
    lefts, squares = normed_pieces(entries, [odd_ref], gain_ref, squares_in[...])
    places = [0, 0]
    for number in range(2):
        total = starts[number][...]
        for part in early[number]:
            place = places[number]
            places[number] += part.shape[0]
            total += terms_of(lefts[place : places[number]], part)
        totals[number][...] = total
    for number in range(2):
        for place in range(counts[number]):
            copies[number](place).wait()
        totals[number][...] += terms_of(lefts[places[number] :], held[number])
    scale = lax.rsqrt(jnp.sum(squares, axis=1, keepdims=True) / D + norm_eps)
    gates, ups = totals[0][...] * scale, totals[1][...] * scale
    hidden_ref[...] = (jax.nn.silu(gates) * ups).astype(jnp.bfloat16)
    for place in range(count):
        down_copy(place).wait()
        here = lambda cols: down_held[place, :, cols]
        out_ref[place] = product(hidden_ref[...], here, CHUNK).astype(jnp.bfloat16)


def hidden_units(entries, odd, gain, early, weights, down_weight, sums):
    rows = odd.shape[1]
    width = weights[0].shape[1]
    count = len(entries)
    later = [count - sum(part.shape[0] for part in parts) for parts in early]
    total = pltpu.VMEM((rows, width), jnp.float32)
    held = [pltpu.VMEM((number, CHUNK, width), jnp.bfloat16) for number in later]
    early_parts = [part for parts in early for part in parts]
    return pl.pallas_call(
        functools.partial(hidden_kernel, entries, [len(parts) for parts in early]),
        in_specs=[VMEM_SPEC] * (2 + len(early_parts)) + [HBM_SPEC] * 3 + [VMEM_SPEC] * 3,
        out_specs=[VMEM_SPEC] * 2,
        out_shape=[
            jax.ShapeDtypeStruct((rows, width), jnp.bfloat16),
            jax.ShapeDtypeStruct((count, rows, CHUNK), jnp.bfloat16),
        ],
        scratch_shapes=[total, total]
        + held
        + [pltpu.SemaphoreType.DMA((number,)) for number in later]
        + [pltpu.VMEM((count, width, CHUNK), jnp.bfloat16), pltpu.SemaphoreType.DMA((count,))],
        compiler_params=pltpu.CompilerParams(
            vmem_limit_bytes=2 * (sum(later) + count) * CHUNK * width + MIB
        ),
        cost_estimate=pl.CostEstimate(
            flops=2 * rows * 3 * count * CHUNK * width,
            bytes_accessed=2 * 3 * count * CHUNK * width,
            transcendentals=rows * width,
        ),
    )(
        odd,
        gain,
        *[in_vmem(part) for part in early_parts],
        *[in_hbm(weight) for weight in weights],
        in_hbm(down_weight),
        *sums,
    )


def down_kernel(hidden_ref, held_ref, out_ref):
    for place in range(held_ref.shape[0]):
        out_ref[place] = product(hidden_ref[...], lambda cols: held_ref[place, :, cols], CHUNK)


def down_terms(hidden, held):
    rows, depth = hidden.shape
    count = held.shape[0]
    return pl.pallas_call(
        down_kernel,
        in_specs=[VMEM_SPEC] * 2,
        out_specs=VMEM_SPEC,
        out_shape=jax.ShapeDtypeStruct((count, rows, CHUNK), jnp.float32),
        compiler_params=pltpu.CompilerParams(vmem_limit_bytes=4 * MIB),
        cost_estimate=pl.CostEstimate(
            flops=2 * rows * depth * CHUNK * count,
            bytes_accessed=2 * depth * CHUNK * count,
            transcendentals=0,
        ),
    )(hidden, in_vmem(held))


def far_kernel(mine_ref, theirs_ref, out_ref):
    for place in range(4):
        out_ref[place] = (mine_ref[place] + theirs_ref[4 + place].astype(jnp.float32)).astype(
            jnp.bfloat16
        )


def far_pairs(mine, theirs):
    return pl.pallas_call(
        far_kernel,
        in_specs=[VMEM_SPEC] * 2,
        out_specs=VMEM_SPEC,
        out_shape=jax.ShapeDtypeStruct((4,) + theirs.shape[1:], jnp.bfloat16),
        compiler_params=pltpu.CompilerParams(vmem_limit_bytes=4 * MIB),
    )(mine, theirs)


def near_kernel(mine_ref, theirs_ref, arrived_ref, own_ref, *out_refs):
    for place, out_ref in enumerate((own_ref,) + out_refs):
        total = mine_ref[place] + theirs_ref[place].astype(jnp.float32)
        total = total + arrived_ref[place].astype(jnp.float32)
        out_ref[...] = total.astype(out_ref.dtype)


def near_sums(mine, theirs, arrived):
    block = theirs.shape[1:]
    return pl.pallas_call(
        near_kernel,
        in_specs=[VMEM_SPEC] * 3,
        out_specs=[VMEM_SPEC] * 4,
        out_shape=[jax.ShapeDtypeStruct(block, jnp.float32)]
        + [jax.ShapeDtypeStruct(block, jnp.bfloat16)] * 3,
        compiler_params=pltpu.CompilerParams(vmem_limit_bytes=4 * MIB),
    )(mine, theirs, arrived)


def finish_kernel(stream_ref, *refs):
    total = stream_ref[...].astype(jnp.float32)
    for share in refs[:-1]:
        total = total + share[...].astype(jnp.float32)
    refs[-1][...] = total.astype(jnp.bfloat16)


def finished(stream, shares):
    return pl.pallas_call(
        finish_kernel,
        in_specs=[VMEM_SPEC] * (1 + len(shares)),
        out_specs=VMEM_SPEC,
        out_shape=jax.ShapeDtypeStruct(stream.shape, jnp.bfloat16),
        compiler_params=pltpu.CompilerParams(vmem_limit_bytes=4 * MIB),
    )(stream, *shares)


def block_body(
    queries,
    new_kv,
    kv_pages,
    page_table,
    lengths,
    residual,
    out_weight,
    norm_gain,
    gate_weight,
    up_weight,
    down_weight,
):
    me = lax.axis_index("shard").astype(jnp.int32)[None]
    table = jnp.concatenate([page_table.reshape(-1), lengths, me])
    own, query_rows = packed(queries, norm_gain)
    middle, late = (4, 5, 6, 7), tuple(range(8, 16))

    (early_gate,) = fetched(table, (gate_weight, rows_at, late[:3]))
    near = stacked(near_pieces(own), (early_gate,))
    second = sent(near, 2)
    pages, left, of_second, *new_terms = readied(table, query_rows, kv_pages, new_kv, near)
    odd = sent(stacked([near, second], new_terms[:1]), 1)
    gains = near, second, odd
    along = page_terms(left, of_second, (0, 1, 2, 3), (near, second), pages)
    theirs = page_terms(left, of_second, late, (odd,), pages, (along,))
    across = page_terms(left, of_second, middle, (near, second), pages)

    theirs = sent(theirs, 1)
    across = across_core(of_second, across, theirs)
    arrived = sent(across, 2)
    gate_held, early_first = fetched(
        across, (gate_weight, rows_at, middle), (up_weight, rows_at, late[:2])
    )
    own = across_y(of_second, along, theirs, arrived, new_terms, (gate_held,))
    up_held, early_second, down_first = fetched(
        own,
        (up_weight, rows_at, middle),
        (up_weight, rows_at, late[2:6]),
        (down_weight, columns_at, middle),
    )
    near = combined(near_pieces(own), (up_held,))

    second = sent(near, 2)
    (down_rest,) = fetched(near, (down_weight, columns_at, (0, 1, 2, 3)))
    odd = sent(stacked([near, second], (down_rest,)), 1)
    stream = projected(near, second, odd, residual, out_weight)

    weights = gate_weight, up_weight
    near = near_pieces(stream)
    sums = feed((0,), near[:1], gains[0], (), *weights)
    first = stacked(near, sums[:1])
    second = sent(first, 2)
    sums = feed((1, 2, 3), near[1:], gains[0], sums, *weights)
    odd = sent(stacked([first, second], sums[:1]), 1)
    *sums, more_gate = feed(
        middle,
        [second],
        gains[1],
        sums,
        gate_held,
        up_held,
        held=True,
        ahead=late[3:5],
        ahead_weight=gate_weight,
    )
    early = (early_gate, more_gate), (early_first, early_second)
    hidden, theirs = hidden_units(late, odd, gains[2], early, weights, down_weight, sums)

    theirs = sent(theirs, 1)
    far = down_terms(hidden, down_first)
    arrived = sent(far_pairs(far, theirs), 2)
    mine = down_terms(hidden, down_rest)
    own, *others = near_sums(mine, theirs, arrived)
    shares = [sent(other, distance) for other, distance in zip(others[::-1], (12, 8, 4))]
    return finished(stream, shares + [own])


def solution(mesh):
    placed = (
        P(("groups", "shard"), None),
        P(("groups", "shard"), None, None),
        P(("groups", "shard"), None, None, None),
        P("groups", None),
        P("groups"),
        P("groups", "shard"),
        P(None, "shard"),
        P("shard"),
        P(None, "shard"),
        P(None, "shard"),
        P("shard", None),
    )
    chosen = block_body if mesh.shape["shard"] == 16 else body
    return jax.shard_map(
        chosen, mesh=mesh, in_specs=placed, out_specs=P("groups", "shard"), check_vma=False
    )
```

```python
import functools
import math

import jax
import jax.numpy as jnp
from jax import lax
from jax.experimental import pallas as pl
from jax.experimental.pallas import tpu as pltpu
from jax.sharding import PartitionSpec as P

D = 8192
HEADS = 64
KV_HEADS = 4
HEAD_DIM = 128


norm_eps = 1e-05


def swapped(array, axis, distance):
    return lax.ppermute(array, axis, [(i, i ^ 1 << distance) for i in range(lax.axis_size(axis))])


def new_token_terms(queries, new_kv, score_scale):
    seq_dev = queries.shape[0]
    group_size = HEADS // KV_HEADS
    query_heads = queries.reshape(seq_dev, KV_HEADS, group_size, HEAD_DIM)
    new_keys = new_kv[:, 0].reshape(seq_dev, KV_HEADS, HEAD_DIM)
    new_values = new_kv[:, 1].reshape(seq_dev, KV_HEADS, HEAD_DIM)
    scores = (
        jnp.einsum("bgqd,bgd->bgq", query_heads, new_keys, preferred_element_type=jnp.float32)
        * score_scale
    )
    weights = jnp.exp(scores)
    numerator = jnp.einsum(
        "bgq,bgd->bgqd",
        weights.astype(jnp.bfloat16),
        new_values,
        preferred_element_type=jnp.float32,
    )
    return (numerator.reshape(seq_dev, D), weights.reshape(seq_dev, HEADS))


def butterfly(items, position, mover):
    count = items[0].shape[0]
    for level in range(count.bit_length() - 1):
        upper_half = position // (1 << level) % 2 == 1
        halves = [
            entry.reshape((count >> level + 1, 2, 1 << level) + entry.shape[1:]) for entry in items
        ]
        outgoing = tuple(
            (jnp.where(upper_half, halves_one[:, 0], halves_one[:, 1]) for halves_one in halves)
        )
        incoming = mover(outgoing, level)
        rebuilt = []
        for entry, halves_one, arrived_one in zip(items, halves, incoming):
            lower_part = jnp.where(upper_half, arrived_one, halves_one[:, 0])
            upper_part = jnp.where(upper_half, halves_one[:, 1], arrived_one)
            rebuilt.append(jnp.stack([lower_part, upper_part], axis=1).reshape(entry.shape))
        items = tuple(rebuilt)
    return items


def body(
    queries,
    new_kv,
    kv_pages,
    page_table,
    lengths,
    residual,
    out_weight,
    norm_gain,
    gate_weight,
    up_weight,
    down_weight,
):
    seq_dev = queries.shape[0]
    page_count = kv_pages.shape[0]
    page_len = kv_pages.shape[2]
    all_seqs = page_table.shape[0]
    max_pages = page_table.shape[1]
    group_size = HEADS // KV_HEADS
    score_scale = 1.0 / math.sqrt(HEAD_DIM)
    device_pos = lax.axis_index("shard")
    own_first = device_pos * seq_dev
    own_lengths = lax.dynamic_slice_in_dim(lengths, own_first, seq_dev, 0)
    own_table = lax.dynamic_slice_in_dim(page_table, own_first, seq_dev, 0)
    holder_local = own_table // page_count % page_count
    page_ids = device_pos * page_count + jnp.arange(page_count, dtype=jnp.int32)
    matches = page_table[None, :, :] == page_ids[:, None, None]
    seq_of = jnp.sum(
        jnp.where(matches, jnp.arange(all_seqs, dtype=jnp.int32)[None, :, None], 0), axis=(1, 2)
    )
    owner_local = seq_of // seq_dev % page_count
    own_numerator, own_denominator = new_token_terms(queries, new_kv, score_scale)
    outgoing = jnp.zeros_like(kv_pages).at[owner_local].set(kv_pages)
    arrived = butterfly(
        (outgoing,), device_pos, lambda sending, level: (swapped(sending[0], "shard", level),)
    )[0]
    fetched = arrived[holder_local]
    context = max_pages * page_len
    key_rows = fetched[:, :, 0].reshape(seq_dev, context, KV_HEADS, HEAD_DIM)
    value_rows = fetched[:, :, 1].reshape(seq_dev, context, KV_HEADS, HEAD_DIM)
    query_heads = queries.reshape(seq_dev, KV_HEADS, group_size, HEAD_DIM)
    scores = (
        jnp.einsum("bgqd,btgd->bgqt", query_heads, key_rows, preferred_element_type=jnp.float32)
        * score_scale
    )
    position = jnp.arange(context, dtype=jnp.int32)
    alive = position[None, :] < own_lengths[:, None]
    weights = jnp.where(alive[:, None, None, :], jnp.exp(scores), 0.0)
    denominator = jnp.sum(weights, axis=-1).reshape(seq_dev, HEADS)
    numerator = jnp.einsum(
        "bgqt,btgd->bgqd",
        weights.astype(jnp.bfloat16),
        value_rows,
        preferred_element_type=jnp.float32,
    )
    numer_rows = numerator.reshape(seq_dev, D) + own_numerator
    denom_rows = denominator + own_denominator
    attended = (
        (numer_rows.reshape(seq_dev, HEADS, HEAD_DIM) / denom_rows[:, :, None])
        .reshape(seq_dev, D)
        .astype(jnp.bfloat16)
    )
    projected = jnp.dot(
        lax.all_gather(attended, "shard", axis=0, tiled=True),
        out_weight,
        preferred_element_type=jnp.float32,
    )
    stream = (residual.astype(jnp.float32) + projected).astype(jnp.bfloat16)
    wide = stream.astype(jnp.float32)
    square_sums = lax.psum(jnp.sum(wide * wide, axis=1), "shard")
    normed = (wide * lax.rsqrt(square_sums / D + norm_eps)[:, None] * norm_gain[None, :]).astype(
        jnp.bfloat16
    )
    block_cols = lax.all_gather(normed, "shard", axis=1, tiled=True)
    gate_acts = jnp.dot(block_cols, gate_weight, preferred_element_type=jnp.float32)
    up_acts = jnp.dot(block_cols, up_weight, preferred_element_type=jnp.float32)
    hidden = (jax.nn.silu(gate_acts) * up_acts).astype(jnp.bfloat16)
    partial_terms = jnp.dot(hidden, down_weight, preferred_element_type=jnp.float32)
    down_terms = lax.psum_scatter(partial_terms, "shard", scatter_dimension=1, tiled=True)
    return (wide + down_terms).astype(jnp.bfloat16)


GROUP = HEADS // KV_HEADS
TAIL = 16
MIB = 2**20
VMEM_SPEC = pl.BlockSpec(memory_space=pltpu.VMEM)
SMEM_SPEC = pl.BlockSpec(memory_space=pltpu.SMEM)
HBM_SPEC = pl.BlockSpec(memory_space=pltpu.HBM)
CHUNK = 512


def sent(array, distance):
    size = lax.axis_size("shard")
    return lax.ppermute(array, "shard", [(i, i ^ distance) for i in range(size)])


def stack_kernel(count, *refs):
    out_ref, place = refs[-1], 0
    for part in refs[:count]:
        size = part.shape[0] if len(part.shape) == 3 else 1
        out_ref[place : place + size] = part[...].reshape((size,) + part.shape[-2:])
        place += size


def stacked(parts, after):
    size = sum(part.shape[0] if part.ndim == 3 else 1 for part in parts)
    return pl.pallas_call(
        functools.partial(stack_kernel, len(parts)),
        in_specs=[VMEM_SPEC] * len(parts) + [pl.BlockSpec(memory_space=pl.ANY)] * len(after),
        out_specs=VMEM_SPEC,
        out_shape=jax.ShapeDtypeStruct((size,) + parts[0].shape[-2:], parts[0].dtype),
        compiler_params=pltpu.CompilerParams(vmem_limit_bytes=4 * MIB),
        cost_estimate=pl.CostEstimate(flops=0, bytes_accessed=16 * MIB, transcendentals=0),
    )(*parts, *after)


def near_pieces(piece):
    sends = {distance: sent(piece, distance) for distance in (8, 12, 4)}
    return [piece] + [sends[distance] for distance in (4, 8, 12)]


def device_at(me, entry):
    return me ^ (entry % 4 * 4 + entry // 4 % 2 * 2 + entry // 8)


def started(count, *copies):
    def start(place, carry):
        for copy_at in copies:
            copy_at(place).start()
        return carry

    lax.fori_loop(0, count, start, 0)


def in_vmem(array):
    return pltpu.with_memory_space_constraint(array, pltpu.VMEM)


def in_hbm(array):
    return pltpu.with_memory_space_constraint(array, pltpu.HBM)


def two_terms(wide):
    high = wide.astype(jnp.bfloat16).astype(jnp.float32)
    return high, wide - high


def pack_kernel(query_hbm, gain_hbm, out_ref, rows_ref, query, gain, wide, sems):
    copies = [
        pltpu.make_async_copy(query_hbm, query, sems.at[0]),
        pltpu.make_async_copy(gain_hbm, gain, sems.at[1]),
    ]
    for copy in copies:
        copy.start()
    for copy in copies:
        copy.wait()
    rows = 2 * HEADS
    for head in range(HEADS):
        cols = slice(head * HEAD_DIM, (head + 1) * HEAD_DIM)
        wide[pl.ds(head, 2, HEADS), :] = query[:, cols].astype(jnp.float32)
    out_ref[:rows, :] = wide[...].astype(jnp.bfloat16)
    rows_ref[...] = wide[...].astype(jnp.bfloat16)
    high, rest = two_terms(gain[...])
    middle, low = two_terms(rest)
    filler = jnp.zeros((16 - 3 * high.shape[0], HEAD_DIM), jnp.float32)
    out_ref[rows:, :] = jnp.concatenate([high, middle, low, filler]).astype(jnp.bfloat16)


def packed(queries, norm_gain):
    rows = 2 * HEADS
    gain = norm_gain.reshape(-1, HEAD_DIM)
    return pl.pallas_call(
        pack_kernel,
        in_specs=[HBM_SPEC] * 2,
        out_specs=[VMEM_SPEC] * 2,
        out_shape=[
            jax.ShapeDtypeStruct((rows + 16, HEAD_DIM), jnp.bfloat16),
            jax.ShapeDtypeStruct((rows, HEAD_DIM), jnp.bfloat16),
        ],
        scratch_shapes=[
            pltpu.VMEM(queries.shape, jnp.bfloat16),
            pltpu.VMEM(gain.shape, jnp.float32),
            pltpu.VMEM((rows, HEAD_DIM), jnp.float32),
            pltpu.SemaphoreType.DMA((2,)),
        ],
        compiler_params=pltpu.CompilerParams(vmem_limit_bytes=4 * MIB),
    )(in_hbm(queries), in_hbm(gain))


def context_terms(query, keys, values, alive):
    numerators, denominators = [], []
    for head in range(KV_HEADS):
        cols = slice(head * HEAD_DIM, (head + 1) * HEAD_DIM)
        scores = lax.dot_general(
            query[head * GROUP : (head + 1) * GROUP],
            keys[:, cols],
            (((1,), (1,)), ((), ())),
            preferred_element_type=jnp.float32,
        ) * (1.0 / math.sqrt(HEAD_DIM))
        weights = jnp.where(alive, jnp.exp(scores), 0.0)
        denominators.append(jnp.sum(weights, axis=1, keepdims=True))
        numerators.append(
            jnp.dot(
                weights.astype(jnp.bfloat16), values[:, cols], preferred_element_type=jnp.float32
            )
        )
    return jnp.concatenate(numerators), jnp.concatenate(denominators)


def ready_kernel(table_ref, query_ref, pages_hbm, new_hbm, after_ref, pages, left_ref, second_ref, new_ref, lower_ref, new, sems):
    _, _, page_len, features = pages.shape
    count = pages_hbm.shape[0]
    sequences = 2 * 16
    per_row = (table_ref.shape[0] - 1) // sequences - 1
    me = table_ref[(per_row + 1) * sequences]
    new_copy = pltpu.make_async_copy(new_hbm, new, sems.at[16])
    new_copy.start()
    page_copy = lambda slot, entry: pltpu.make_async_copy(
        pages_hbm.at[slot], pages.at[entry], sems.at[entry]
    )
    line = lambda value: jnp.full((1, HEAD_DIM), value, dtype=jnp.int32)

    def ready(entry, carry):
        owner = device_at(me, entry)
        place, other = 0, 0
        for index in range(2 * per_row):
            holder = table_ref[2 * owner * per_row + index] // count
            place = jnp.where(holder == me, index, place)
            other = jnp.where(holder == me ^ 1, index, other)
        row = place // per_row
        slot = table_ref[2 * owner * per_row + place] % count
        page_copy(slot, entry).start()
        left = table_ref[sequences * per_row + 2 * owner + row] - page_len * (place % per_row)
        here = pl.ds(entry, 1)
        left_ref[here, :] = line(left)
        second_ref[here, :] = line(row)
        second_ref[pl.ds(16 + entry, 1), :] = line(other // per_row)
        return carry

    lax.fori_loop(0, 16, ready, 0)
    first_token = lax.broadcasted_iota(jnp.int32, (GROUP, 8), 1) < 1
    new_copy.wait()
    for row in range(2):
        lines = slice(row * HEADS, (row + 1) * HEADS)
        numerator, total = context_terms(
            query_ref[lines, :],
            jnp.broadcast_to(new[row, 0:1, :], (8, features)),
            jnp.broadcast_to(new[row, 1:2, :], (8, features)),
            first_token,
        )
        new_ref[lines, :] = numerator
        lower = jnp.swapaxes(jnp.broadcast_to(total, (HEADS, HEAD_DIM)), 0, 1)
        lower_ref[8 * row : 8 * (row + 1), :] = lower[:8]
    for entry in range(16):
        page_copy(0, entry).wait()


def readied(table, query_rows, kv_pages, new_kv, after):
    return pl.pallas_call(
        ready_kernel,
        in_specs=[SMEM_SPEC, VMEM_SPEC] + [HBM_SPEC] * 2 + [pl.BlockSpec(memory_space=pl.ANY)],
        out_specs=[VMEM_SPEC] * 5,
        out_shape=[
            pltpu.VMEM(kv_pages.shape, kv_pages.dtype),
            jax.ShapeDtypeStruct((16, HEAD_DIM), jnp.int32),
            jax.ShapeDtypeStruct((32, HEAD_DIM), jnp.int32),
            jax.ShapeDtypeStruct((2 * HEADS, HEAD_DIM), jnp.float32),
            jax.ShapeDtypeStruct((16, HEADS), jnp.float32),
        ],
        scratch_shapes=[pltpu.VMEM(new_kv.shape, jnp.bfloat16), pltpu.SemaphoreType.DMA((17,))],
        compiler_params=pltpu.CompilerParams(vmem_limit_bytes=4 * MIB),
        cost_estimate=pl.CostEstimate(flops=2**22, bytes_accessed=2**21, transcendentals=2**11),
    )(table, query_rows, in_hbm(kv_pages), in_hbm(new_kv), after)


def pages_kernel(entries, left_ref, second_ref, *refs):
    refs = list(refs)
    near, across = (refs.pop(0), refs.pop(0)) if entries[0] < 8 else (None, None)
    odd = None if entries[0] < 8 else refs.pop(0)
    pages, out_ref, scores, weights = refs[0], *refs[-3:]
    page_len, features = pages.shape[2:]
    line = lax.broadcasted_iota(jnp.int32, (HEADS, features), 0) // GROUP
    block = lax.broadcasted_iota(jnp.int32, (HEADS, features), 1) // HEAD_DIM
    own_block = (line == block).astype(jnp.float32).astype(jnp.bfloat16)
    for here, entry in enumerate(entries):
        source, place = piece_at(near, across, odd, entry)
        second = second_ref[entry : entry + 1, :].astype(jnp.float32)
        query = source[place, :HEADS, :].astype(jnp.float32) * (1.0 - second)
        query += source[place, HEADS : 2 * HEADS, :].astype(jnp.float32) * second
        query = query.astype(jnp.bfloat16)
        spread = jnp.concatenate([query] * KV_HEADS, axis=1) * own_block
        scores[here] = lax.dot_general(
            spread,
            pages[entry, 0],
            (((1,), (1,)), ((), ())),
            preferred_element_type=jnp.float32,
        )
    position = lax.broadcasted_iota(jnp.int32, (HEADS, page_len), 1)
    lane = lax.broadcasted_iota(jnp.int32, (HEADS, HEAD_DIM), 1)
    denominators = jnp.zeros((HEADS, HEAD_DIM), jnp.float32)
    for here, entry in enumerate(entries):
        raised = jnp.exp(scores[here] * (1.0 / math.sqrt(HEAD_DIM)))
        weight = jnp.where(position < left_ref[entry : entry + 1, :page_len], raised, 0.0)
        weights[here] = weight.astype(jnp.bfloat16)
        total = jnp.sum(weight, axis=1, keepdims=True)
        denominators = jnp.where(lane == here, total, denominators)
    for here, entry in enumerate(entries):
        numerator = jnp.dot(
            weights[here], pages[entry, 1], preferred_element_type=jnp.float32
        )
        for head in range(KV_HEADS):
            lines = slice(head * GROUP, (head + 1) * GROUP)
            out_ref[here * HEADS + head * GROUP : here * HEADS + (head + 1) * GROUP, :] = numerator[
                lines, head * HEAD_DIM : (head + 1) * HEAD_DIM
            ].astype(jnp.bfloat16)
    sealed(out_ref, jnp.swapaxes(denominators, 0, 1)[: len(entries)])


def sealed(out_ref, denominators):
    count = denominators.shape[0]
    filler = jnp.zeros((TAIL - count, HEAD_DIM), jnp.float32)
    lasts = jnp.concatenate(two_terms(denominators), axis=1)
    out_ref[count * HEADS :, :] = jnp.concatenate([lasts, filler]).astype(jnp.bfloat16)


def opened(message, place):
    start = message.shape[0] - TAIL
    last = message[start:, :].astype(jnp.float32)[place : place + 1]
    numerator = message[place * HEADS : (place + 1) * HEADS, :].astype(jnp.float32)
    return numerator, last[:, :HEADS] + last[:, HEADS:]


def piece_at(near, second, odd, entry):
    if entry < 4:
        return near, entry
    return (second, entry - 4) if entry < 8 else (odd, entry - 8)


def page_terms(left, second, entries, pieces, pages, beside=()):
    return pl.pallas_call(
        functools.partial(pages_kernel, entries),
        in_specs=[VMEM_SPEC] * (len(pieces) + 3)
        + [pl.BlockSpec(memory_space=pl.ANY)] * len(beside),
        out_specs=VMEM_SPEC,
        out_shape=jax.ShapeDtypeStruct((len(entries) * HEADS + TAIL, HEAD_DIM), jnp.bfloat16),
        scratch_shapes=[
            pltpu.VMEM((len(entries), HEADS, pages.shape[2]), jnp.float32),
            pltpu.VMEM((len(entries), HEADS, pages.shape[2]), jnp.bfloat16),
        ],
        compiler_params=pltpu.CompilerParams(vmem_limit_bytes=6 * MIB),
        cost_estimate=pl.CostEstimate(flops=2**26, bytes_accessed=2**20, transcendentals=2**14),
    )(left, second, *pieces, in_vmem(pages), *beside)


def two_rows(second_ref, entry, mine, theirs):
    sums = [[0.0, 0.0], [0.0, 0.0]]
    for line, (numerator, denominator) in zip((entry, 16 + entry), (mine, theirs)):
        second = second_ref[line : line + 1, :].astype(jnp.float32)
        for row, share in enumerate((1.0 - second, second)):
            sums[row][0] = sums[row][0] + numerator * share
            sums[row][1] = sums[row][1] + denominator * share[:, :HEADS]
    return sums


def core_kernel(second_ref, mine_ref, theirs_ref, out_ref):
    lowers = []
    for place in range(4):
        mine, theirs = opened(mine_ref, place), opened(theirs_ref, 4 + place)
        for row, (part, lower) in enumerate(two_rows(second_ref, 4 + place, mine, theirs)):
            start = (2 * place + row) * HEADS
            out_ref[start : start + HEADS, :] = part.astype(jnp.bfloat16)
            lowers.append(lower)
    sealed(out_ref, jnp.concatenate(lowers))


def across_core(second, mine, theirs):
    return pl.pallas_call(
        core_kernel,
        in_specs=[VMEM_SPEC] * 3,
        out_specs=VMEM_SPEC,
        out_shape=jax.ShapeDtypeStruct((8 * HEADS + TAIL, HEAD_DIM), jnp.bfloat16),
        compiler_params=pltpu.CompilerParams(vmem_limit_bytes=4 * MIB),
    )(second, mine, theirs)


def chip_kernel(second_ref, mine_ref, theirs_ref, arrived_ref, new_ref, lower_ref, *refs):
    out_ref = refs[-1]
    lowers = []
    for place in range(4):
        mine, theirs = opened(mine_ref, place), opened(theirs_ref, place)
        for row, (part, lower) in enumerate(two_rows(second_ref, place, mine, theirs)):
            arrived, arrived_lower = opened(arrived_ref, 2 * place + row)
            part, lower = part + arrived, lower + arrived_lower
            if place == 0:
                part = part + new_ref[row * HEADS : (row + 1) * HEADS, :]
                lower = lower + lower_ref[8 * row : 8 * row + 1, :]
            start = (2 * place + row) * HEADS
            out_ref[start : start + HEADS, :] = part.astype(jnp.bfloat16)
            lowers.append(lower)
    sealed(out_ref, jnp.concatenate(lowers))


def across_y(second, mine, theirs, arrived, new_terms, beside):
    return pl.pallas_call(
        chip_kernel,
        in_specs=[VMEM_SPEC] * 6 + [pl.BlockSpec(memory_space=pl.ANY)] * len(beside),
        out_specs=VMEM_SPEC,
        out_shape=jax.ShapeDtypeStruct((8 * HEADS + TAIL, HEAD_DIM), jnp.bfloat16),
        compiler_params=pltpu.CompilerParams(vmem_limit_bytes=4 * MIB),
    )(second, mine, theirs, arrived, *new_terms, *beside)


def combine_kernel(*refs):
    shares, out_ref = refs[:4], refs[-1]
    parts, lowers = [], []
    for place in range(4):
        for row in range(2):
            terms = [opened(share, 2 * (place ^ j) + row) for j, share in enumerate(shares)]
            parts.append(sum(part for part, _ in terms))
            lowers.append(sum(lower for _, lower in terms))
    lower = jnp.concatenate([jnp.concatenate(lowers), jnp.zeros((8, HEADS), jnp.float32)], axis=1)
    columns = jnp.swapaxes(lower, 0, 1)
    for index, part in enumerate(parts):
        lines = slice(index % 2 * HEADS, (index % 2 + 1) * HEADS)
        column = columns[:HEADS, index : index + 1]
        out_ref[index // 2, lines, :] = (part / column).astype(jnp.bfloat16)


def combined(shares, beside):
    return pl.pallas_call(
        combine_kernel,
        in_specs=[VMEM_SPEC] * 4 + [pl.BlockSpec(memory_space=pl.ANY)] * len(beside),
        out_specs=VMEM_SPEC,
        out_shape=jax.ShapeDtypeStruct((4, 2 * HEADS, HEAD_DIM), jnp.bfloat16),
        compiler_params=pltpu.CompilerParams(vmem_limit_bytes=4 * MIB),
        cost_estimate=pl.CostEstimate(
            flops=2**22, bytes_accessed=48 * MIB, transcendentals=2**11
        ),
    )(*shares, *beside)


def fetch_kernel(parts, after_ref, *refs):
    weights, outs, sems = refs[: len(parts)], refs[len(parts) : -1], refs[-1]
    me = lax.axis_index("shard")
    copies = []
    for (place_of, entries), weight_hbm, out_ref in zip(parts, weights, outs):
        for place, entry in enumerate(entries):
            copies.append(
                pltpu.make_async_copy(
                    place_of(weight_hbm, device_at(me, entry)),
                    out_ref.at[place],
                    sems.at[len(copies)],
                )
            )
    for copy in copies:
        copy.start()
    for copy in copies:
        copy.wait()


def fetched(after, *parts):
    count = sum(len(entries) for _, _, entries in parts)
    weights = [weight for weight, _, _ in parts]
    shapes = [
        pltpu.VMEM((len(entries),) + place_of(weight, None), weight.dtype)
        for weight, place_of, entries in parts
    ]
    size = sum(math.prod(shape.shape) for shape in shapes)
    return pl.pallas_call(
        functools.partial(fetch_kernel, [part[1:] for part in parts]),
        in_specs=[pl.BlockSpec(memory_space=pl.ANY)] + [HBM_SPEC] * len(parts),
        out_specs=[VMEM_SPEC] * len(parts),
        out_shape=shapes,
        scratch_shapes=[pltpu.SemaphoreType.DMA((count,))],
        compiler_params=pltpu.CompilerParams(vmem_limit_bytes=MIB),
        cost_estimate=pl.CostEstimate(flops=0, bytes_accessed=2 * size, transcendentals=0),
    )(after, *[in_hbm(weight) for weight in weights])


def rows_at(weight, device):
    if device is None:
        return (CHUNK, weight.shape[1])
    return weight.at[pl.ds(pl.multiple_of(device * CHUNK, CHUNK), CHUNK)]


def columns_at(weight, device):
    if device is None:
        return (weight.shape[0], CHUNK)
    return weight.at[:, pl.ds(pl.multiple_of(device * CHUNK, CHUNK), CHUNK)]


def out_kernel(
    near_ref,
    second_ref,
    odd_ref,
    weight_ref,
    residual,
    out_ref,
    wide,
    left,
):
    me = lax.axis_index("shard")
    for entry in range(16):
        source, place = piece_at(near_ref, second_ref, odd_ref, entry)
        start = pl.multiple_of(device_at(me, entry) * 2 * HEADS, 2 * HEADS)
        wide[pl.ds(start, 2 * HEADS), :] = source[place].astype(jnp.float32)
    for head in range(HEADS):
        rows = [wide[pl.ds(row * HEADS + head, 16, 2 * HEADS), :] for row in range(2)]
        left[:, head * HEAD_DIM : (head + 1) * HEAD_DIM] = jnp.concatenate(rows).astype(
            jnp.bfloat16
        )
    total = jnp.dot(left[...], weight_ref[...], preferred_element_type=jnp.float32)
    line = lax.broadcasted_iota(jnp.int32, (32, 32), 0)
    entry = lax.broadcasted_iota(jnp.int32, (32, 32), 1)
    turn = ((line % 2) * 16 + line // 2 == entry).astype(jnp.float32)
    turned = lax.dot_general(
        turn,
        total,
        (((1,), (0,)), ((), ())),
        precision=lax.Precision.HIGHEST,
        preferred_element_type=jnp.float32,
    )
    out_ref[...] = (residual[...].astype(jnp.float32) + turned).astype(jnp.bfloat16)


def projected(near, second, odd, residual, held_weight):
    rows, width = residual.shape
    return pl.pallas_call(
        out_kernel,
        in_specs=[VMEM_SPEC] * 5,
        out_specs=VMEM_SPEC,
        out_shape=jax.ShapeDtypeStruct((rows, width), jnp.bfloat16),
        scratch_shapes=[
            pltpu.VMEM((32 * HEADS, HEAD_DIM), jnp.float32),
            pltpu.VMEM((rows, D), jnp.bfloat16),
        ],
        compiler_params=pltpu.CompilerParams(vmem_limit_bytes=4 * MIB),
        cost_estimate=pl.CostEstimate(
            flops=2 * rows * D * width, bytes_accessed=2 * D * width, transcendentals=0
        ),
    )(near, second, odd, held_weight, residual)


def normed_pieces(entries, pieces, gain_ref, squares):
    lefts = []
    for place, entry in enumerate(entries):
        stream = pieces[place][...] if len(pieces) == len(entries) else pieces[0][place]
        wide = stream.astype(jnp.float32)
        squares = squares + wide * wide
        terms = gain_ref[entry % 4 if entry < 8 else entry - 8, 2 * HEADS :, :]
        terms = terms.astype(jnp.float32)
        gain = terms[0:4] + terms[4:8] + terms[8:12]
        gain = jnp.concatenate([gain[part : part + 1] for part in range(4)], axis=1)
        lefts.append((wide * gain).astype(jnp.bfloat16))
    return lefts, squares


def product(left, weight_at, width):
    step = 128 if width % 128 == 0 else width
    tiles = [
        jnp.dot(left, weight_at(slice(start, start + step)), preferred_element_type=jnp.float32)
        for start in range(0, width, step)
    ]
    return jnp.concatenate(tiles, axis=1)


def terms_of(lefts, blocks):
    left = jnp.concatenate(lefts, axis=1)
    here = lambda cols: blocks[:, :, cols].reshape(left.shape[1], -1)
    return product(left, here, blocks.shape[-1])


def feed_kernel(entries, piece_count, held, ahead, *refs):
    refs = list(refs)
    take = lambda number: [refs.pop(0) for _ in range(number)]
    pieces = take(piece_count)
    gain_ref, gate_ref, up_ref = take(3)
    gates_in, ups_in, squares_in = [None] * 3 if entries[0] == 0 else take(3)
    ahead_hbm = take(1)[0] if ahead else None
    gates, ups, squares_out = take(3)
    copies = []
    if ahead:
        ahead_out, ahead_sems = refs
        me = lax.axis_index("shard")
        ahead_copy = lambda place: pltpu.make_async_copy(
            rows_at(ahead_hbm, device_at(me, ahead[0] + place)),
            ahead_out.at[place],
            ahead_sems.at[place],
        )
        started(len(ahead), ahead_copy)
    if not held:
        sources = gate_ref, up_ref
        *targets, sems = refs
        gate_ref, up_ref = targets
        me = lax.axis_index("shard")
        count = len(entries)
        copies = [
            lambda place, number=number: pltpu.make_async_copy(
                rows_at(sources[number], device_at(me, entries[0] + place)),
                targets[number].at[place],
                sems.at[number * count + place],
            )
            for number in range(2)
        ]
        started(count, *copies)
    squares = 0.0 if squares_in is None else squares_in[...]
    lefts, squares_out[...] = normed_pieces(entries, pieces, gain_ref, squares)
    both = ((gates, gates_in, gate_ref), (ups, ups_in, up_ref))
    if held:
        for total, start, blocks in both:
            total[...] = start[...] + terms_of(lefts, blocks)
        for place in range(len(ahead)):
            ahead_copy(place).wait()
        return
    for place in range(len(entries)):
        for number, (total, start, blocks) in enumerate(both):
            copies[number](place).wait()
            here = lambda cols: blocks[place, :, cols]
            terms = product(lefts[place], here, blocks.shape[-1])
            if place > 0:
                total[...] += terms
            else:
                total[...] = terms if start is None else start[...] + terms


def feed(entries, pieces, gain, sums, gate_weight, up_weight, held=False, ahead=(), ahead_weight=None):
    rows = pieces[0].shape[-2]
    width = gate_weight.shape[-1]
    count = len(entries)
    total = jax.ShapeDtypeStruct((rows, width), jnp.float32)
    here = in_vmem if held else in_hbm
    slots = pltpu.VMEM((count, CHUNK, width), jnp.bfloat16)
    return pl.pallas_call(
        functools.partial(feed_kernel, entries, len(pieces), held, ahead),
        in_specs=[VMEM_SPEC] * (len(pieces) + 1)
        + [VMEM_SPEC if held else HBM_SPEC] * 2
        + [VMEM_SPEC] * len(sums)
        + [HBM_SPEC] * bool(ahead),
        out_specs=[VMEM_SPEC] * (3 + bool(ahead)),
        out_shape=[total, total, jax.ShapeDtypeStruct((rows, CHUNK), jnp.float32)]
        + [pltpu.VMEM((len(ahead), CHUNK, width), jnp.bfloat16)] * bool(ahead),
        scratch_shapes=[pltpu.SemaphoreType.DMA((max(len(ahead), 1),))] * bool(ahead)
        if held
        else [slots, slots, pltpu.SemaphoreType.DMA((2 * count,))],
        compiler_params=pltpu.CompilerParams(
            vmem_limit_bytes=2 * MIB + (0 if held else 4 * count * CHUNK * width)
        ),
        cost_estimate=pl.CostEstimate(
            flops=4 * rows * count * CHUNK * width,
            bytes_accessed=4 * count * CHUNK * width,
            transcendentals=0,
        ),
    )(*pieces, gain, here(gate_weight), here(up_weight), *sums, *([in_hbm(ahead_weight)] if ahead else []))


def hidden_kernel(entries, early_counts, *refs):
    refs = list(refs)
    take = lambda number: [refs.pop(0) for _ in range(number)]
    odd_ref, gain_ref = take(2)
    early = [take(number) for number in early_counts]
    sources = take(2)
    (down_hbm,) = take(1)
    starts = take(2)
    squares_in, hidden_ref, out_ref = take(3)
    totals = take(2)
    held, sems = take(2), take(2)
    down_held, down_sems = refs
    me = lax.axis_index("shard")
    count = len(entries)
    counts = [buffer.shape[0] for buffer in held]
    copies = [
        lambda place, number=number: pltpu.make_async_copy(
            rows_at(sources[number], device_at(me, entries[-1] + 1 - counts[number] + place)),
            held[number].at[place],
            sems[number].at[place],
        )
        for number in range(2)
    ]
    down_copy = lambda place: pltpu.make_async_copy(
        columns_at(down_hbm, device_at(me, entries[0] + place)),
        down_held.at[place],
        down_sems.at[place],
    )
    for number in range(2):
        started(counts[number], copies[number])
    started(count, down_copy)
    lefts, squares = normed_pieces(entries, [odd_ref], gain_ref, squares_in[...])
    places = [0, 0]
    for number in range(2):
        total = starts[number][...]
        for part in early[number]:
            place = places[number]
            places[number] += part.shape[0]
            total += terms_of(lefts[place : places[number]], part)
        totals[number][...] = total
    for number in range(2):
        for place in range(counts[number]):
            copies[number](place).wait()
        totals[number][...] += terms_of(lefts[places[number] :], held[number])
    scale = lax.rsqrt(jnp.sum(squares, axis=1, keepdims=True) / D + norm_eps)
    gates, ups = totals[0][...] * scale, totals[1][...] * scale
    hidden_ref[...] = (jax.nn.silu(gates) * ups).astype(jnp.bfloat16)
    for place in range(count):
        down_copy(place).wait()
        here = lambda cols: down_held[place, :, cols]
        out_ref[place] = product(hidden_ref[...], here, CHUNK).astype(jnp.bfloat16)


def hidden_units(entries, odd, gain, early, weights, down_weight, sums):
    rows = odd.shape[1]
    width = weights[0].shape[1]
    count = len(entries)
    later = [count - sum(part.shape[0] for part in parts) for parts in early]
    total = pltpu.VMEM((rows, width), jnp.float32)
    held = [pltpu.VMEM((number, CHUNK, width), jnp.bfloat16) for number in later]
    early_parts = [part for parts in early for part in parts]
    return pl.pallas_call(
        functools.partial(hidden_kernel, entries, [len(parts) for parts in early]),
        in_specs=[VMEM_SPEC] * (2 + len(early_parts)) + [HBM_SPEC] * 3 + [VMEM_SPEC] * 3,
        out_specs=[VMEM_SPEC] * 2,
        out_shape=[
            jax.ShapeDtypeStruct((rows, width), jnp.bfloat16),
            jax.ShapeDtypeStruct((count, rows, CHUNK), jnp.bfloat16),
        ],
        scratch_shapes=[total, total]
        + held
        + [pltpu.SemaphoreType.DMA((number,)) for number in later]
        + [pltpu.VMEM((count, width, CHUNK), jnp.bfloat16), pltpu.SemaphoreType.DMA((count,))],
        compiler_params=pltpu.CompilerParams(
            vmem_limit_bytes=2 * (sum(later) + count) * CHUNK * width + MIB
        ),
        cost_estimate=pl.CostEstimate(
            flops=2 * rows * 3 * count * CHUNK * width,
            bytes_accessed=2 * 3 * count * CHUNK * width,
            transcendentals=rows * width,
        ),
    )(
        odd,
        gain,
        *[in_vmem(part) for part in early_parts],
        *[in_hbm(weight) for weight in weights],
        in_hbm(down_weight),
        *sums,
    )


def down_kernel(hidden_ref, held_ref, out_ref):
    for place in range(held_ref.shape[0]):
        out_ref[place] = product(hidden_ref[...], lambda cols: held_ref[place, :, cols], CHUNK)


def down_terms(hidden, held):
    rows, depth = hidden.shape
    count = held.shape[0]
    return pl.pallas_call(
        down_kernel,
        in_specs=[VMEM_SPEC] * 2,
        out_specs=VMEM_SPEC,
        out_shape=jax.ShapeDtypeStruct((count, rows, CHUNK), jnp.float32),
        compiler_params=pltpu.CompilerParams(vmem_limit_bytes=4 * MIB),
        cost_estimate=pl.CostEstimate(
            flops=2 * rows * depth * CHUNK * count,
            bytes_accessed=2 * depth * CHUNK * count,
            transcendentals=0,
        ),
    )(hidden, in_vmem(held))


def far_kernel(mine_ref, theirs_ref, out_ref):
    for place in range(4):
        out_ref[place] = (mine_ref[place] + theirs_ref[4 + place].astype(jnp.float32)).astype(
            jnp.bfloat16
        )


def far_pairs(mine, theirs):
    return pl.pallas_call(
        far_kernel,
        in_specs=[VMEM_SPEC] * 2,
        out_specs=VMEM_SPEC,
        out_shape=jax.ShapeDtypeStruct((4,) + theirs.shape[1:], jnp.bfloat16),
        compiler_params=pltpu.CompilerParams(vmem_limit_bytes=4 * MIB),
    )(mine, theirs)


def near_kernel(mine_ref, theirs_ref, arrived_ref, own_ref, *out_refs):
    for place, out_ref in enumerate((own_ref,) + out_refs):
        total = mine_ref[place] + theirs_ref[place].astype(jnp.float32)
        total = total + arrived_ref[place].astype(jnp.float32)
        out_ref[...] = total.astype(out_ref.dtype)


def near_sums(mine, theirs, arrived):
    block = theirs.shape[1:]
    return pl.pallas_call(
        near_kernel,
        in_specs=[VMEM_SPEC] * 3,
        out_specs=[VMEM_SPEC] * 4,
        out_shape=[jax.ShapeDtypeStruct(block, jnp.float32)]
        + [jax.ShapeDtypeStruct(block, jnp.bfloat16)] * 3,
        compiler_params=pltpu.CompilerParams(vmem_limit_bytes=4 * MIB),
    )(mine, theirs, arrived)


def finish_kernel(stream_ref, *refs):
    total = stream_ref[...].astype(jnp.float32)
    for share in refs[:-1]:
        total = total + share[...].astype(jnp.float32)
    refs[-1][...] = total.astype(jnp.bfloat16)


def finished(stream, shares):
    return pl.pallas_call(
        finish_kernel,
        in_specs=[VMEM_SPEC] * (1 + len(shares)),
        out_specs=VMEM_SPEC,
        out_shape=jax.ShapeDtypeStruct(stream.shape, jnp.bfloat16),
        compiler_params=pltpu.CompilerParams(vmem_limit_bytes=4 * MIB),
    )(stream, *shares)


def block_body(
    queries,
    new_kv,
    kv_pages,
    page_table,
    lengths,
    residual,
    out_weight,
    norm_gain,
    gate_weight,
    up_weight,
    down_weight,
):
    me = lax.axis_index("shard").astype(jnp.int32)[None]
    table = jnp.concatenate([page_table.reshape(-1), lengths, me])
    own, query_rows = packed(queries, norm_gain)
    middle, late = (4, 5, 6, 7), tuple(range(8, 16))

    (early_gate,) = fetched(table, (gate_weight, rows_at, late[:3]))
    near = stacked(near_pieces(own), (early_gate,))
    second = sent(near, 2)
    pages, left, of_second, *new_terms = readied(table, query_rows, kv_pages, new_kv, near)
    odd = sent(stacked([near, second], new_terms[:1]), 1)
    gains = near, second, odd
    along = page_terms(left, of_second, (0, 1, 2, 3), (near, second), pages)
    theirs = page_terms(left, of_second, late, (odd,), pages, (along,))
    across = page_terms(left, of_second, middle, (near, second), pages)

    theirs = sent(theirs, 1)
    across = across_core(of_second, across, theirs)
    arrived = sent(across, 2)
    gate_held, early_first = fetched(
        across, (gate_weight, rows_at, middle), (up_weight, rows_at, late[:2])
    )
    own = across_y(of_second, along, theirs, arrived, new_terms, (gate_held,))
    up_held, early_second, down_first = fetched(
        own,
        (up_weight, rows_at, middle),
        (up_weight, rows_at, late[2:6]),
        (down_weight, columns_at, middle),
    )
    near = combined(near_pieces(own), (up_held,))

    second = sent(near, 2)
    (down_rest,) = fetched(near, (down_weight, columns_at, (0, 1, 2, 3)))
    odd = sent(stacked([near, second], (down_rest,)), 1)
    stream = projected(near, second, odd, residual, out_weight)

    weights = gate_weight, up_weight
    near = near_pieces(stream)
    sums = feed((0,), near[:1], gains[0], (), *weights)
    first = stacked(near, sums[:1])
    second = sent(first, 2)
    sums = feed((1, 2, 3), near[1:], gains[0], sums, *weights)
    odd = sent(stacked([first, second], sums[:1]), 1)
    *sums, more_gate = feed(
        middle,
        [second],
        gains[1],
        sums,
        gate_held,
        up_held,
        held=True,
        ahead=late[3:5],
        ahead_weight=gate_weight,
    )
    early = (early_gate, more_gate), (early_first, early_second)
    hidden, theirs = hidden_units(late, odd, gains[2], early, weights, down_weight, sums)

    theirs = sent(theirs, 1)
    far = down_terms(hidden, down_first)
    arrived = sent(far_pairs(far, theirs), 2)
    mine = down_terms(hidden, down_rest)
    own, *others = near_sums(mine, theirs, arrived)
    shares = [sent(other, distance) for other, distance in zip(others[::-1], (12, 8, 4))]
    return finished(stream, shares + [own])


def solution(mesh):
    placed = (
        P(("groups", "shard"), None),
        P(("groups", "shard"), None, None),
        P(("groups", "shard"), None, None, None),
        P("groups", None),
        P("groups"),
        P("groups", "shard"),
        P(None, "shard"),
        P("shard"),
        P(None, "shard"),
        P(None, "shard"),
        P("shard", None),
    )
    chosen = block_body if mesh.shape["shard"] == 16 else body
    return jax.shard_map(
        chosen, mesh=mesh, in_specs=placed, out_specs=P("groups", "shard"), check_vma=False
    )
```
